128 devices in a mesh: face: 8 (over z_lo, y), tile: 16 (over x, z_hi, core).
Axes of the slice: x: 4, y: 4, z: 4 (z_hi: 2, z_lo: 2; z = z_hi * 2 + z_lo), core: 2. Of those that a mesh axis runs over, the one named last changes fastest.
Arguments:
- obs_values: bfloat16 [32768, 256], P(('face', 'tile')), may hold values from -6 to 6
- obs_tile: int32 [32768, 1], P(('face', 'tile')), may hold values from 0 to 127; in each aligned block of 256 rows (0 to 255, 256 to 511, ...) at most 4 rows name the same one
- interp: bfloat16 [128, 128, 4, 256], P(('face', 'tile')), may hold values from -0.375 to 0.375
- tile_spin: int32 [128, 1], P(('face', 'tile')), may hold values from 0 to 3
- w_embed: bfloat16 [256, 512], replicated, may hold values from -0.375 to 0.375
- dw_kernel: bfloat16 [49, 512], replicated, may hold values from -0.875 to 0.875
- norm_gain: bfloat16 [512], replicated, may hold values from 0.099609375 to 1.8984375
- w_one: bfloat16 [512, 2048], replicated, may hold values from -0.25 to 0.25
- w_two: bfloat16 [2048, 512], replicated, may hold values from -0.125 to 0.125
- cotangent: bfloat16 [32768, 512], P(('face', 'tile')), may hold values from -0.032958984 to 0.032958984
Outputs:
- features: bfloat16 [32768, 512], P(('face', 'tile'))
- grad_embed: float32 [256, 512], replicated
- grad_kernel: float32 [49, 512], replicated
- grad_gain: float32 [512], replicated
- grad_one: float32 [512, 2048], replicated
- grad_two: float32 [2048, 512], replicated
The draws below stay inside these ranges and needn't reach their ends.
Inputs may be any that keep to these rules, and one draw needn't show every extreme that they name: `obs_tile`: in the rows of one device no tile is named more than 4 times; in some device one tile is named exactly 4 times.
All inputs are finite; a program needn't handle non-finite values.
Results may differ from the reference program's by a relative error of at most 0.0081.
Values may be sent and summed in bfloat16 or wider, within the bound.
No kernel may reach another device: no remote copies, remote signals or barrier semaphores. Data moves between devices by JAX's collectives and lax.ppermute only.
A program may use at most 256 MiB of HBM per device.

```python
import math
from functools import partial
import jax
import jax.numpy as jnp
import numpy as np
from jax import lax

V = 256
C = 512
HID = 2048
SIDE = 16
OBS_DEV = 256
TILE_ROWS = 8
TILE_COLS = 16
TILES = 128
CELLS = 256
MOST = 4


def set_ends(result, stream_key, least, largest):
    spot = [jax.random.randint(jax.random.fold_in(stream_key, axis), (), 0, length) for axis, length in enumerate(result.shape)]
    main_axis = result.shape.index(max(result.shape))
    beside = spot[:main_axis] + [(spot[main_axis] + 1) % result.shape[main_axis]] + spot[main_axis + 1:]
    return result.at[tuple(spot)].set(least).at[tuple(beside)].set(largest)


def block_scale(stream_key, extent, cuts, least, largest):
    def one(position, blocks):
        draws = jax.random.uniform(jax.random.fold_in(jax.random.fold_in(stream_key, 6), position), (blocks,), jnp.float32, least / len(cuts), largest / len(cuts))
        return jnp.repeat(jnp.exp(draws), extent[position] // blocks).reshape((-1,) + (1,) * (len(extent) - position - 1))

    factor_of = one(*cuts[0])
    for cut in cuts[1:]:
        factor_of = factor_of * one(*cut)
    return factor_of


def deal_out(rng, own, number, rows, number_of, top, limit, slope):
    ranking = jax.random.permutation(rng, number_of)
    heavy_load, common = portions_of(number_of, rows * top, limit, slope, True), portions_of(number_of, rows * top, limit, slope, False)
    places = jnp.arange(number_of)

    def named(tallies, offset_by):
        used = int((tallies > 0).sum())
        fixed = max(1, used // 4)
        passed = fixed + (places - fixed + offset_by * (used - fixed)) % max(1, number_of - fixed)
        return jnp.zeros((number_of,), jnp.int32).at[ranking[jnp.where(places < fixed, places, passed)]].set(jnp.asarray(tallies, jnp.int32))

    tallies = jnp.where(number % 4 == 0, named(heavy_load, number // 4), named(common, number - number // 4 - 1))
    mixed = jax.random.permutation(jax.random.fold_in(own, 3), number_of)
    source_of, taker = mixed[0:number_of // 2 * 2:2], mixed[1:number_of // 2 * 2:2]
    room = jnp.minimum(tallies[source_of] - 1, limit - tallies[taker]) // 2
    room = jnp.where((source_of == ranking[0]) | (taker == ranking[0]) | (tallies[taker] == 0), 0, jnp.maximum(room, 0))
    passed = jax.random.randint(jax.random.fold_in(own, 4), (number_of // 2,), 0, 1 << 20) % (room + 1)
    tallies = tallies.at[source_of].add(-passed).at[taker].add(passed)
    items = jnp.searchsorted(jnp.cumsum(tallies), jnp.arange(rows * top), side="right").astype(jnp.int32)
    grid = items.reshape(top, rows).T
    grid = grid[jax.random.permutation(jax.random.fold_in(own, 1), rows)]
    offset_by = jax.random.randint(jax.random.fold_in(own, 2), (rows, 1), 0, top)
    return jnp.take_along_axis(grid, (jnp.arange(top)[None, :] + offset_by) % top, axis=1)


def portions_of(number_of, total, most, skew, full):
    portions = [(1 << 20) // math.isqrt(grade ** skew) + 1 for grade in range(1, number_of + 1)]
    largest = most if full else min(most, max(-(-total // number_of), total * portions[0] // sum(portions)))
    least = 1 if total - largest >= number_of - 1 else 0
    counts, spare = [largest] + [least] * (number_of - 1), total - largest - least * (number_of - 1)
    while spare > 0:
        free = [i for i in range(1, number_of) if counts[i] < largest] or [i for i in range(1, number_of) if counts[i] < most]
        mass, budget = sum([portions[i] for i in free]), spare
        for i in free:
            addition = min(most - counts[i], max(1, budget * portions[i] // mass), spare)
            counts[i] = counts[i] + addition
            spare = spare - addition
    return np.array(counts)


def normal_values(own_key, extent, scale, bound, split=(), kind=jnp.bfloat16):
    loudness = block_scale(own_key, extent, split, -0.22, 0.18) if split else 1.0
    values = jax.random.normal(own_key, extent, jnp.float32) * scale * loudness
    return jnp.minimum(jnp.maximum(values, -bound), bound).astype(kind)


def setup_inputs(seed: int = 0) -> dict:
    arg_keys = jax.random.split(jax.random.key(seed), 11)
    obs_values = normal_values(arg_keys[0], (TILES * OBS_DEV, V), 1.0, 6.0, ((0, 128),))
    obs_tile_keys = jax.random.split(jax.random.fold_in(arg_keys[1], 1), (TILES * OBS_DEV) // OBS_DEV)
    obs_tile_turns = jax.random.permutation(jax.random.fold_in(arg_keys[1], 3), (TILES * OBS_DEV) // OBS_DEV)
    obs_tile = jax.vmap(lambda own, number: deal_out(jax.random.fold_in(arg_keys[1], 2), own, number, OBS_DEV, TILES, 1, MOST, 2))(obs_tile_keys, obs_tile_turns).reshape((TILES * OBS_DEV, 1))
    interp = normal_values(arg_keys[2], (TILES, TILES, MOST, CELLS), OBS_DEV ** -0.5, 0.375, ((0, 128),))
    tile_spin = set_ends(jax.random.randint(arg_keys[3], (TILES, 1), 0, 4), jax.random.fold_in(arg_keys[3], 1), 0, 3).astype(jnp.int32)
    w_embed = normal_values(arg_keys[4], (V, C), V ** -0.5, 0.375)
    dw_kernel = normal_values(arg_keys[5], (49, C), 49 ** -0.5, 0.875)
    norm_gain = jnp.clip(1.0 + 0.18 * jax.random.normal(arg_keys[6], (C,), jnp.float32), 0.099609375, 1.8984375).astype(jnp.bfloat16)
    w_one = normal_values(arg_keys[7], (C, HID), C ** -0.5, 0.25)
    w_two = normal_values(arg_keys[8], (HID, C), HID ** -0.5, 0.125)
    cotangent = normal_values(arg_keys[9], (TILES * CELLS, C), ((TILES * CELLS) ** -0.5), 0.032958984, ((0, 128),))
    return dict(obs_values=obs_values, obs_tile=obs_tile, interp=interp, tile_spin=tile_spin, w_embed=w_embed, dw_kernel=dw_kernel, norm_gain=norm_gain, w_one=w_one, w_two=w_two, cotangent=cotangent)


def quarter_turn(block, quarter):
    return lax.switch(quarter, [partial(jnp.rot90, k=turns, axes=(0, 1)) for turns in range(4)], block)

def tile_pass(field, embedded, cot_tile, dw_kernel, norm_gain, w_one, w_two):
    side_len = embedded.shape[0]
    channels = embedded.shape[2]
    cell_count = side_len * side_len
    kernel_taps = dw_kernel.astype(jnp.float32)
    gain_values = norm_gain.astype(jnp.float32)
    convolved = jnp.zeros((side_len, side_len, channels), jnp.float32)
    for kernel_tap in range(49):
        row_shift, col_shift = divmod(kernel_tap, 7)
        convolved = convolved + field[row_shift:row_shift + side_len, col_shift:col_shift + side_len].astype(jnp.float32) * kernel_taps[kernel_tap]
    flattened = convolved.reshape(cell_count, channels)
    centred = flattened - lax.optimization_barrier(jnp.mean(flattened, axis=-1, keepdims=True))
    inverse = lax.rsqrt(lax.optimization_barrier(jnp.mean(centred * centred, axis=-1, keepdims=True)) + 1e-06)
    normal = centred * inverse
    scaled = (normal * gain_values).astype(jnp.bfloat16)
    hidden_pre = jnp.dot(scaled, w_one, preferred_element_type=jnp.float32)
    active, gelu_back = jax.vjp(partial(jax.nn.gelu, approximate=True), hidden_pre)
    active = active.astype(jnp.bfloat16)
    branch = jnp.dot(active, w_two, preferred_element_type=jnp.float32)
    output = (embedded.reshape(cell_count, channels).astype(jnp.float32) + branch).astype(jnp.bfloat16)
    contract_rows = (((0,), (0,)), ((), ()))
    contract_cols = (((1,), (1,)), ((), ()))
    grad_two = lax.dot_general(active, cot_tile, contract_rows, preferred_element_type=jnp.float32)
    d_active = lax.dot_general(cot_tile, w_two, contract_cols, preferred_element_type=jnp.float32)
    d_hidden = gelu_back(d_active)[0].astype(jnp.bfloat16)
    grad_one = lax.dot_general(scaled, d_hidden, contract_rows, preferred_element_type=jnp.float32)
    d_scaled = lax.dot_general(d_hidden, w_one, contract_cols, preferred_element_type=jnp.float32)
    grad_gain = lax.optimization_barrier(jnp.sum(d_scaled * normal, axis=0))
    d_normal = d_scaled * gain_values
    d_conv = (d_normal - lax.optimization_barrier(jnp.mean(d_normal, axis=-1, keepdims=True)) - normal * lax.optimization_barrier(jnp.mean(d_normal * normal, axis=-1, keepdims=True))) * inverse
    d_conv = d_conv.reshape(side_len, side_len, channels)
    kernel_rows = []
    for kernel_tap in range(49):
        row_shift, col_shift = divmod(kernel_tap, 7)
        kernel_rows.append(lax.optimization_barrier(jnp.sum(field[row_shift:row_shift + side_len, col_shift:col_shift + side_len].astype(jnp.float32) * d_conv, axis=(0, 1))))
    grad_kernel = jnp.stack(kernel_rows)
    spread = jnp.pad(d_conv, ((6, 6), (6, 6), (0, 0)))
    d_field = jnp.zeros((side_len + 6, side_len + 6, channels), jnp.float32)
    for kernel_tap in range(49):
        row_shift, col_shift = divmod(kernel_tap, 7)
        d_field = d_field + spread[6 - row_shift:12 - row_shift + side_len, 6 - col_shift:12 - col_shift + side_len] * kernel_taps[kernel_tap]
    return (output, grad_one, grad_two, grad_gain, grad_kernel, d_field)

def reference(obs_values, obs_tile, interp, tile_spin, w_embed, dw_kernel, norm_gain, w_one, w_two, cotangent):
    tile_count = TILES
    tile_ids = jnp.arange(tile_count, dtype=jnp.int32)
    targets = obs_tile[:, 0].reshape(tile_count, OBS_DEV)
    onehot = (targets[:, :, None] == tile_ids[None, None, :]).astype(jnp.int32)
    slot_rank = lax.optimization_barrier(jnp.sum((jnp.cumsum(onehot, axis=1) - 1) * onehot, axis=2)).astype(jnp.int32)
    sources = jnp.broadcast_to(tile_ids[:, None], (tile_count, OBS_DEV))
    buckets = jnp.zeros((tile_count, tile_count, MOST, V), jnp.bfloat16)
    buckets = buckets.at[targets, sources, slot_rank].set(obs_values.reshape(tile_count, OBS_DEV, V))

    def grid_one(pair):
        weights, bucket = pair
        return lax.dot_general(weights.reshape(tile_count * MOST, CELLS), bucket.reshape(tile_count * MOST, V), (((0,), (0,)), ((), ())), preferred_element_type=jnp.float32).astype(jnp.bfloat16)
    gridded = lax.map(grid_one, (interp, buckets))

    def embed_one(grid_tile):
        return jnp.dot(grid_tile, w_embed, preferred_element_type=jnp.float32).astype(jnp.bfloat16)
    embedded = lax.map(embed_one, gridded).reshape(tile_count, SIDE, SIDE, C)
    spins = tile_spin[:, 0].astype(jnp.int32)
    back_spins = ((4 - spins) % 4).astype(jnp.int32)
    logical = lax.map(lambda pair: quarter_turn(pair[0], pair[1]), (embedded, spins))
    grid_tiles = logical.reshape(TILE_ROWS, TILE_COLS, SIDE, SIDE, C)
    padded = jnp.pad(grid_tiles, ((0, 0), (0, 0), (3, 3), (3, 3), (0, 0)))
    padded = padded.at[:, :, 0:3, 3:SIDE + 3].set(jnp.roll(grid_tiles[:, :, SIDE - 3:], 1, axis=0))
    padded = padded.at[:, :, SIDE + 3:, 3:SIDE + 3].set(jnp.roll(grid_tiles[:, :, 0:3], -1, axis=0))
    padded = padded.at[:, :, 3:SIDE + 3, 0:3].set(jnp.roll(grid_tiles[:, :, :, SIDE - 3:], 1, axis=1))
    padded = padded.at[:, :, 3:SIDE + 3, SIDE + 3:].set(jnp.roll(grid_tiles[:, :, :, 0:3], -1, axis=1))
    padded = padded.reshape(tile_count, SIDE + 6, SIDE + 6, C)
    cot_tiles = cotangent.reshape(tile_count, CELLS, C)

    def forward_step(carry, item):
        embedded_tile, padded_tile, cot_tile, spin_value, back_value = item
        field = quarter_turn(padded_tile, back_value)
        output, grad_one, grad_two, grad_gain, grad_kernel, d_field = tile_pass(field, embedded_tile, cot_tile, dw_kernel, norm_gain, w_one, w_two)
        carry = (carry[0] + grad_kernel, carry[1] + grad_gain, carry[2] + grad_one, carry[3] + grad_two)
        return (carry, (output, quarter_turn(d_field, spin_value)))
    start = (jnp.zeros((49, C), jnp.float32), jnp.zeros((C,), jnp.float32), jnp.zeros((C, HID), jnp.float32), jnp.zeros((HID, C), jnp.float32))
    totals, stacked = lax.scan(forward_step, start, (embedded, padded, cot_tiles, spins, back_spins))
    outputs, d_logical = stacked
    d_logical = d_logical.reshape(TILE_ROWS, TILE_COLS, SIDE + 6, SIDE + 6, C)

    def rounded(piece):
        return lax.optimization_barrier(piece.astype(jnp.bfloat16)).astype(jnp.float32)
    collected = d_logical[:, :, 3:SIDE + 3, 3:SIDE + 3]
    collected = collected.at[:, :, 0:3].add(jnp.roll(rounded(d_logical[:, :, SIDE + 3:, 3:SIDE + 3]), 1, axis=0))
    collected = collected.at[:, :, SIDE - 3:].add(jnp.roll(rounded(d_logical[:, :, 0:3, 3:SIDE + 3]), -1, axis=0))
    collected = collected.at[:, :, :, 0:3].add(jnp.roll(rounded(d_logical[:, :, 3:SIDE + 3, SIDE + 3:]), 1, axis=1))
    collected = collected.at[:, :, :, SIDE - 3:].add(jnp.roll(rounded(d_logical[:, :, 3:SIDE + 3, 0:3]), -1, axis=1))
    collected = collected.reshape(tile_count, SIDE, SIDE, C)

    def backward_step(running, item):
        grid_tile, collected_tile, cot_tile, back_value = item
        d_embedded = quarter_turn(collected_tile, back_value) + cot_tile.reshape(SIDE, SIDE, C).astype(jnp.float32)
        d_round = d_embedded.reshape(CELLS, C).astype(jnp.bfloat16)
        return (running + lax.dot_general(grid_tile, d_round, (((0,), (0,)), ((), ())), preferred_element_type=jnp.float32), None)
    grad_embed, unused = lax.scan(backward_step, jnp.zeros((V, C), jnp.float32), (gridded, collected, cot_tiles, back_spins))
    return (outputs.reshape(tile_count * CELLS, C), grad_embed, totals[0], totals[1], totals[2], totals[3])
```

```python
import jax
import jax.numpy as jnp
from jax import lax
from jax.experimental import pallas as pl
from jax.experimental.pallas import tpu as pltpu
from jax.sharding import PartitionSpec as P

F32 = jnp.float32
BF16 = jnp.bfloat16
SIDE = 16
CELLS = SIDE * SIDE
HALO = 3
TAPS = 7
FULL = SIDE + 2 * HALO
PITCH = 24
HALF = SIDE // 2
LANE = 128
ROWS2 = HALF + TAPS - 1
STRIP = HALO * SIDE
BOTH = ("face", "tile")
ROOT = 0.7978845608028654
CUBE = 0.044715

NN = (((1,), (0,)), ((), ()))
NT = (((1,), (1,)), ((), ()))
TN = (((0,), (0,)), ((), ()))


def dot(a, b, dims=NN):
    return lax.dot_general(a, b, dims, preferred_element_type=F32)


def call(kernel, outs, scratch, limit, *args):
    vmem = pl.BlockSpec(memory_space=pltpu.VMEM)
    return pl.pallas_call(
        kernel,
        out_shape=[jax.ShapeDtypeStruct(s, d) for s, d in outs],
        in_specs=[vmem] * len(args),
        out_specs=[vmem] * len(outs),
        scratch_shapes=[pltpu.VMEM(s, d) for s, d in scratch],
        compiler_params=pltpu.CompilerParams(vmem_limit_bytes=limit * 2**20),
    )(*args)


def block(i, j, pitch):
    return pl.ds(pl.multiple_of((i * pitch + j) * 8, 8), 8)


def comb(i, j, pitch, h, cb):
    return pl.ds((i * pitch + j) * 8 + h * 4 + cb, 8, stride=8)


def route_kernel(col_ref, row_ref, obs_ref, out_ref):
    row = row_ref[...]
    count = row.shape[1]
    earlier = lax.broadcasted_iota(jnp.int32, (count, count), 0) < lax.broadcasted_iota(
        jnp.int32, (count, count), 1
    )
    same = jnp.where((col_ref[...] == row) & earlier, 1.0, 0.0)
    rank = jnp.sum(same, axis=0, keepdims=True).astype(jnp.int32)
    place = row * 8 + rank
    lines = out_ref.shape[0]
    line = lax.broadcasted_iota(jnp.int32, (lines, count), 0)
    chosen = jnp.where((line - (line & 4)) == place, 1.0, 0.0).astype(BF16)
    moved = dot(chosen, obs_ref[...])
    first = (lax.broadcasted_iota(jnp.int32, (lines, LANE), 0) & 4) == 0
    out_ref[...] = jnp.where(first, moved[:, :LANE], moved[:, LANE:]).astype(BF16)


def embed_kernel(got_ref, weights_ref, w_embed_ref, pick_ref, grid_ref, emb_ref, *strip_refs):
    got = got_ref[...].astype(F32)
    first = (lax.broadcasted_iota(jnp.int32, got.shape, 0) & 4) == 0
    spread = jnp.concatenate(
        [jnp.where(first, got, 0.0), jnp.where(first, 0.0, got)], axis=1
    ).astype(BF16)
    gridded = dot(weights_ref[...], spread).astype(BF16)
    grid_ref[...] = gridded
    embedded = dot(gridded, w_embed_ref[...]).astype(BF16)
    emb_ref[...] = embedded
    strips = dot(pick_ref[...], embedded).astype(BF16)
    for k, ref in enumerate(strip_refs):
        ref[...] = strips[k * STRIP : (k + 1) * STRIP]


def forward_kernel(
    emb_ref, s0, s1, s2, s3, place_ref, kern_ref, gain_ref, w_one_ref, d_act_ref, cot_ref,
    field_ref, normal_ref, inv_ref, active_ref, d_hid_ref, one_ref, two_ref,
    cells_ref, flat_ref, conv_ref, scaled_ref,
):
    cells_ref[0:CELLS] = emb_ref[...]
    for k, ref in enumerate((s0, s1, s2, s3)):
        cells_ref[CELLS + k * STRIP : CELLS + (k + 1) * STRIP] = ref[...]
    flat_ref[...] = dot(place_ref[...], cells_ref[...])
    for x in range(FULL):
        for g in range(3):
            for cb in range(4):
                value = flat_ref[pl.ds(x * PITCH + 8 * g, 8), pl.ds(cb * LANE, LANE)]
                if x < ROWS2:
                    field_ref[comb(x, 8 * g, PITCH, 0, cb), :] = value
                if x >= HALF:
                    field_ref[comb(x - HALF, 8 * g, PITCH, 1, cb), :] = value

    def conv_row(i, carry):
        sums = [jnp.zeros((8, LANE), F32)] * SIDE
        for a in range(TAPS):
            taps = [kern_ref[pl.ds((a * TAPS + b) * 8, 8), :] for b in range(TAPS)]
            for y in range(FULL):
                here = field_ref[block(i + a, y, PITCH), :]
                for b in range(TAPS):
                    if 0 <= y - b < SIDE:
                        sums[y - b] = sums[y - b] + here * taps[b]
        for j in range(SIDE):
            conv_ref[block(i, j, SIDE), :] = sums[j]
        return carry

    lax.fori_loop(0, HALF, conv_row, 0)

    for r in range(SIDE):
        h, i = divmod(r, HALF)
        parts = [
            jnp.concatenate([conv_ref[comb(i, 8 * g, SIDE, h, cb), :] for g in range(2)], axis=0)
            for cb in range(4)
        ]
        value = jnp.concatenate(parts, axis=1)
        centred = value - jnp.mean(value, axis=1, keepdims=True)
        inverse = lax.rsqrt(jnp.mean(centred * centred, axis=1, keepdims=True) + 1e-06)
        normal = centred * inverse
        rows = pl.ds(r * SIDE, SIDE)
        normal_ref[rows, :] = normal
        inv_ref[rows, :] = jnp.broadcast_to(inverse, (SIDE, LANE))
        scaled_ref[rows, :] = (normal * gain_ref[...]).astype(BF16)

    step = 256
    for k in range(w_one_ref.shape[1] // step):
        some = pl.ds(k * step, step)
        pre = dot(scaled_ref[...], w_one_ref[:, some])
        square = pre * pre
        tanh = jnp.tanh(pre * (ROOT + (ROOT * CUBE) * square))
        upper = 0.5 + 0.5 * tanh
        active = (pre * upper).astype(BF16)
        slope = upper + (0.5 * pre) * (1.0 - tanh * tanh) * (ROOT + (3.0 * ROOT * CUBE) * square)
        d_hid = (d_act_ref[:, some] * slope).astype(BF16)
        active_ref[:, some] = active
        d_hid_ref[:, some] = d_hid
        two_ref[some, :] = dot(active, cot_ref[...], TN).astype(two_ref.dtype)
        one_ref[:, some] = dot(scaled_ref[...], d_hid, TN).astype(one_ref.dtype)


def backward_kernel(
    emb_ref, field_ref, normal_ref, inv_ref, active_ref, d_hid_ref, w_one_ref, w_two_ref,
    gain_ref, kern_ref, cot_ref, back_ref,
    out_ref, taps_ref, gain_out_ref, inner_ref, t0, t1, t2, t3,
    d_scaled_ref, d_conv_ref, spread_ref, flat_ref,
):
    d_scaled_ref[...] = dot(d_hid_ref[...], w_one_ref[...], NT)
    total = jnp.zeros((SIDE, normal_ref.shape[1]), F32)
    for r in range(SIDE):
        h, i = divmod(r, HALF)
        rows = pl.ds(r * SIDE, SIDE)
        normal, d_scaled = normal_ref[rows, :], d_scaled_ref[rows, :]
        total = total + d_scaled * normal
        d_normal = d_scaled * gain_ref[...]
        mean = jnp.mean(d_normal, axis=1, keepdims=True)
        along = jnp.mean(d_normal * normal, axis=1, keepdims=True)
        d_conv = (d_normal - mean - normal * along) * inv_ref[rows, 0:1]
        for g in range(2):
            for cb in range(4):
                d_conv_ref[comb(i, 8 * g, SIDE, h, cb), :] = d_conv[
                    8 * g : 8 * g + 8, cb * LANE : (cb + 1) * LANE
                ]
    gain_out_ref[...] = jnp.sum(total, axis=0, keepdims=True)

    spread_ref[...] = jnp.zeros_like(spread_ref)
    taps_ref[...] = jnp.zeros_like(taps_ref)

    def conv_row(i, carry):
        for a in range(TAPS):
            taps = [kern_ref[pl.ds((a * TAPS + b) * 8, 8), :] for b in range(TAPS)]
            for y in range(FULL):
                value = spread_ref[block(i + a, y, PITCH), :]
                for b in range(TAPS):
                    if 0 <= y - b < SIDE:
                        value = value + d_conv_ref[block(i, y - b, SIDE), :] * taps[b]
                spread_ref[block(i + a, y, PITCH), :] = value
        return carry

    lax.fori_loop(0, HALF, conv_row, 0)

    def tap_row(i, carry):
        for a in range(TAPS):
            sums = [taps_ref[pl.ds((a * TAPS + b) * 8, 8), :] for b in range(TAPS)]
            for y in range(FULL):
                here = field_ref[block(i + a, y, PITCH), :]
                for b in range(TAPS):
                    if 0 <= y - b < SIDE:
                        sums[b] = sums[b] + here * d_conv_ref[block(i, y - b, SIDE), :]
            for b in range(TAPS):
                taps_ref[pl.ds((a * TAPS + b) * 8, 8), :] = sums[b]
        return carry

    lax.fori_loop(0, HALF, tap_row, 0)

    def field_part(x, start, cb):
        value = None
        if x < ROWS2:
            value = spread_ref[comb(x, start, PITCH, 0, cb), :]
        if x >= HALF:
            more = spread_ref[comb(x - HALF, start, PITCH, 1, cb), :]
            value = more if value is None else value + more
        return value

    for x in range(FULL):
        for cb in range(4):
            lanes = pl.ds(cb * LANE, LANE)
            for g in range(3):
                flat_ref[pl.ds(x * PITCH + 8 * g, 8), lanes] = field_part(x, 8 * g, cb)
            if HALO <= x < SIDE + HALO:
                for g in range(2):
                    rows = pl.ds((x - HALO) * SIDE + 8 * g, 8)
                    inner_ref[rows, lanes] = field_part(x, HALO + 8 * g, cb)
    inner_ref[...] = inner_ref[...] + cot_ref[...].astype(F32)
    strips = dot(back_ref[...], flat_ref[...].astype(BF16)).astype(BF16)
    for k, ref in enumerate((t0, t1, t2, t3)):
        ref[...] = strips[k * STRIP : (k + 1) * STRIP]
    out_ref[...] = (emb_ref[...].astype(F32) + dot(active_ref[...], w_two_ref[...])).astype(BF16)


def collect_kernel(inner_ref, t0, t1, t2, t3, add_ref, grid_ref, out_ref, cells_ref):
    for k, ref in enumerate((t0, t1, t2, t3)):
        cells_ref[k * STRIP : (k + 1) * STRIP] = ref[...]
    d_round = (inner_ref[...] + dot(add_ref[...], cells_ref[...])).astype(BF16)
    out_ref[...] = dot(grid_ref[...], d_round, TN)


def turned(spin, x, y, last):
    row = jnp.where(spin == 0, x, jnp.where(spin == 1, last - y, jnp.where(spin == 2, last - x, y)))
    col = jnp.where(spin == 0, y, jnp.where(spin == 1, x, jnp.where(spin == 2, last - y, last - x)))
    return row, col


def selectors(spin):
    p = jnp.arange(FULL * PITCH, dtype=jnp.int32)
    x, y = p // PITCH, p % PITCH
    row, col = turned(spin, x, y, FULL - 1)
    end = SIDE + HALO
    in_row, in_col = (row >= HALO) & (row < end), (col >= HALO) & (col < end)
    strip = jnp.where(
        (row < HALO) & in_col, row * SIDE + col - HALO,
        jnp.where((row >= end) & in_col, STRIP + (row - end) * SIDE + col - HALO,
        jnp.where((col < HALO) & in_row, 2 * STRIP + col * SIDE + row - HALO,
        jnp.where((col >= end) & in_row, 3 * STRIP + (col - end) * SIDE + row - HALO, -1))),
    )
    strip = jnp.where(y < FULL, strip, -1)
    own = (x >= HALO) & (x < end) & (y >= HALO) & (y < end)
    source = jnp.where(own, (x - HALO) * SIDE + y - HALO, jnp.where(strip >= 0, strip + CELLS, -1))
    place = (source[:, None] == jnp.arange(CELLS + 4 * STRIP, dtype=jnp.int32)[None]).astype(BF16)
    back = (jnp.arange(4 * STRIP, dtype=jnp.int32)[:, None] == strip[None]).astype(BF16)

    q = jnp.arange(CELLS, dtype=jnp.int32)
    row, col = turned(spin, q // SIDE, q % SIDE, SIDE - 1)
    cut = SIDE - HALO
    by_row = jnp.where(row >= cut, (row - cut) * SIDE + col, jnp.where(row < HALO, STRIP + row * SIDE + col, -1))
    by_col = jnp.where(col >= cut, 2 * STRIP + (col - cut) * SIDE + row, jnp.where(col < HALO, 3 * STRIP + col * SIDE + row, -1))
    k = jnp.arange(4 * STRIP, dtype=jnp.int32)
    pick = ((k[:, None] == by_row[None]) | (k[:, None] == by_col[None])).astype(BF16)
    add = ((by_row[:, None] == k[None]) | (by_col[:, None] == k[None])).astype(BF16)
    return place, back, pick, add


def exchange(strips, forth):
    moves = (("face", 1), ("face", -1), ("tile", 1), ("tile", -1))
    out = []
    for strip, (axis, way) in zip(strips, moves):
        size, way = lax.axis_size(axis), way if forth else -way
        out.append(lax.ppermute(strip, axis, [(i, (i + way) % size) for i in range(size)]))
    return out


def on_device(
    obs_values, obs_tile, interp, tile_spin, w_embed, dw_kernel, norm_gain, w_one, w_two, cotangent
):
    tiles = lax.axis_size(BOTH)
    width, channels = w_embed.shape
    hidden = w_one.shape[1]
    slots = interp.shape[2]
    place, back, pick, add = selectors(tile_spin[0, 0])
    taps = jnp.broadcast_to(
        dw_kernel.astype(F32).reshape(TAPS * TAPS, 1, 4, LANE), (TAPS * TAPS, 2, 4, LANE)
    ).reshape(TAPS * TAPS * 8, LANE)
    gain = norm_gain.astype(F32)[None]
    weights = jnp.concatenate([interp[0], interp[0]], axis=1).reshape(tiles * 2 * slots, CELLS).T

    (leaving,) = call(
        route_kernel, [((tiles * 8, LANE), BF16)], [], 16,
        obs_tile, obs_tile.reshape(1, -1), obs_values,
    )
    arrived = lax.all_to_all(leaving.reshape(tiles, 8, LANE), BOTH, 0, 0, tiled=True)
    d_active = dot(cotangent, w_two, NT)

    strip = ((STRIP, channels), BF16)
    gridded, embedded, *strips = call(
        embed_kernel, [((CELLS, width), BF16), ((CELLS, channels), BF16)] + [strip] * 4, [], 16,
        arrived.reshape(tiles * 8, LANE), weights, w_embed, pick,
    )
    strips = exchange(strips, True)
    cells2 = ROWS2 * PITCH * 8
    field, normal, inverse, active, d_hidden, grad_one, grad_two = call(
        forward_kernel,
        [
            ((cells2, LANE), F32),
            ((CELLS, channels), F32),
            ((CELLS, LANE), F32),
            ((CELLS, hidden), BF16),
            ((CELLS, hidden), BF16),
            ((channels, hidden), BF16),
            ((hidden, channels), BF16),
        ],
        [
            ((CELLS + 4 * STRIP, channels), BF16),
            ((FULL * PITCH, channels), F32),
            ((CELLS * 4, LANE), F32),
            ((CELLS, channels), BF16),
        ],
        40,
        embedded, *strips, place, taps, gain, w_one, d_active, cotangent,
    )
    grad_one, grad_two = lax.psum((grad_one, grad_two), BOTH)

    output, grad_taps, grad_gain, inner, *strips = call(
        backward_kernel,
        [
            ((CELLS, channels), BF16),
            ((TAPS * TAPS * 8, LANE), F32),
            ((1, channels), F32),
            ((CELLS, channels), F32),
        ]
        + [strip] * 4,
        [
            ((CELLS, channels), F32),
            ((CELLS * 4, LANE), F32),
            ((cells2, LANE), F32),
            ((FULL * PITCH, channels), F32),
        ],
        40,
        embedded, field, normal, inverse, active, d_hidden, w_one, w_two, gain, taps, cotangent, back,
    )
    strips = exchange(strips, False)
    (grad_embed,) = call(
        collect_kernel, [((width, channels), F32)], [((4 * STRIP, channels), BF16)], 16,
        inner, *strips, add, gridded,
    )
    grad_kernel = jnp.sum(grad_taps.reshape(TAPS * TAPS, 2, 4 * LANE), axis=1)
    small = jnp.concatenate([grad_embed, grad_kernel, grad_gain], axis=0)
    small = lax.psum(small, BOTH)
    return (
        output,
        small[:width],
        small[width : width + TAPS * TAPS],
        small[width + TAPS * TAPS],
        grad_one.astype(F32),
        grad_two.astype(F32),
    )


def solution(mesh):
    split = P(BOTH, None)
    in_specs = (split, split, P(BOTH, None, None, None), split) + (P(),) * 5 + (split,)
    return jax.shard_map(
        on_device, mesh=mesh, in_specs=in_specs, out_specs=(split,) + (P(),) * 5, check_vma=False
    )
```

```python
import jax
import jax.numpy as jnp
from jax import lax
from jax.experimental import pallas as pl
from jax.experimental.pallas import tpu as pltpu
from jax.sharding import PartitionSpec as P

F32 = jnp.float32
BF16 = jnp.bfloat16
SIDE = 16
CELLS = SIDE * SIDE
HALO = 3
TAPS = 7
FULL = SIDE + 2 * HALO
PITCH = 24
HALF = SIDE // 2
LANE = 128
ROWS2 = HALF + TAPS - 1
STRIP = HALO * SIDE
STEP = 256
ALL = ("face", "col", "core")
CHIPS = ("face", "col")
ROOT = 0.7978845608028654
CUBE = 0.044715

NN = (((1,), (0,)), ((), ()))
NT = (((1,), (1,)), ((), ()))
TN = (((0,), (0,)), ((), ()))


def dot(a, b, dims=NN):
    return lax.dot_general(a, b, dims, preferred_element_type=F32)


def call(kernel, outs, scratch, limit, *args):
    vmem, scalar = pl.BlockSpec(memory_space=pltpu.VMEM), pl.BlockSpec(memory_space=pltpu.SMEM)
    return pl.pallas_call(
        kernel,
        out_shape=[jax.ShapeDtypeStruct(s, d) for s, d in outs],
        in_specs=[scalar if a.shape == (1,) else vmem for a in args],
        out_specs=[vmem] * len(outs),
        scratch_shapes=[pltpu.VMEM(s, d) for s, d in scratch],
        compiler_params=pltpu.CompilerParams(vmem_limit_bytes=limit * 2**20),
    )(*args)


def block(i, j, pitch):
    return pl.ds(pl.multiple_of((i * pitch + j) * 8, 8), 8)


def comb(i, j, pitch, h, cb):
    return pl.ds((i * pitch + j) * 8 + h * 4 + cb, 8, stride=8)


def route_kernel(col_ref, row_ref, obs_ref, out_ref):
    row = row_ref[...]
    count = row.shape[1]
    earlier = lax.broadcasted_iota(jnp.int32, (count, count), 0) < lax.broadcasted_iota(
        jnp.int32, (count, count), 1
    )
    same = jnp.where((col_ref[...] == row) & earlier, 1.0, 0.0)
    rank = jnp.sum(same, axis=0, keepdims=True).astype(jnp.int32)
    place = row * 8 + rank
    lines = out_ref.shape[0]
    line = lax.broadcasted_iota(jnp.int32, (lines, count), 0)
    chosen = jnp.where((line - (line & 4)) == place, 1.0, 0.0).astype(BF16)
    moved = dot(chosen, obs_ref[...])
    first = (lax.broadcasted_iota(jnp.int32, (lines, LANE), 0) & 4) == 0
    out_ref[...] = jnp.where(first, moved[:, :LANE], moved[:, LANE:]).astype(BF16)


def embed_kernel(got_ref, weights_ref, w_embed_ref, pick_ref, grid_ref, emb_ref, *strip_refs):
    got = got_ref[...].astype(F32)
    first = (lax.broadcasted_iota(jnp.int32, got.shape, 0) & 4) == 0
    spread = jnp.concatenate(
        [jnp.where(first, got, 0.0), jnp.where(first, 0.0, got)], axis=1
    ).astype(BF16)
    gridded = dot(weights_ref[...], spread).astype(BF16)
    grid_ref[...] = gridded
    emb_ref[...] = dot(gridded, w_embed_ref[...]).astype(BF16)
    strips = dot(pick_ref[...], gridded).astype(BF16)
    for k, ref in enumerate(strip_refs):
        ref[...] = strips[k * STRIP : (k + 1) * STRIP]


def tiles_of(part, two, one):
    for k in range(64):
        r, c = divmod(k, 4)
        yield part * 128 + k, two, pl.ds(r * 16, 16), pl.ds(c * LANE, LANE)
    for k in range(64):
        r, c = divmod(k, 2)
        yield part * 128 + 64 + k, one, pl.ds(r * 16, 16), pl.ds(c * LANE, LANE)


def forward_kernel(
    core_ref, emb_ref, s0, s1, s2, s3, place_ref, kern_ref, gain_ref, w_embed_ref, w_one_ref, d_act_ref, cot_ref,
    field_ref, normal_ref, inv_ref, scaled_ref, active_ref, d_hid_ref, theirs_ref,
    strips_ref, cells_ref, flat_ref, conv_ref, two_ref, one_ref,
):
    for k, ref in enumerate((s0, s1, s2, s3)):
        strips_ref[k * STRIP : (k + 1) * STRIP] = ref[...]
    cells_ref[0:CELLS] = emb_ref[...]
    cells_ref[CELLS:] = dot(strips_ref[...], w_embed_ref[...]).astype(BF16)
    flat_ref[...] = dot(place_ref[...], cells_ref[...])
    for x in range(FULL):
        for g in range(3):
            for cb in range(4):
                value = flat_ref[pl.ds(x * PITCH + 8 * g, 8), pl.ds(cb * LANE, LANE)]
                if x < ROWS2:
                    field_ref[comb(x, 8 * g, PITCH, 0, cb), :] = value
                if x >= HALF:
                    field_ref[comb(x - HALF, 8 * g, PITCH, 1, cb), :] = value

    def conv_row(i, carry):
        sums = [jnp.zeros((8, LANE), F32)] * SIDE
        for a in range(TAPS):
            taps = [kern_ref[pl.ds((a * TAPS + b) * 8, 8), :] for b in range(TAPS)]
            for y in range(FULL):
                here = field_ref[block(i + a, y, PITCH), :]
                for b in range(TAPS):
                    if 0 <= y - b < SIDE:
                        sums[y - b] = sums[y - b] + here * taps[b]
        for j in range(SIDE):
            conv_ref[block(i, j, SIDE), :] = sums[j]
        return carry

    lax.fori_loop(0, HALF, conv_row, 0)

    for r in range(SIDE):
        h, i = divmod(r, HALF)
        parts = [
            jnp.concatenate([conv_ref[comb(i, 8 * g, SIDE, h, cb), :] for g in range(2)], axis=0)
            for cb in range(4)
        ]
        value = jnp.concatenate(parts, axis=1)
        centred = value - jnp.mean(value, axis=1, keepdims=True)
        inverse = lax.rsqrt(jnp.mean(centred * centred, axis=1, keepdims=True) + 1e-06)
        normal = centred * inverse
        rows = pl.ds(r * SIDE, SIDE)
        normal_ref[rows, :] = normal
        inv_ref[rows, :] = jnp.broadcast_to(inverse, (SIDE, LANE))
        scaled_ref[rows, :] = (normal * gain_ref[...]).astype(BF16)

    for k in range(w_one_ref.shape[1] // STEP):
        some = pl.ds(k * STEP, STEP)
        pre = dot(scaled_ref[...], w_one_ref[:, some])
        square = pre * pre
        tanh = jnp.tanh(pre * (ROOT + (ROOT * CUBE) * square))
        upper = 0.5 + 0.5 * tanh
        slope = upper + (0.5 * pre) * (1.0 - tanh * tanh) * (ROOT + (3.0 * ROOT * CUBE) * square)
        active_ref[:, some] = (pre * upper).astype(BF16)
        d_hid_ref[:, some] = (d_act_ref[:, some] * slope).astype(BF16)

    steps = theirs_ref.shape[0] // 128
    for k in range(steps):
        some = pl.ds(pl.multiple_of(((1 - core_ref[0]) * steps + k) * STEP, STEP), STEP)
        two_ref[...] = dot(active_ref[:, some], cot_ref[...], TN)
        one_ref[...] = dot(scaled_ref[...], d_hid_ref[:, some], TN)
        for t, ref, rows, lanes in tiles_of(k, two_ref, one_ref):
            theirs_ref[t] = ref[rows, lanes].astype(BF16)


def backward_kernel(
    core_ref, grid_ref, s0, s1, s2, s3, place_ref, field_ref, normal_ref, inv_ref, d_hid_ref, w_one_ref,
    gain_ref, kern_ref, cot_ref,
    mine_ref, theirs_ref,
    d_scaled_ref, d_conv_ref, spread_ref, flat_ref, taps_ref, cells_ref, small_ref,
):
    d_scaled_ref[...] = dot(d_hid_ref[...], w_one_ref[...], NT)
    total = jnp.zeros((SIDE, normal_ref.shape[1]), F32)
    for r in range(SIDE):
        h, i = divmod(r, HALF)
        rows = pl.ds(r * SIDE, SIDE)
        normal, d_scaled = normal_ref[rows, :], d_scaled_ref[rows, :]
        total = total + d_scaled * normal
        d_normal = d_scaled * gain_ref[...]
        mean = jnp.mean(d_normal, axis=1, keepdims=True)
        along = jnp.mean(d_normal * normal, axis=1, keepdims=True)
        d_conv = (d_normal - mean - normal * along) * inv_ref[rows, 0:1]
        for g in range(2):
            for cb in range(4):
                d_conv_ref[comb(i, 8 * g, SIDE, h, cb), :] = d_conv[
                    8 * g : 8 * g + 8, cb * LANE : (cb + 1) * LANE
                ]
    grad_gain = jnp.sum(total, axis=0, keepdims=True)

    spread_ref[...] = jnp.zeros_like(spread_ref)
    taps_ref[...] = jnp.zeros_like(taps_ref)

    def conv_row(i, carry):
        for a in range(TAPS):
            taps = [kern_ref[pl.ds((a * TAPS + b) * 8, 8), :] for b in range(TAPS)]
            for y in range(FULL):
                value = spread_ref[block(i + a, y, PITCH), :]
                for b in range(TAPS):
                    if 0 <= y - b < SIDE:
                        value = value + d_conv_ref[block(i, y - b, SIDE), :] * taps[b]
                spread_ref[block(i + a, y, PITCH), :] = value
        return carry

    lax.fori_loop(0, HALF, conv_row, 0)

    def tap_row(i, carry):
        for a in range(TAPS):
            sums = [taps_ref[pl.ds((a * TAPS + b) * 8, 8), :] for b in range(TAPS)]
            for y in range(FULL):
                here = field_ref[block(i + a, y, PITCH), :]
                for b in range(TAPS):
                    if 0 <= y - b < SIDE:
                        sums[b] = sums[b] + here * d_conv_ref[block(i, y - b, SIDE), :]
            for b in range(TAPS):
                taps_ref[pl.ds((a * TAPS + b) * 8, 8), :] = sums[b]
        return carry

    lax.fori_loop(0, HALF, tap_row, 0)

    for x in range(FULL):
        for g in range(3):
            for cb in range(4):
                value = None
                if x < ROWS2:
                    value = spread_ref[comb(x, 8 * g, PITCH, 0, cb), :]
                if x >= HALF:
                    more = spread_ref[comb(x - HALF, 8 * g, PITCH, 1, cb), :]
                    value = more if value is None else value + more
                flat_ref[pl.ds(x * PITCH + 8 * g, 8), pl.ds(cb * LANE, LANE)] = value

    cells_ref[0:CELLS] = grid_ref[...]
    for k, ref in enumerate((s0, s1, s2, s3)):
        cells_ref[CELLS + k * STRIP : CELLS + (k + 1) * STRIP] = ref[...]
    spots = dot(place_ref[...], cells_ref[...]).astype(BF16)
    grad_embed = dot(spots, flat_ref[...].astype(BF16), TN) + dot(grid_ref[...], cot_ref[...], TN)

    half = mine_ref.shape[0]
    small_ref[...] = jnp.zeros_like(small_ref)
    for t in range(half):
        r, c = divmod(t, 4)
        small_ref[t * 16 : (t + 1) * 16] = grad_embed[r * 16 : (r + 1) * 16, c * LANE : (c + 1) * LANE]
    base = half * 16
    for t in range(TAPS * TAPS):
        both = taps_ref[t * 8 : (t + 1) * 8, :]
        small_ref[base + t * 4 : base + (t + 1) * 4] = both[:4] + both[4:]
    for c in range(4):
        at = base + TAPS * TAPS * 4 + c
        small_ref[at : at + 1] = grad_gain[:, c * LANE : (c + 1) * LANE]
    core = core_ref[0]
    for t in range(half):
        mine_ref[t] = small_ref[pl.ds(pl.multiple_of((core * half + t) * 16, 16), 16), :]
        theirs_ref[t] = small_ref[
            pl.ds(pl.multiple_of(((1 - core) * half + t) * 16, 16), 16), :
        ].astype(BF16)


def pair_kernel(
    core_ref, scaled_ref, active_ref, d_hid_ref, cot_ref, big_ref, mine_ref, small_ref, out_ref, two_ref, one_ref
):
    steps = big_ref.shape[0] // 128
    for k in range(steps):
        some = pl.ds(pl.multiple_of((core_ref[0] * steps + k) * STEP, STEP), STEP)
        two_ref[...] = dot(active_ref[:, some], cot_ref[...], TN)
        one_ref[...] = dot(scaled_ref[...], d_hid_ref[:, some], TN)
        for t, ref, rows, lanes in tiles_of(k, two_ref, one_ref):
            out_ref[t // 8, t % 8] = (ref[rows, lanes] + big_ref[t].astype(F32)).astype(BF16)
    for t in range(out_ref.shape[0]):
        out_ref[t, 8] = (mine_ref[t] + small_ref[t].astype(F32)).astype(BF16)


def feature_kernel(emb_ref, active_ref, w_two_ref, out_ref):
    out_ref[...] = (emb_ref[...].astype(F32) + dot(active_ref[...], w_two_ref[...])).astype(BF16)


def sum_kernel(in_ref, out_ref):
    parts, tiles = in_ref.shape[:2]

    def add(d, sums):
        return [s + in_ref[d, t].astype(F32) for t, s in enumerate(sums)]

    sums = lax.fori_loop(0, parts, add, [jnp.zeros(in_ref.shape[2:], F32)] * tiles)
    sums = [s.astype(BF16) for s in sums]

    def spread(d, carry):
        for t in range(tiles):
            out_ref[d, t] = sums[t]
        return carry

    lax.fori_loop(0, parts, spread, 0)


def assemble_kernel(core_ref, in_ref, *refs):
    one_ref, two_ref = refs[-2:]
    for t, ref, rows, lanes in tiles_of(0, two_ref, one_ref):
        ref[rows, lanes] = in_ref[t // 8, t % 8].astype(F32)


def assemble(core, gathered, shapes, before):
    steps = shapes[0][1] // STEP // 2
    whole = [pl.BlockSpec(memory_space=pl.ANY)] * len(before)
    return pl.pallas_call(
        assemble_kernel,
        out_shape=[jax.ShapeDtypeStruct(s, F32) for s in shapes],
        grid_spec=pltpu.PrefetchScalarGridSpec(
            num_scalar_prefetch=1,
            grid=(steps,),
            in_specs=[pl.BlockSpec((16,) + gathered.shape[1:], lambda k, core: (k, 0, 0, 0))] + whole,
            out_specs=[
                pl.BlockSpec((shapes[0][0], STEP), lambda k, core: (0, core[0] * steps + k)),
                pl.BlockSpec((STEP, shapes[1][1]), lambda k, core: (core[0] * steps + k, 0)),
            ],
        ),
        input_output_aliases={2 + k: k for k in range(len(before))},
        compiler_params=pltpu.CompilerParams(vmem_limit_bytes=24 * 2**20),
    )(core, gathered, *before)


def turned(spin, x, y, last):
    row = jnp.where(spin == 0, x, jnp.where(spin == 1, last - y, jnp.where(spin == 2, last - x, y)))
    col = jnp.where(spin == 0, y, jnp.where(spin == 1, x, jnp.where(spin == 2, last - y, last - x)))
    return row, col


def selectors(spin):
    p = jnp.arange(FULL * PITCH, dtype=jnp.int32)
    x, y = p // PITCH, p % PITCH
    row, col = turned(spin, x, y, FULL - 1)
    end = SIDE + HALO
    in_row, in_col = (row >= HALO) & (row < end), (col >= HALO) & (col < end)
    strip = jnp.where(
        (row < HALO) & in_col, row * SIDE + col - HALO,
        jnp.where((row >= end) & in_col, STRIP + (row - end) * SIDE + col - HALO,
        jnp.where((col < HALO) & in_row, 2 * STRIP + col * SIDE + row - HALO,
        jnp.where((col >= end) & in_row, 3 * STRIP + (col - end) * SIDE + row - HALO, -1))),
    )
    strip = jnp.where(y < FULL, strip, -1)
    own = (x >= HALO) & (x < end) & (y >= HALO) & (y < end)
    source = jnp.where(own, (x - HALO) * SIDE + y - HALO, jnp.where(strip >= 0, strip + CELLS, -1))
    place = (source[:, None] == jnp.arange(CELLS + 4 * STRIP, dtype=jnp.int32)[None]).astype(BF16)

    q = jnp.arange(CELLS, dtype=jnp.int32)
    row, col = turned(spin, q // SIDE, q % SIDE, SIDE - 1)
    cut = SIDE - HALO
    by_row = jnp.where(row >= cut, (row - cut) * SIDE + col, jnp.where(row < HALO, STRIP + row * SIDE + col, -1))
    by_col = jnp.where(col >= cut, 2 * STRIP + (col - cut) * SIDE + row, jnp.where(col < HALO, 3 * STRIP + col * SIDE + row, -1))
    k = jnp.arange(4 * STRIP, dtype=jnp.int32)
    pick = ((k[:, None] == by_row[None]) | (k[:, None] == by_col[None])).astype(BF16)
    return place, pick


def exchange(strips):
    moves = (("face", 1), ("face", -1), (("col", "core"), 1), (("col", "core"), -1))
    out = []
    for strip, (axis, way) in zip(strips, moves):
        size = lax.axis_size(axis)
        out.append(lax.ppermute(strip, axis, [(i, (i + way) % size) for i in range(size)]))
    return out


def swap(value):
    return lax.ppermute(value, "core", [(0, 1), (1, 0)])


def on_device(
    obs_values, obs_tile, interp, tile_spin, w_embed, dw_kernel, norm_gain, w_one, w_two, cotangent
):
    tiles, chips = lax.axis_size(ALL), lax.axis_size(CHIPS)
    width, channels = w_embed.shape
    hidden = w_one.shape[1]
    slots = interp.shape[2]
    core = lax.axis_index("core").reshape(1)
    place, pick = selectors(tile_spin[0, 0])
    taps = jnp.broadcast_to(
        dw_kernel.astype(F32).reshape(TAPS * TAPS, 1, 4, LANE), (TAPS * TAPS, 2, 4, LANE)
    ).reshape(TAPS * TAPS * 8, LANE)
    gain = norm_gain.astype(F32)[None]
    weights = jnp.concatenate([interp[0], interp[0]], axis=1).reshape(tiles * 2 * slots, CELLS).T

    (leaving,) = call(
        route_kernel, [((tiles * 8, LANE), BF16)], [], 16,
        obs_tile, obs_tile.reshape(1, -1), obs_values,
    )
    arrived = lax.all_to_all(leaving.reshape(tiles, 8, LANE), ALL, 0, 0, tiled=True)
    d_active = dot(cotangent, w_two, NT)

    gridded, embedded, *strips = call(
        embed_kernel,
        [((CELLS, width), BF16), ((CELLS, channels), BF16)] + [((STRIP, width), BF16)] * 4, [], 16,
        arrived.reshape(tiles * 8, LANE), weights, w_embed, pick,
    )
    strips = exchange(strips)
    cells2 = ROWS2 * PITCH * 8
    flat = ((FULL * PITCH, channels), F32)
    step_sums = [((STEP, channels), F32), ((channels, STEP), F32)]
    half = hidden * channels // (16 * LANE)
    field, normal, inverse, scaled, active, d_hidden, theirs = call(
        forward_kernel,
        [
            ((cells2, LANE), F32),
            ((CELLS, channels), F32),
            ((CELLS, LANE), F32),
            ((CELLS, channels), BF16),
            ((CELLS, hidden), BF16),
            ((CELLS, hidden), BF16),
            ((half, 16, LANE), BF16),
        ],
        [
            ((4 * STRIP, width), BF16),
            ((CELLS + 4 * STRIP, channels), BF16),
            flat,
            ((CELLS * 4, LANE), F32),
        ]
        + step_sums,
        40,
        core, embedded, *strips, place, taps, gain, w_embed, w_one, d_active, cotangent,
    )
    big = swap(theirs)

    mine, theirs = call(
        backward_kernel,
        [((chips, 16, LANE), F32), ((chips, 16, LANE), BF16)],
        [
            ((CELLS, channels), F32),
            ((CELLS * 4, LANE), F32),
            ((cells2, LANE), F32),
            flat,
            ((TAPS * TAPS * 8, LANE), F32),
            ((CELLS + 4 * STRIP, width), BF16),
            ((2 * chips * 16, LANE), F32),
        ],
        40,
        core, gridded, *strips, place, field, normal, inverse, d_hidden, w_one, gain, taps, cotangent,
    )
    small = swap(theirs)
    (paired,) = call(
        pair_kernel, [((chips, 9, 16, LANE), BF16)], step_sums, 40,
        core, scaled, active, d_hidden, cotangent, big, mine, small,
    )
    (output,) = call(
        feature_kernel, [((CELLS, channels), BF16)], [], 16, embedded, active, w_two
    )
    paired = lax.all_to_all(paired, CHIPS, 0, 0, tiled=True)
    (summed,) = call(sum_kernel, [((chips, 9, 16, LANE), BF16)], [], 16, paired)
    here = lax.all_to_all(summed, CHIPS, 0, 0, tiled=True)
    there = swap(here)
    shapes = [(channels, hidden), (hidden, channels)]
    grads = assemble(core, here, shapes, [])
    grad_one, grad_two = assemble(1 - core, there, shapes, grads)

    first = jnp.where(core[0] == 0, here[:, 8], there[:, 8]).astype(F32)
    last = jnp.where(core[0] == 0, there[:, 8], here[:, 8]).astype(F32)
    grad_embed = first.reshape(16, 4, 16, LANE).transpose(0, 2, 1, 3).reshape(width, channels)
    count = TAPS * TAPS
    rows = last.reshape(chips * 16, LANE)[: (count + 1) * 4].reshape(count + 1, channels)
    return output, grad_embed, rows[:count], rows[count], grad_one, grad_two


def solution(mesh):
    faces, tiles = mesh.shape["face"], mesh.shape["tile"]
    fine = jax.sharding.Mesh(mesh.devices.reshape(faces, tiles // 2, 2), ALL)
    split = P(ALL, None)
    in_specs = (split, split, P(ALL, None, None, None), split) + (P(),) * 5 + (split,)
    return jax.shard_map(
        on_device, mesh=fine, in_specs=in_specs, out_specs=(split,) + (P(),) * 5, check_vma=False
    )
```

```python
import jax
import jax.numpy as jnp
from jax import lax
from jax.experimental import pallas as pl
from jax.experimental.pallas import tpu as pltpu
from jax.sharding import PartitionSpec as P

F32 = jnp.float32
BF16 = jnp.bfloat16
SIDE = 16
CELLS = SIDE * SIDE
HALO = 3
TAPS = 7
FULL = SIDE + 2 * HALO
PITCH = 24
HALF = SIDE // 2
LANE = 128
ROWS2 = HALF + TAPS - 1
STRIP = HALO * SIDE
STEP = 256
ALL = ("face", "col", "core")
CHIPS = ("face", "col")
ROOT = 0.7978845608028654
CUBE = 0.044715

NN = (((1,), (0,)), ((), ()))
NT = (((1,), (1,)), ((), ()))
TN = (((0,), (0,)), ((), ()))


def dot(a, b, dims=NN):
    return lax.dot_general(a, b, dims, preferred_element_type=F32)


def call(kernel, outs, scratch, limit, *args, far=(), far_outs=(), copies=0, aliases=None):
    vmem, scalar = pl.BlockSpec(memory_space=pltpu.VMEM), pl.BlockSpec(memory_space=pltpu.SMEM)
    away = pl.BlockSpec(memory_space=pl.ANY)
    return pl.pallas_call(
        kernel,
        out_shape=[jax.ShapeDtypeStruct(s, d) for s, d in outs],
        in_specs=[
            scalar if a.shape == (1,) else away if k in far else vmem for k, a in enumerate(args)
        ],
        out_specs=[away if k in far_outs else vmem for k in range(len(outs))],
        scratch_shapes=[pltpu.VMEM(s, d) for s, d in scratch]
        + [pltpu.SemaphoreType.DMA((copies,))] * bool(copies),
        input_output_aliases=aliases or {},
        compiler_params=pltpu.CompilerParams(vmem_limit_bytes=limit * 2**20),
    )(*args)


def start(sem, *pairs):
    moves = [pltpu.make_async_copy(a, b, sem.at[k]) for k, (a, b) in enumerate(pairs)]
    for move in moves:
        move.start()
    return moves


def block(i, j, pitch):
    return pl.ds(pl.multiple_of((i * pitch + j) * 8, 8), 8)


def comb(i, j, pitch, h, cb):
    return pl.ds((i * pitch + j) * 8 + h * 4 + cb, 8, stride=8)


def route_kernel(row_far, obs_far, out_ref, row_ref, obs_ref, sem):
    fetch_row, fetch_obs = start(sem, (row_far, row_ref), (obs_far, obs_ref))
    fetch_row.wait()
    row = row_ref[...]
    count = row.shape[1]
    across = jnp.broadcast_to(row, (count, count)).astype(F32)
    earlier = lax.broadcasted_iota(jnp.int32, (count, count), 0) < lax.broadcasted_iota(
        jnp.int32, (count, count), 1
    )
    same = jnp.where((across.T == across) & earlier, 1.0, 0.0)
    rank = jnp.sum(same, axis=0, keepdims=True).astype(jnp.int32)
    place = row * 8 + rank
    lines = out_ref.shape[0]
    line = lax.broadcasted_iota(jnp.int32, (lines, count), 0)
    chosen = jnp.where((line - (line & 4)) == place, 1.0, 0.0).astype(BF16)
    fetch_obs.wait()
    moved = dot(chosen, obs_ref[...])
    first = (lax.broadcasted_iota(jnp.int32, (lines, LANE), 0) & 4) == 0
    out_ref[...] = jnp.where(first, moved[:, :LANE], moved[:, LANE:]).astype(BF16)


def prepare_kernel(interp_ref, cot_ref, w_two_ref, weights_ref, d_act_ref):
    weights = interp_ref[...].astype(F32)
    tiles, slots = weights.shape[:2]
    for k in range(slots):
        weights_ref[:, k * tiles : (k + 1) * tiles] = weights[:, k, :].T.astype(BF16)
    for k in range(w_two_ref.shape[0] // STEP):
        some = pl.ds(k * STEP, STEP)
        d_act_ref[:, some] = dot(cot_ref[...], w_two_ref[some, :], NT)


def embed_kernel(
    got_ref, weights_ref, w_embed_ref, pick_ref, grid_ref, emb_ref, s0, s1, s2, s3, wide_ref, rows_ref
):
    wide_ref[...] = got_ref[...].astype(F32)
    tiles = got_ref.shape[0] // 8
    for k in range(4):
        for half in range(2):
            for g in range(0, tiles, 16):
                two = [
                    wide_ref[pl.ds((g + e) * 8 + half * 4 + k, 8, stride=8), :] for e in (0, 8)
                ]
                rows_ref[pl.ds(k * tiles + g, 16), pl.ds(half * LANE, LANE)] = jnp.concatenate(
                    two, axis=0
                ).astype(BF16)
    gridded = dot(weights_ref[...], rows_ref[...]).astype(BF16)
    grid_ref[...] = gridded
    strips = dot(pick_ref[...], gridded).astype(BF16)
    for k, ref in enumerate((s0, s1, s2, s3)):
        ref[...] = strips[k * STRIP : (k + 1) * STRIP]
    emb_ref[...] = dot(gridded, w_embed_ref[...]).astype(BF16)


def tiles_of(part, two, one):
    for k in range(64):
        r, c = divmod(k, 4)
        yield part * 128 + k, two, pl.ds(r * 16, 16), pl.ds(c * LANE, LANE)
    for k in range(64):
        r, c = divmod(k, 2)
        yield part * 128 + 64 + k, one, pl.ds(r * 16, 16), pl.ds(c * LANE, LANE)


def forward_kernel(
    core_ref, emb_ref, s0, s1, s2, s3, place_ref, dw_ref, gain_ref, w_embed_ref, w_one_ref, d_act_far, cot_ref,
    field_ref, normal_ref, inv_ref, scaled_ref, active_ref, d_hid_ref, kern_ref, theirs_ref,
    strips_ref, cells_ref, flat_ref, conv_ref, two_ref, one_ref, d_act_ref, sem,
):
    (fetch,) = start(sem, (d_act_far, d_act_ref))
    taps = dw_ref[...].astype(F32)
    last = taps.shape[0] - 1
    for h in range(2):
        for cb in range(4):
            lanes = slice(cb * LANE, (cb + 1) * LANE)
            for g in range(0, last, 8):
                kern_ref[pl.ds(g * 8 + h * 4 + cb, 8, stride=8), :] = taps[g : g + 8, lanes]
            kern_ref[pl.ds(last * 8 + h * 4 + cb, 1), :] = taps[last:, lanes]
    for k, ref in enumerate((s0, s1, s2, s3)):
        strips_ref[k * STRIP : (k + 1) * STRIP] = ref[...]
    cells_ref[0:CELLS] = emb_ref[...]
    cells_ref[CELLS:] = dot(strips_ref[...], w_embed_ref[...]).astype(BF16)
    flat_ref[...] = dot(place_ref[...], cells_ref[...])
    for x in range(FULL):
        for g in range(3):
            for cb in range(4):
                value = flat_ref[pl.ds(x * PITCH + 8 * g, 8), pl.ds(cb * LANE, LANE)]
                if x < ROWS2:
                    field_ref[comb(x, 8 * g, PITCH, 0, cb), :] = value
                if x >= HALF:
                    field_ref[comb(x - HALF, 8 * g, PITCH, 1, cb), :] = value

    def conv_row(i, carry):
        sums = [jnp.zeros((8, LANE), F32)] * SIDE
        for a in range(TAPS):
            taps = [kern_ref[pl.ds((a * TAPS + b) * 8, 8), :] for b in range(TAPS)]
            for y in range(FULL):
                here = field_ref[block(i + a, y, PITCH), :]
                for b in range(TAPS):
                    if 0 <= y - b < SIDE:
                        sums[y - b] = sums[y - b] + here * taps[b]
        for j in range(SIDE):
            conv_ref[block(i, j, SIDE), :] = sums[j]
        return carry

    lax.fori_loop(0, HALF, conv_row, 0)

    for r in range(SIDE):
        h, i = divmod(r, HALF)
        parts = [
            jnp.concatenate([conv_ref[comb(i, 8 * g, SIDE, h, cb), :] for g in range(2)], axis=0)
            for cb in range(4)
        ]
        value = jnp.concatenate(parts, axis=1)
        centred = value - jnp.mean(value, axis=1, keepdims=True)
        inverse = lax.rsqrt(jnp.mean(centred * centred, axis=1, keepdims=True) + 1e-06)
        normal = centred * inverse
        rows = pl.ds(r * SIDE, SIDE)
        normal_ref[rows, :] = normal
        inv_ref[rows, :] = jnp.broadcast_to(inverse, (SIDE, LANE))
        scaled_ref[rows, :] = (normal * gain_ref[...].astype(F32)).astype(BF16)

    fetch.wait()
    for k in range(w_one_ref.shape[1] // STEP):
        some = pl.ds(k * STEP, STEP)
        pre = dot(scaled_ref[...], w_one_ref[:, some])
        square = pre * pre
        tanh = jnp.tanh(pre * (ROOT + (ROOT * CUBE) * square))
        upper = 0.5 + 0.5 * tanh
        slope = upper + (0.5 * pre) * (1.0 - tanh * tanh) * (ROOT + (3.0 * ROOT * CUBE) * square)
        active_ref[:, some] = (pre * upper).astype(BF16)
        d_hid_ref[:, some] = (d_act_ref[:, some] * slope).astype(BF16)

    steps = theirs_ref.shape[0] // 128
    for k in range(steps):
        some = pl.ds(pl.multiple_of(((1 - core_ref[0]) * steps + k) * STEP, STEP), STEP)
        two_ref[...] = dot(active_ref[:, some], cot_ref[...], TN)
        one_ref[...] = dot(scaled_ref[...], d_hid_ref[:, some], TN)
        for t, ref, rows, lanes in tiles_of(k, two_ref, one_ref):
            theirs_ref[t] = ref[rows, lanes].astype(BF16)


def backward_kernel(
    core_ref, grid_ref, s0, s1, s2, s3, place_ref, field_ref, normal_ref, inv_ref, d_hid_ref, w_one_ref,
    gain_ref, kern_ref, cot_ref,
    mine_ref, theirs_ref,
    d_scaled_ref, d_conv_ref, spread_ref, flat_ref, taps_ref, cells_ref, small_ref,
):
    d_scaled_ref[...] = dot(d_hid_ref[...], w_one_ref[...], NT)
    total = jnp.zeros((SIDE, normal_ref.shape[1]), F32)
    for r in range(SIDE):
        h, i = divmod(r, HALF)
        rows = pl.ds(r * SIDE, SIDE)
        normal, d_scaled = normal_ref[rows, :], d_scaled_ref[rows, :]
        total = total + d_scaled * normal
        d_normal = d_scaled * gain_ref[...].astype(F32)
        mean = jnp.mean(d_normal, axis=1, keepdims=True)
        along = jnp.mean(d_normal * normal, axis=1, keepdims=True)
        d_conv = (d_normal - mean - normal * along) * inv_ref[rows, 0:1]
        for g in range(2):
            for cb in range(4):
                d_conv_ref[comb(i, 8 * g, SIDE, h, cb), :] = d_conv[
                    8 * g : 8 * g + 8, cb * LANE : (cb + 1) * LANE
                ]
    grad_gain = jnp.sum(total, axis=0, keepdims=True)

    spread_ref[...] = jnp.zeros_like(spread_ref)
    taps_ref[...] = jnp.zeros_like(taps_ref)

    def conv_row(i, carry):
        for a in range(TAPS):
            taps = [kern_ref[pl.ds((a * TAPS + b) * 8, 8), :] for b in range(TAPS)]
            for y in range(FULL):
                value = spread_ref[block(i + a, y, PITCH), :]
                for b in range(TAPS):
                    if 0 <= y - b < SIDE:
                        value = value + d_conv_ref[block(i, y - b, SIDE), :] * taps[b]
                spread_ref[block(i + a, y, PITCH), :] = value
        return carry

    lax.fori_loop(0, HALF, conv_row, 0)

    def tap_row(i, carry):
        for a in range(TAPS):
            sums = [taps_ref[pl.ds((a * TAPS + b) * 8, 8), :] for b in range(TAPS)]
            for y in range(FULL):
                here = field_ref[block(i + a, y, PITCH), :]
                for b in range(TAPS):
                    if 0 <= y - b < SIDE:
                        sums[b] = sums[b] + here * d_conv_ref[block(i, y - b, SIDE), :]
            for b in range(TAPS):
                taps_ref[pl.ds((a * TAPS + b) * 8, 8), :] = sums[b]
        return carry

    lax.fori_loop(0, HALF, tap_row, 0)

    for x in range(FULL):
        for g in range(3):
            for cb in range(4):
                value = None
                if x < ROWS2:
                    value = spread_ref[comb(x, 8 * g, PITCH, 0, cb), :]
                if x >= HALF:
                    more = spread_ref[comb(x - HALF, 8 * g, PITCH, 1, cb), :]
                    value = more if value is None else value + more
                flat_ref[pl.ds(x * PITCH + 8 * g, 8), pl.ds(cb * LANE, LANE)] = value

    cells_ref[0:CELLS] = grid_ref[...]
    for k, ref in enumerate((s0, s1, s2, s3)):
        cells_ref[CELLS + k * STRIP : CELLS + (k + 1) * STRIP] = ref[...]
    spots = dot(place_ref[...], cells_ref[...]).astype(BF16)
    grad_embed = dot(spots, flat_ref[...].astype(BF16), TN) + dot(grid_ref[...], cot_ref[...], TN)

    half = mine_ref.shape[0]
    small_ref[...] = jnp.zeros_like(small_ref)
    for t in range(half):
        r, c = divmod(t, 4)
        small_ref[t * 16 : (t + 1) * 16] = grad_embed[r * 16 : (r + 1) * 16, c * LANE : (c + 1) * LANE]
    base = half * 16
    for t in range(TAPS * TAPS):
        both = taps_ref[t * 8 : (t + 1) * 8, :]
        small_ref[base + t * 4 : base + (t + 1) * 4] = both[:4] + both[4:]
    for c in range(4):
        at = base + TAPS * TAPS * 4 + c
        small_ref[at : at + 1] = grad_gain[:, c * LANE : (c + 1) * LANE]
    core = core_ref[0]
    for t in range(half):
        mine_ref[t] = small_ref[pl.ds(pl.multiple_of((core * half + t) * 16, 16), 16), :]
        theirs_ref[t] = small_ref[
            pl.ds(pl.multiple_of(((1 - core) * half + t) * 16, 16), 16), :
        ].astype(BF16)


def pair_kernel(
    core_ref, scaled_ref, active_ref, d_hid_ref, cot_ref, big_ref, emb_ref, w_two_far,
    out_ref, feature_far,
    two_ref, one_ref, w_two_ref, feature_ref, sem,
):
    (fetch,) = start(sem, (w_two_far, w_two_ref))
    steps = big_ref.shape[0] // 128
    for k in range(steps):
        some = pl.ds(pl.multiple_of((core_ref[0] * steps + k) * STEP, STEP), STEP)
        two_ref[...] = dot(active_ref[:, some], cot_ref[...], TN)
        one_ref[...] = dot(scaled_ref[...], d_hid_ref[:, some], TN)
        for t, ref, rows, lanes in tiles_of(k, two_ref, one_ref):
            out_ref[t // 8, t % 8] = (ref[rows, lanes] + big_ref[t].astype(F32)).astype(BF16)
    fetch.wait()
    feature_ref[...] = (emb_ref[...].astype(F32) + dot(active_ref[...], w_two_ref[...])).astype(BF16)
    put = pltpu.make_async_copy(feature_ref, feature_far, sem.at[1])
    put.start()
    put.wait()


def join_kernel(mine_ref, small_ref, paired_far, out_far, tile_ref, sem):
    tile_ref[...] = (mine_ref[...] + small_ref[...].astype(F32)).astype(BF16)
    put = pltpu.make_async_copy(tile_ref, out_far.at[:, 8], sem.at[0])
    put.start()
    put.wait()


def sum_kernel(in_ref, out_ref):
    parts, tiles = in_ref.shape[:2]

    def add(d, sums):
        return [s + in_ref[d, t].astype(F32) for t, s in enumerate(sums)]

    sums = lax.fori_loop(0, parts, add, [jnp.zeros(in_ref.shape[2:], F32)] * tiles)
    sums = [s.astype(BF16) for s in sums]

    def spread(d, carry):
        for t in range(tiles):
            out_ref[d, t] = sums[t]
        return carry

    lax.fori_loop(0, parts, spread, 0)


def assemble_half(core, in_ref, one_far, two_far, one_ref, two_ref, sem):
    steps = one_ref.shape[0]
    puts = []
    for k in range(steps):
        for t, ref, rows, lanes in tiles_of(k, two_ref, one_ref):
            ref[k, rows, lanes] = in_ref[t // 8, t % 8].astype(F32)
        some = pl.ds(pl.multiple_of((core * steps + k) * STEP, STEP), STEP)
        puts += [
            pltpu.make_async_copy(one_ref.at[k], one_far.at[:, some], sem.at[2 * k]),
            pltpu.make_async_copy(two_ref.at[k], two_far.at[some, :], sem.at[2 * k + 1]),
        ]
        puts[-2].start()
        puts[-1].start()
    return puts


def first_kernel(core_ref, in_ref, one_far, two_far, one_ref, two_ref, sem):
    for put in assemble_half(core_ref[0], in_ref, one_far, two_far, one_ref, two_ref, sem):
        put.wait()


def second_kernel(
    core_ref, in_ref, mine_ref, one_old, two_old,
    one_far, two_far, embed_far, taps_far, gain_far,
    one_ref, two_ref, rows_ref, embed_ref, taps_ref, gain_ref, sem,
):
    core = core_ref[0]
    puts = assemble_half(1 - core, in_ref, one_far, two_far, one_ref, two_ref, sem)
    count = taps_ref.shape[0]

    def place(first, last):
        for t in range(in_ref.shape[0]):
            r, c = divmod(t, 4)
            embed_ref[r * 16 : (r + 1) * 16, c * LANE : (c + 1) * LANE] = first[t, 8].astype(F32)
        for t in range(rows_ref.shape[0] // 16):
            rows_ref[t * 16 : (t + 1) * 16, :] = last[t, 8].astype(F32)

    @pl.when(core == 0)
    def _():
        place(mine_ref, in_ref)

    @pl.when(core == 1)
    def _():
        place(in_ref, mine_ref)

    for cb in range(4):
        lanes = pl.ds(cb * LANE, LANE)
        for g in range(0, count - 1, 8):
            taps_ref[pl.ds(g, 8), lanes] = rows_ref[pl.ds(g * 4 + cb, 8, stride=4), :]
        taps_ref[pl.ds(count - 1, 1), lanes] = rows_ref[pl.ds((count - 1) * 4 + cb, 1), :]
        gain_ref[:, lanes] = rows_ref[pl.ds(count * 4 + cb, 1), :]
    base = len(puts)
    for k, pair in enumerate(((embed_ref, embed_far), (taps_ref, taps_far), (gain_ref, gain_far))):
        puts.append(pltpu.make_async_copy(*pair, sem.at[base + k]))
        puts[-1].start()
    for put in puts:
        put.wait()


def turned(spin, x, y, last):
    row = jnp.where(spin == 0, x, jnp.where(spin == 1, last - y, jnp.where(spin == 2, last - x, y)))
    col = jnp.where(spin == 0, y, jnp.where(spin == 1, x, jnp.where(spin == 2, last - y, last - x)))
    return row, col


def selectors(spin):
    p = jnp.arange(FULL * PITCH, dtype=jnp.int32)
    x, y = p // PITCH, p % PITCH
    row, col = turned(spin, x, y, FULL - 1)
    end = SIDE + HALO
    in_row, in_col = (row >= HALO) & (row < end), (col >= HALO) & (col < end)
    strip = jnp.where(
        (row < HALO) & in_col, row * SIDE + col - HALO,
        jnp.where((row >= end) & in_col, STRIP + (row - end) * SIDE + col - HALO,
        jnp.where((col < HALO) & in_row, 2 * STRIP + col * SIDE + row - HALO,
        jnp.where((col >= end) & in_row, 3 * STRIP + (col - end) * SIDE + row - HALO, -1))),
    )
    strip = jnp.where(y < FULL, strip, -1)
    own = (x >= HALO) & (x < end) & (y >= HALO) & (y < end)
    source = jnp.where(own, (x - HALO) * SIDE + y - HALO, jnp.where(strip >= 0, strip + CELLS, -1))
    place = (source[:, None] == jnp.arange(CELLS + 4 * STRIP, dtype=jnp.int32)[None]).astype(BF16)

    q = jnp.arange(CELLS, dtype=jnp.int32)
    row, col = turned(spin, q // SIDE, q % SIDE, SIDE - 1)
    cut = SIDE - HALO
    by_row = jnp.where(row >= cut, (row - cut) * SIDE + col, jnp.where(row < HALO, STRIP + row * SIDE + col, -1))
    by_col = jnp.where(col >= cut, 2 * STRIP + (col - cut) * SIDE + row, jnp.where(col < HALO, 3 * STRIP + col * SIDE + row, -1))
    k = jnp.arange(4 * STRIP, dtype=jnp.int32)
    pick = ((k[:, None] == by_row[None]) | (k[:, None] == by_col[None])).astype(BF16)
    return place, pick


def exchange(strips):
    moves = (("face", 1), ("face", -1), (("col", "core"), 1), (("col", "core"), -1))
    out = []
    for strip, (axis, way) in zip(strips, moves):
        size = lax.axis_size(axis)
        out.append(lax.ppermute(strip, axis, [(i, (i + way) % size) for i in range(size)]))
    return out


def swap(value):
    return lax.ppermute(value, "core", [(0, 1), (1, 0)])


def on_device(
    obs_values, obs_tile, interp, tile_spin, w_embed, dw_kernel, norm_gain, w_one, w_two, cotangent
):
    tiles, chips = lax.axis_size(ALL), lax.axis_size(CHIPS)
    width, channels = w_embed.shape
    hidden = w_one.shape[1]
    slots = interp.shape[2]
    core = lax.axis_index("core").reshape(1)
    place, pick = selectors(tile_spin[0, 0])
    gain = norm_gain[None]

    (leaving,) = call(
        route_kernel,
        [((tiles * 8, LANE), BF16)],
        [((1, obs_values.shape[0]), jnp.int32), (obs_values.shape, BF16)],
        16, obs_tile.reshape(1, -1), obs_values, far=(0, 1), copies=2,
    )
    arrived = lax.all_to_all(leaving.reshape(tiles, 8, LANE), ALL, 0, 0, tiled=True)
    weights, d_active = call(
        prepare_kernel, [((CELLS, tiles * slots), BF16), ((CELLS, hidden), F32)], [], 16,
        interp[0], cotangent, w_two,
    )

    gridded, embedded, *strips = call(
        embed_kernel,
        [((CELLS, width), BF16), ((CELLS, channels), BF16)] + [((STRIP, width), BF16)] * 4,
        [((tiles * 8, LANE), F32), ((tiles * slots, width), BF16)],
        12, arrived.reshape(tiles * 8, LANE), weights, w_embed, pick,
    )
    strips = exchange(strips)
    cells2 = ROWS2 * PITCH * 8
    flat = ((FULL * PITCH, channels), F32)
    kernel = ((TAPS * TAPS * 8, LANE), F32)
    step_sums = [((STEP, channels), F32), ((channels, STEP), F32)]
    half = hidden * channels // (16 * LANE)
    field, normal, inverse, scaled, active, d_hidden, taps, theirs = call(
        forward_kernel,
        [
            ((cells2, LANE), F32),
            ((CELLS, channels), F32),
            ((CELLS, LANE), F32),
            ((CELLS, channels), BF16),
            ((CELLS, hidden), BF16),
            ((CELLS, hidden), BF16),
            kernel,
            ((half, 16, LANE), BF16),
        ],
        [
            ((4 * STRIP, width), BF16),
            ((CELLS + 4 * STRIP, channels), BF16),
            flat,
            ((CELLS * 4, LANE), F32),
        ]
        + step_sums
        + [((CELLS, hidden), F32)],
        20,
        core, embedded, *strips, place, dw_kernel, gain, w_embed, w_one, d_active, cotangent,
        far=(11,), copies=1,
    )
    big = swap(theirs)

    mine, theirs = call(
        backward_kernel,
        [((chips, 16, LANE), F32), ((chips, 16, LANE), BF16)],
        [
            ((CELLS, channels), F32),
            ((CELLS * 4, LANE), F32),
            ((cells2, LANE), F32),
            flat,
            kernel,
            ((CELLS + 4 * STRIP, width), BF16),
            ((2 * chips * 16, LANE), F32),
        ],
        20,
        core, gridded, *strips, place, field, normal, inverse, d_hidden, w_one, gain, taps, cotangent,
    )
    small = swap(theirs)
    whole = ((chips, 9, 16, LANE), BF16)
    paired, output = call(
        pair_kernel, [whole, ((CELLS, channels), BF16)],
        step_sums + [((hidden, channels), BF16), ((CELLS, channels), BF16)], 20,
        core, scaled, active, d_hidden, cotangent, big, embedded, w_two, far=(7,), far_outs=(1,), copies=2,
    )
    (paired,) = call(
        join_kernel, [whole], [((chips, 16, LANE), BF16)], 4,
        mine, small, paired, far=(2,), far_outs=(0,), copies=1, aliases={2: 0},
    )
    paired = lax.all_to_all(paired, CHIPS, 0, 0, tiled=True)
    (summed,) = call(sum_kernel, [whole], [], 4, paired)
    here = lax.all_to_all(summed, CHIPS, 0, 0, tiled=True)
    there = swap(here)

    large = [((channels, hidden), F32), ((hidden, channels), F32)]
    steps = hidden // STEP // 2
    buffers = [((steps, channels, STEP), F32), ((steps, STEP, channels), F32)]
    grads = call(
        first_kernel, large, buffers, 12, core, here, far_outs=(0, 1), copies=2 * steps
    )
    count = TAPS * TAPS
    minor = [((width, channels), F32), ((count, channels), F32), ((1, channels), F32)]
    grad_one, grad_two, grad_embed, grad_kernel, grad_gain = call(
        second_kernel, large + minor,
        buffers + [((-(-(count + 1) * 4 // 16) * 16, LANE), F32)] + minor, 16,
        core, there, here, *grads,
        far=(3, 4), far_outs=range(5), copies=2 * steps + 3, aliases={3: 0, 4: 1},
    )
    return output, grad_embed, grad_kernel, grad_gain[0], grad_one, grad_two


def solution(mesh):
    faces, tiles = mesh.shape["face"], mesh.shape["tile"]
    fine = jax.sharding.Mesh(mesh.devices.reshape(faces, tiles // 2, 2), ALL)
    split = P(ALL, None)
    in_specs = (split, split, P(ALL, None, None, None), split) + (P(),) * 5 + (split,)
    return jax.shard_map(
        on_device, mesh=fine, in_specs=in_specs, out_specs=(split,) + (P(),) * 5, check_vma=False
    )
```

```python
import jax
import jax.numpy as jnp
from jax import lax
from jax.experimental import pallas as pl
from jax.experimental.pallas import tpu as pltpu
from jax.sharding import PartitionSpec as P

F32 = jnp.float32
BF16 = jnp.bfloat16
SIDE = 16
CELLS = SIDE * SIDE
HALO = 3
TAPS = 7
FULL = SIDE + 2 * HALO
PITCH = 24
HALF = SIDE // 2
LANE = 128
ROWS2 = HALF + TAPS - 1
STRIP = HALO * SIDE
SHELF = 65536
STEP = 256
ALL = ("face", "col", "core")
CHIPS = ("face", "col")
ROOT = 0.7978845608028654
CUBE = 0.044715

NN = (((1,), (0,)), ((), ()))
NT = (((1,), (1,)), ((), ()))
TN = (((0,), (0,)), ((), ()))


def dot(a, b, dims=NN):
    return lax.dot_general(a, b, dims, preferred_element_type=F32)


def call(kernel, outs, scratch, limit, *args, far=(), far_outs=(), copies=0, aliases=None):
    vmem, scalar = pl.BlockSpec(memory_space=pltpu.VMEM), pl.BlockSpec(memory_space=pltpu.SMEM)
    away = pl.BlockSpec(memory_space=pltpu.HBM)
    return pl.pallas_call(
        kernel,
        out_shape=[jax.ShapeDtypeStruct(s, d) for s, d in outs],
        in_specs=[
            scalar if a.shape == (1,) else away if k in far else vmem for k, a in enumerate(args)
        ],
        out_specs=[away if k in far_outs else vmem for k in range(len(outs))],
        scratch_shapes=[pltpu.VMEM(s, d) for s, d in scratch]
        + [pltpu.SemaphoreType.DMA((copies,))] * bool(copies),
        input_output_aliases=aliases or {},
        compiler_params=pltpu.CompilerParams(vmem_limit_bytes=int(limit * 2**20)),
    )(*args)


def start(sem, *pairs):
    moves = [pltpu.make_async_copy(a, b, sem.at[k]) for k, (a, b) in enumerate(pairs)]
    for move in moves:
        move.start()
    return moves


def block(i, j, pitch):
    return pl.ds(pl.multiple_of((i * pitch + j) * 8, 8), 8)


def comb(i, j, pitch, h, cb):
    return pl.ds((i * pitch + j) * 8 + h * 4 + cb, 8, stride=8)


def route_kernel(core_ref, row_far, obs_far, out_ref, row_ref, obs_ref, sem):
    fetch_row, fetch_obs = start(sem, (row_far, row_ref), (obs_far, obs_ref))
    fetch_row.wait()
    row = row_ref[...]
    count = row.shape[1]
    across = jnp.broadcast_to(row, (count, count)).astype(F32)
    earlier = lax.broadcasted_iota(jnp.int32, (count, count), 0) < lax.broadcasted_iota(
        jnp.int32, (count, count), 1
    )
    same = jnp.where((across.T == across) & earlier, 1.0, 0.0)
    rank = jnp.sum(same, axis=0, keepdims=True).astype(jnp.int32)
    place = row * 8 + rank
    lines = out_ref.shape[0]
    line = lax.broadcasted_iota(jnp.int32, (lines, count), 0)
    chosen = jnp.where((line - (line & 4)) == place, 1.0, 0.0).astype(BF16)
    fetch_obs.wait()
    moved = dot(chosen, obs_ref[...])
    first = (lax.broadcasted_iota(jnp.int32, (lines, LANE), 0) & 4) == 0
    out_ref[...] = jnp.where(first, moved[:, :LANE], moved[:, LANE:]).astype(BF16)


def shelf(width, slots, hidden, channels):
    rows = (CELLS, 4 * STRIP, width + 80, hidden)
    lanes = (slots, CELLS, channels, channels)
    ends = [sum(rows[: k + 1]) for k in range(len(rows))]
    return [(pl.ds(e - r, r), pl.ds(0, n)) for e, r, n in zip(ends, rows, lanes)]


def prepare_kernel(
    interp_ref, pick_ref, w_embed_ref, dw_ref, gain_ref, w_two_far, shelf_far,
    weights_ref, small_ref, near_ref, w_two_ref, sem,
):
    tiles, slots = interp_ref.shape[:2]
    width, channels = w_embed_ref.shape
    spots = shelf(width, tiles * slots, w_two_far.shape[0], channels)
    fetch = pltpu.make_async_copy(w_two_far, w_two_ref, sem.at[4])
    fetch.start()
    moves = [
        pltpu.make_async_copy(a, shelf_far.at[spot], sem.at[k])
        for k, (a, spot) in enumerate(zip((weights_ref, pick_ref, near_ref, w_two_ref), spots))
    ]
    moves[1].start()
    small_ref[...] = jnp.zeros_like(small_ref)
    small_ref[0 : TAPS * TAPS] = dw_ref[...].astype(F32)
    small_ref[64:] = jnp.broadcast_to(gain_ref[...].astype(F32), (16, channels))
    near_ref[0:width] = w_embed_ref[...]
    near_ref[width:] = small_ref[...].astype(BF16)
    moves[2].start()
    weights = interp_ref[...].astype(F32)
    for k in range(slots):
        weights_ref[:, k * tiles : (k + 1) * tiles] = weights[:, k, :].T.astype(BF16)
    moves[0].start()
    fetch.wait()
    moves[3].start()
    for move in moves:
        move.wait()


def embed_kernel(
    got_ref, shelf_far, grid_ref, emb_ref, near_ref, s0, s1, s2, s3, wide_ref, rows_ref, weights_ref, pick_ref, sem
):
    width, channels = near_ref.shape[0] - 80, near_ref.shape[1]
    spots = shelf(width, weights_ref.shape[1], 0, channels)
    targets = (weights_ref, pick_ref, near_ref)
    fetches = start(sem, *((shelf_far.at[spot], b) for spot, b in zip(spots, targets)))
    wide_ref[...] = got_ref[...].astype(F32)
    tiles = got_ref.shape[0] // 8
    for k in range(4):
        for half in range(2):
            for g in range(0, tiles, 16):
                two = [
                    wide_ref[pl.ds((g + e) * 8 + half * 4 + k, 8, stride=8), :] for e in (0, 8)
                ]
                rows_ref[pl.ds(k * tiles + g, 16), pl.ds(half * LANE, LANE)] = jnp.concatenate(
                    two, axis=0
                ).astype(BF16)
    for fetch in fetches:
        fetch.wait()
    gridded = dot(weights_ref[...], rows_ref[...]).astype(BF16)
    grid_ref[...] = gridded
    strips = dot(pick_ref[...], gridded).astype(BF16)
    for k, ref in enumerate((s0, s1, s2, s3)):
        ref[...] = strips[k * STRIP : (k + 1) * STRIP]
    emb_ref[...] = dot(gridded, near_ref[0:width]).astype(BF16)


def tiles_of(part, two, one):
    for k in range(64):
        r, c = divmod(k, 4)
        yield part * 128 + k, two, pl.ds(r * 16, 16), pl.ds(c * LANE, LANE)
    for k in range(64):
        r, c = divmod(k, 2)
        yield part * 128 + 64 + k, one, pl.ds(r * 16, 16), pl.ds(c * LANE, LANE)


def forward_kernel(
    core_ref, emb_ref, s0, s1, s2, s3, place_ref, near_ref, w_one_ref, shelf_far, cot_ref,
    field_ref, normal_ref, inv_ref, scaled_ref, active_ref, d_hid_ref, kern_ref, theirs_ref,
    strips_ref, cells_ref, flat_ref, conv_ref, two_ref, one_ref, w_two_ref, sem,
):
    width, channels = near_ref.shape[0] - 80, near_ref.shape[1]
    spot = shelf(width, 0, w_two_ref.shape[0], channels)[3]
    (fetch,) = start(sem, (shelf_far.at[spot], w_two_ref))
    taps = near_ref[width : width + 64].astype(F32)
    last = TAPS * TAPS - 1
    for h in range(2):
        for cb in range(4):
            lanes = slice(cb * LANE, (cb + 1) * LANE)
            for g in range(0, last, 8):
                kern_ref[pl.ds(g * 8 + h * 4 + cb, 8, stride=8), :] = taps[g : g + 8, lanes]
            kern_ref[pl.ds(last * 8 + h * 4 + cb, 1), :] = taps[last : last + 1, lanes]
    for k, ref in enumerate((s0, s1, s2, s3)):
        strips_ref[k * STRIP : (k + 1) * STRIP] = ref[...]
    cells_ref[0:CELLS] = emb_ref[...]
    cells_ref[CELLS:] = dot(strips_ref[...], near_ref[0:width]).astype(BF16)
    flat_ref[...] = dot(place_ref[...], cells_ref[...])
    for x in range(FULL):
        for g in range(3):
            for cb in range(4):
                value = flat_ref[pl.ds(x * PITCH + 8 * g, 8), pl.ds(cb * LANE, LANE)]
                if x < ROWS2:
                    field_ref[comb(x, 8 * g, PITCH, 0, cb), :] = value
                if x >= HALF:
                    field_ref[comb(x - HALF, 8 * g, PITCH, 1, cb), :] = value

    def conv_row(i, carry):
        sums = [jnp.zeros((8, LANE), F32)] * SIDE
        for a in range(TAPS):
            taps = [kern_ref[pl.ds((a * TAPS + b) * 8, 8), :] for b in range(TAPS)]
            for y in range(FULL):
                here = field_ref[block(i + a, y, PITCH), :]
                for b in range(TAPS):
                    if 0 <= y - b < SIDE:
                        sums[y - b] = sums[y - b] + here * taps[b]
        for j in range(SIDE):
            conv_ref[block(i, j, SIDE), :] = sums[j]
        return carry

    lax.fori_loop(0, HALF, conv_row, 0)

    gain = near_ref[width + 64 :].astype(F32)
    for r in range(SIDE):
        h, i = divmod(r, HALF)
        parts = [
            jnp.concatenate([conv_ref[comb(i, 8 * g, SIDE, h, cb), :] for g in range(2)], axis=0)
            for cb in range(4)
        ]
        value = jnp.concatenate(parts, axis=1)
        centred = value - jnp.mean(value, axis=1, keepdims=True)
        inverse = lax.rsqrt(jnp.mean(centred * centred, axis=1, keepdims=True) + 1e-06)
        normal = centred * inverse
        rows = pl.ds(r * SIDE, SIDE)
        normal_ref[rows, :] = normal
        inv_ref[rows, :] = jnp.broadcast_to(inverse, (SIDE, LANE))
        scaled_ref[rows, :] = (normal * gain).astype(BF16)

    fetch.wait()
    for k in range(w_one_ref.shape[1] // STEP):
        some = pl.ds(k * STEP, STEP)
        pre = dot(scaled_ref[...], w_one_ref[:, some])
        square = pre * pre
        tanh = jnp.tanh(pre * (ROOT + (ROOT * CUBE) * square))
        upper = 0.5 + 0.5 * tanh
        slope = upper + (0.5 * pre) * (1.0 - tanh * tanh) * (ROOT + (3.0 * ROOT * CUBE) * square)
        active_ref[:, some] = (pre * upper).astype(BF16)
        d_act = dot(cot_ref[...], w_two_ref[some, :], NT)
        d_hid_ref[:, some] = (d_act * slope).astype(BF16)

    steps = theirs_ref.shape[0] // 128
    for k in range(steps):
        some = pl.ds(pl.multiple_of(((1 - core_ref[0]) * steps + k) * STEP, STEP), STEP)
        two_ref[...] = dot(active_ref[:, some], cot_ref[...], TN)
        one_ref[...] = dot(scaled_ref[...], d_hid_ref[:, some], TN)
        for t, ref, rows, lanes in tiles_of(k, two_ref, one_ref):
            theirs_ref[t] = ref[rows, lanes].astype(BF16)


def backward_kernel(
    core_ref, grid_ref, s0, s1, s2, s3, place_ref, field_ref, normal_ref, inv_ref, d_hid_ref, w_one_ref,
    near_ref, kern_ref, cot_ref,
    mine_ref, theirs_ref,
    d_scaled_ref, d_conv_ref, spread_ref, flat_ref, taps_ref, cells_ref, small_ref,
):
    d_scaled_ref[...] = dot(d_hid_ref[...], w_one_ref[...], NT)
    total = jnp.zeros((SIDE, normal_ref.shape[1]), F32)
    gain = near_ref[near_ref.shape[0] - 16 :].astype(F32)
    for r in range(SIDE):
        h, i = divmod(r, HALF)
        rows = pl.ds(r * SIDE, SIDE)
        normal, d_scaled = normal_ref[rows, :], d_scaled_ref[rows, :]
        total = total + d_scaled * normal
        d_normal = d_scaled * gain
        mean = jnp.mean(d_normal, axis=1, keepdims=True)
        along = jnp.mean(d_normal * normal, axis=1, keepdims=True)
        d_conv = (d_normal - mean - normal * along) * inv_ref[rows, 0:1]
        for g in range(2):
            for cb in range(4):
                d_conv_ref[comb(i, 8 * g, SIDE, h, cb), :] = d_conv[
                    8 * g : 8 * g + 8, cb * LANE : (cb + 1) * LANE
                ]
    grad_gain = jnp.sum(total, axis=0, keepdims=True)

    spread_ref[...] = jnp.zeros_like(spread_ref)
    taps_ref[...] = jnp.zeros_like(taps_ref)

    def conv_row(i, carry):
        for a in range(TAPS):
            taps = [kern_ref[pl.ds((a * TAPS + b) * 8, 8), :] for b in range(TAPS)]
            for y in range(FULL):
                value = spread_ref[block(i + a, y, PITCH), :]
                for b in range(TAPS):
                    if 0 <= y - b < SIDE:
                        value = value + d_conv_ref[block(i, y - b, SIDE), :] * taps[b]
                spread_ref[block(i + a, y, PITCH), :] = value
        return carry

    lax.fori_loop(0, HALF, conv_row, 0)

    def tap_row(i, carry):
        for a in range(TAPS):
            sums = [taps_ref[pl.ds((a * TAPS + b) * 8, 8), :] for b in range(TAPS)]
            for y in range(FULL):
                here = field_ref[block(i + a, y, PITCH), :]
                for b in range(TAPS):
                    if 0 <= y - b < SIDE:
                        sums[b] = sums[b] + here * d_conv_ref[block(i, y - b, SIDE), :]
            for b in range(TAPS):
                taps_ref[pl.ds((a * TAPS + b) * 8, 8), :] = sums[b]
        return carry

    lax.fori_loop(0, HALF, tap_row, 0)

    for x in range(FULL):
        for g in range(3):
            for cb in range(4):
                value = None
                if x < ROWS2:
                    value = spread_ref[comb(x, 8 * g, PITCH, 0, cb), :]
                if x >= HALF:
                    more = spread_ref[comb(x - HALF, 8 * g, PITCH, 1, cb), :]
                    value = more if value is None else value + more
                flat_ref[pl.ds(x * PITCH + 8 * g, 8), pl.ds(cb * LANE, LANE)] = value

    cells_ref[0:CELLS] = grid_ref[...]
    for k, ref in enumerate((s0, s1, s2, s3)):
        cells_ref[CELLS + k * STRIP : CELLS + (k + 1) * STRIP] = ref[...]
    spots = dot(place_ref[...], cells_ref[...]).astype(BF16)
    grad_embed = dot(spots, flat_ref[...].astype(BF16), TN) + dot(grid_ref[...], cot_ref[...], TN)

    half = mine_ref.shape[0]
    small_ref[...] = jnp.zeros_like(small_ref)
    for t in range(half):
        r, c = divmod(t, 4)
        small_ref[t * 16 : (t + 1) * 16] = grad_embed[r * 16 : (r + 1) * 16, c * LANE : (c + 1) * LANE]
    base = half * 16
    for t in range(TAPS * TAPS):
        both = taps_ref[t * 8 : (t + 1) * 8, :]
        small_ref[base + t * 4 : base + (t + 1) * 4] = both[:4] + both[4:]
    for c in range(4):
        at = base + TAPS * TAPS * 4 + c
        small_ref[at : at + 1] = grad_gain[:, c * LANE : (c + 1) * LANE]
    core = core_ref[0]
    for t in range(half):
        mine_ref[t] = small_ref[pl.ds(pl.multiple_of((core * half + t) * 16, 16), 16), :]
        theirs_ref[t] = small_ref[
            pl.ds(pl.multiple_of(((1 - core) * half + t) * 16, 16), 16), :
        ].astype(BF16)


def pair_kernel(core_ref, scaled_ref, active_ref, d_hid_ref, cot_ref, big_ref, out_ref, two_ref, one_ref):
    steps = big_ref.shape[0] // 128
    for k in range(steps):
        some = pl.ds(pl.multiple_of((core_ref[0] * steps + k) * STEP, STEP), STEP)
        two_ref[...] = dot(active_ref[:, some], cot_ref[...], TN)
        one_ref[...] = dot(scaled_ref[...], d_hid_ref[:, some], TN)
        for t, ref, rows, lanes in tiles_of(k, two_ref, one_ref):
            out_ref[t // 8, t % 8] = (ref[rows, lanes] + big_ref[t].astype(F32)).astype(BF16)


def join_kernel(mine_ref, small_ref, paired_far, out_far, tile_ref, sem):
    tile_ref[...] = (mine_ref[...] + small_ref[...].astype(F32)).astype(BF16)
    put = pltpu.make_async_copy(tile_ref, out_far.at[:, 8], sem.at[0])
    put.start()
    put.wait()


def sum_kernel(in_ref, out_ref):
    parts, tiles = in_ref.shape[:2]

    def add(d, sums):
        return [s + in_ref[d, t].astype(F32) for t, s in enumerate(sums)]

    sums = lax.fori_loop(0, parts, add, [jnp.zeros(in_ref.shape[2:], F32)] * tiles)
    sums = [s.astype(BF16) for s in sums]

    def spread(d, carry):
        for t in range(tiles):
            out_ref[d, t] = sums[t]
        return carry

    lax.fori_loop(0, parts, spread, 0)


def assemble_half(core, in_ref, one_far, two_far, one_ref, two_ref, sem):
    steps = one_ref.shape[0]
    puts = []
    for k in range(steps):
        for t, ref, rows, lanes in tiles_of(k, two_ref, one_ref):
            ref[k, rows, lanes] = in_ref[t // 8, t % 8].astype(F32)
        some = pl.ds(pl.multiple_of((core * steps + k) * STEP, STEP), STEP)
        puts += [
            pltpu.make_async_copy(one_ref.at[k], one_far.at[:, some], sem.at[2 * k]),
            pltpu.make_async_copy(two_ref.at[k], two_far.at[some, :], sem.at[2 * k + 1]),
        ]
        puts[-2].start()
        puts[-1].start()
    return puts


def first_kernel(
    core_ref, in_ref, emb_ref, active_ref, w_two_ref,
    one_far, two_far, feature_far, one_ref, two_ref, feature_ref, sem,
):
    puts = assemble_half(core_ref[0], in_ref, one_far, two_far, one_ref, two_ref, sem)
    feature_ref[...] = (emb_ref[...].astype(F32) + dot(active_ref[...], w_two_ref[...])).astype(BF16)
    puts.append(pltpu.make_async_copy(feature_ref, feature_far, sem.at[len(puts)]))
    puts[-1].start()
    for put in puts:
        put.wait()


def second_kernel(
    core_ref, in_ref, mine_ref, one_old, two_old,
    one_far, two_far, embed_far, taps_far, gain_far,
    one_ref, two_ref, rows_ref, embed_ref, taps_ref, gain_ref, sem,
):
    core = core_ref[0]
    puts = assemble_half(1 - core, in_ref, one_far, two_far, one_ref, two_ref, sem)
    count = taps_ref.shape[0]

    def place(first, last):
        for t in range(in_ref.shape[0]):
            r, c = divmod(t, 4)
            embed_ref[r * 16 : (r + 1) * 16, c * LANE : (c + 1) * LANE] = first[t, 8].astype(F32)
        for t in range(rows_ref.shape[0] // 16):
            rows_ref[t * 16 : (t + 1) * 16, :] = last[t, 8].astype(F32)

    @pl.when(core == 0)
    def _():
        place(mine_ref, in_ref)

    @pl.when(core == 1)
    def _():
        place(in_ref, mine_ref)

    for cb in range(4):
        lanes = pl.ds(cb * LANE, LANE)
        for g in range(0, count - 1, 8):
            taps_ref[pl.ds(g, 8), lanes] = rows_ref[pl.ds(g * 4 + cb, 8, stride=4), :]
        taps_ref[pl.ds(count - 1, 1), lanes] = rows_ref[pl.ds((count - 1) * 4 + cb, 1), :]
        gain_ref[:, lanes] = rows_ref[pl.ds(count * 4 + cb, 1), :]
    base = len(puts)
    for k, pair in enumerate(((embed_ref, embed_far), (taps_ref, taps_far), (gain_ref, gain_far))):
        puts.append(pltpu.make_async_copy(*pair, sem.at[base + k]))
        puts[-1].start()
    for put in puts:
        put.wait()


def turned(spin, x, y, last):
    row = jnp.where(spin == 0, x, jnp.where(spin == 1, last - y, jnp.where(spin == 2, last - x, y)))
    col = jnp.where(spin == 0, y, jnp.where(spin == 1, x, jnp.where(spin == 2, last - y, last - x)))
    return row, col


def selectors(spin):
    p = jnp.arange(FULL * PITCH, dtype=jnp.int32)
    x, y = p // PITCH, p % PITCH
    row, col = turned(spin, x, y, FULL - 1)
    end = SIDE + HALO
    in_row, in_col = (row >= HALO) & (row < end), (col >= HALO) & (col < end)
    strip = jnp.where(
        (row < HALO) & in_col, row * SIDE + col - HALO,
        jnp.where((row >= end) & in_col, STRIP + (row - end) * SIDE + col - HALO,
        jnp.where((col < HALO) & in_row, 2 * STRIP + col * SIDE + row - HALO,
        jnp.where((col >= end) & in_row, 3 * STRIP + (col - end) * SIDE + row - HALO, -1))),
    )
    strip = jnp.where(y < FULL, strip, -1)
    own = (x >= HALO) & (x < end) & (y >= HALO) & (y < end)
    source = jnp.where(own, (x - HALO) * SIDE + y - HALO, jnp.where(strip >= 0, strip + CELLS, -1))
    place = (source[:, None] == jnp.arange(CELLS + 4 * STRIP, dtype=jnp.int32)[None]).astype(BF16)

    q = jnp.arange(CELLS, dtype=jnp.int32)
    row, col = turned(spin, q // SIDE, q % SIDE, SIDE - 1)
    cut = SIDE - HALO
    by_row = jnp.where(row >= cut, (row - cut) * SIDE + col, jnp.where(row < HALO, STRIP + row * SIDE + col, -1))
    by_col = jnp.where(col >= cut, 2 * STRIP + (col - cut) * SIDE + row, jnp.where(col < HALO, 3 * STRIP + col * SIDE + row, -1))
    k = jnp.arange(4 * STRIP, dtype=jnp.int32)
    pick = ((k[:, None] == by_row[None]) | (k[:, None] == by_col[None])).astype(BF16)
    return place, pick


def exchange(strips):
    moves = (("face", 1), ("face", -1), (("col", "core"), 1), (("col", "core"), -1))
    out = []
    for strip, (axis, way) in zip(strips, moves):
        size = lax.axis_size(axis)
        out.append(lax.ppermute(strip, axis, [(i, (i + way) % size) for i in range(size)]))
    return out


def swap(value):
    return lax.ppermute(value, "core", [(0, 1), (1, 0)])


def on_device(
    obs_values, obs_tile, interp, tile_spin, w_embed, dw_kernel, norm_gain, w_one, w_two, cotangent
):
    tiles, chips = lax.axis_size(ALL), lax.axis_size(CHIPS)
    width, channels = w_embed.shape
    hidden = w_one.shape[1]
    slots = interp.shape[2]
    core = lax.axis_index("core").reshape(1)
    place, pick = selectors(tile_spin[0, 0])
    (leaving,) = call(
        route_kernel,
        [((tiles * 8, LANE), BF16)],
        [((1, obs_values.shape[0]), jnp.int32), (obs_values.shape, BF16)],
        60.5, core, obs_tile.reshape(1, -1), obs_values, far=(1, 2), copies=2,
    )
    arrived = lax.all_to_all(leaving.reshape(tiles, 8, LANE), ALL, 0, 0, tiled=True)
    stacked = ((CELLS, tiles * slots), BF16)
    near = ((width + 80, channels), BF16)
    (shelved,) = call(
        prepare_kernel, [((SHELF, channels), BF16)], [stacked, ((80, channels), F32), near, (w_two.shape, BF16)],
        60.5, interp[0], pick, w_embed, dw_kernel, norm_gain[None], w_two, far=(5,), far_outs=(0,), copies=5,
    )
    gridded, embedded, nearby, *strips = call(
        embed_kernel,
        [((CELLS, width), BF16), ((CELLS, channels), BF16), near] + [((STRIP, width), BF16)] * 4,
        [((tiles * 8, LANE), F32), ((tiles * slots, width), BF16), stacked, (pick.shape, BF16)],
        16, arrived.reshape(tiles * 8, LANE), shelved, far=(1,), copies=3,
    )
    strips = exchange(strips)
    cells2 = ROWS2 * PITCH * 8
    flat = ((FULL * PITCH, channels), F32)
    kernel = ((TAPS * TAPS * 8, LANE), F32)
    step_sums = [((STEP, channels), F32), ((channels, STEP), F32)]
    half = hidden * channels // (16 * LANE)
    field, normal, inverse, scaled, active, d_hidden, taps, theirs = call(
        forward_kernel,
        [
            ((cells2, LANE), F32),
            ((CELLS, channels), F32),
            ((CELLS, LANE), F32),
            ((CELLS, channels), BF16),
            ((CELLS, hidden), BF16),
            ((CELLS, hidden), BF16),
            kernel,
            ((half, 16, LANE), BF16),
        ],
        [
            ((4 * STRIP, width), BF16),
            ((CELLS + 4 * STRIP, channels), BF16),
            flat,
            ((CELLS * 4, LANE), F32),
        ]
        + step_sums
        + [((hidden, channels), BF16)],
        20,
        core, embedded, *strips, place, nearby, w_one, shelved, cotangent, far=(9,), copies=1,
    )
    big = swap(theirs)

    mine, theirs = call(
        backward_kernel,
        [((chips, 16, LANE), F32), ((chips, 16, LANE), BF16)],
        [
            ((CELLS, channels), F32),
            ((CELLS * 4, LANE), F32),
            ((cells2, LANE), F32),
            flat,
            kernel,
            ((CELLS + 4 * STRIP, width), BF16),
            ((2 * chips * 16, LANE), F32),
        ],
        20,
        core, gridded, *strips, place, field, normal, inverse, d_hidden, w_one, nearby, taps, cotangent,
    )
    small = swap(theirs)
    whole = ((chips, 9, 16, LANE), BF16)
    (paired,) = call(
        pair_kernel, [whole], step_sums, 20, core, scaled, active, d_hidden, cotangent, big
    )
    (paired,) = call(
        join_kernel, [whole], [((chips, 16, LANE), BF16)], 4,
        mine, small, paired, far=(2,), far_outs=(0,), copies=1, aliases={2: 0},
    )
    paired = lax.all_to_all(paired, CHIPS, 0, 0, tiled=True)
    (summed,) = call(sum_kernel, [whole], [], 4, paired)
    here = lax.all_to_all(summed, CHIPS, 0, 0, tiled=True)
    there = swap(here)

    large = [((channels, hidden), F32), ((hidden, channels), F32)]
    steps = hidden // STEP // 2
    buffers = [((steps, channels, STEP), F32), ((steps, STEP, channels), F32)]
    *grads, output = call(
        first_kernel, large + [((CELLS, channels), BF16)], buffers + [((CELLS, channels), BF16)], 16,
        core, here, embedded, active, w_two, far_outs=(0, 1, 2), copies=2 * steps + 1,
    )
    count = TAPS * TAPS
    minor = [((width, channels), F32), ((count, channels), F32), ((1, channels), F32)]
    grad_one, grad_two, grad_embed, grad_kernel, grad_gain = call(
        second_kernel, large + minor,
        buffers + [((-(-(count + 1) * 4 // 16) * 16, LANE), F32)] + minor, 16,
        core, there, here, *grads,
        far=(3, 4), far_outs=range(5), copies=2 * steps + 3, aliases={3: 0, 4: 1},
    )
    return output, grad_embed, grad_kernel, grad_gain[0], grad_one, grad_two


def solution(mesh):
    faces, tiles = mesh.shape["face"], mesh.shape["tile"]
    fine = jax.sharding.Mesh(mesh.devices.reshape(faces, tiles // 2, 2), ALL)
    split = P(ALL, None)
    in_specs = (split, split, P(ALL, None, None, None), split) + (P(),) * 5 + (split,)
    return jax.shard_map(
        on_device, mesh=fine, in_specs=in_specs, out_specs=(split,) + (P(),) * 5, check_vma=False
    )
```

```python
import jax
import jax.numpy as jnp
from jax import lax
from jax.experimental import pallas as pl
from jax.experimental.pallas import tpu as pltpu
from jax.sharding import PartitionSpec as P

F32 = jnp.float32
BF16 = jnp.bfloat16
SIDE = 16
CELLS = SIDE * SIDE
HALO = 3
TAPS = 7
FULL = SIDE + 2 * HALO
PITCH = 24
HALF = SIDE // 2
LANE = 128
ROWS2 = HALF + TAPS - 1
STRIP = HALO * SIDE
SHELF = 65536
STEP = 256
ALL = ("face", "col", "core")
CHIPS = ("face", "col")
ROOT = 0.7978845608028654
CUBE = 0.044715

NN = (((1,), (0,)), ((), ()))
NT = (((1,), (1,)), ((), ()))
TN = (((0,), (0,)), ((), ()))


def dot(a, b, dims=NN):
    return lax.dot_general(a, b, dims, preferred_element_type=F32)


def call(kernel, outs, scratch, limit, *args, far=(), far_outs=(), copies=0, aliases=None):
    vmem, scalar = pl.BlockSpec(memory_space=pltpu.VMEM), pl.BlockSpec(memory_space=pltpu.SMEM)
    away = pl.BlockSpec(memory_space=pltpu.HBM)
    return pl.pallas_call(
        kernel,
        out_shape=[jax.ShapeDtypeStruct(s, d) for s, d in outs],
        in_specs=[
            scalar if a.shape == (1,) else away if k in far else vmem for k, a in enumerate(args)
        ],
        out_specs=[away if k in far_outs else vmem for k in range(len(outs))],
        scratch_shapes=[pltpu.VMEM(s, d) for s, d in scratch]
        + [pltpu.SemaphoreType.DMA((copies,))] * bool(copies),
        input_output_aliases=aliases or {},
        compiler_params=pltpu.CompilerParams(vmem_limit_bytes=int(limit * 2**20)),
    )(*args)


def start(sem, *pairs):
    moves = [pltpu.make_async_copy(a, b, sem.at[k]) for k, (a, b) in enumerate(pairs)]
    for move in moves:
        move.start()
    return moves


def strip_at(k):
    return pl.ds(pl.multiple_of(k * STRIP, 16), STRIP)


def take_strips(core, refs, strips_ref):
    for ref, k in zip(refs, (0, 1, 2 + core, 3 - core)):
        strips_ref[strip_at(k), :] = ref[...]


def block(i, j, pitch):
    return pl.ds(pl.multiple_of((i * pitch + j) * 8, 8), 8)


def comb(i, j, pitch, h, cb):
    return pl.ds((i * pitch + j) * 8 + h * 4 + cb, 8, stride=8)


def route_kernel(core_ref, row_far, obs_far, out_ref, row_ref, obs_ref, sem):
    fetch_row, fetch_obs = start(sem, (row_far, row_ref), (obs_far, obs_ref))
    fetch_row.wait()
    row = row_ref[...]
    count = row.shape[1]
    across = jnp.broadcast_to(row, (count, count)).astype(F32)
    earlier = lax.broadcasted_iota(jnp.int32, (count, count), 0) < lax.broadcasted_iota(
        jnp.int32, (count, count), 1
    )
    same = jnp.where((across.T == across) & earlier, 1.0, 0.0)
    rank = jnp.sum(same, axis=0, keepdims=True).astype(jnp.int32)
    place = row * 8 + rank
    lines = out_ref.shape[0]
    line = lax.broadcasted_iota(jnp.int32, (lines, count), 0)
    chosen = jnp.where((line - (line & 4)) == place, 1.0, 0.0).astype(BF16)
    fetch_obs.wait()
    moved = dot(chosen, obs_ref[...])
    first = (lax.broadcasted_iota(jnp.int32, (lines, LANE), 0) & 4) == 0
    out_ref[...] = jnp.where(first, moved[:, :LANE], moved[:, LANE:]).astype(BF16)


def shelf(width, slots, hidden, channels):
    rows = (CELLS, 4 * STRIP, width + 80, hidden)
    lanes = (slots, CELLS, channels, channels)
    ends = [sum(rows[: k + 1]) for k in range(len(rows))]
    return [(pl.ds(e - r, r), pl.ds(0, n)) for e, r, n in zip(ends, rows, lanes)]


def prepare_kernel(
    interp_ref, pick_ref, w_embed_ref, dw_ref, gain_ref, w_two_far, shelf_far,
    weights_ref, small_ref, near_ref, w_two_ref, sem,
):
    tiles, slots = interp_ref.shape[:2]
    width, channels = w_embed_ref.shape
    spots = shelf(width, tiles * slots, w_two_far.shape[0], channels)
    fetch = pltpu.make_async_copy(w_two_far, w_two_ref, sem.at[4])
    fetch.start()
    moves = [
        pltpu.make_async_copy(a, shelf_far.at[spot], sem.at[k])
        for k, (a, spot) in enumerate(zip((weights_ref, pick_ref, near_ref, w_two_ref), spots))
    ]
    moves[1].start()
    small_ref[...] = jnp.zeros_like(small_ref)
    small_ref[0 : TAPS * TAPS] = dw_ref[...].astype(F32)
    small_ref[64:] = jnp.broadcast_to(gain_ref[...].astype(F32), (16, channels))
    near_ref[0:width] = w_embed_ref[...]
    near_ref[width:] = small_ref[...].astype(BF16)
    moves[2].start()
    weights = interp_ref[...].astype(F32)
    for k in range(slots):
        weights_ref[:, k * tiles : (k + 1) * tiles] = weights[:, k, :].T.astype(BF16)
    moves[0].start()
    fetch.wait()
    moves[3].start()
    for move in moves:
        move.wait()


def embed_kernel(
    core_ref, got_ref, shelf_far, grid_ref, emb_ref, near_ref, up_ref, down_ref, far_ref, by_ref,
    wide_ref, rows_ref, weights_ref, pick_ref, strips_ref, sem,
):
    width, channels = near_ref.shape[0] - 80, near_ref.shape[1]
    spots = shelf(width, weights_ref.shape[1], 0, channels)
    targets = (weights_ref, pick_ref, near_ref)
    fetches = start(sem, *((shelf_far.at[spot], b) for spot, b in zip(spots, targets)))
    wide_ref[...] = got_ref[...].astype(F32)
    tiles = got_ref.shape[0] // 8
    for k in range(4):
        for half in range(2):
            for g in range(0, tiles, 16):
                two = [
                    wide_ref[pl.ds((g + e) * 8 + half * 4 + k, 8, stride=8), :] for e in (0, 8)
                ]
                rows_ref[pl.ds(k * tiles + g, 16), pl.ds(half * LANE, LANE)] = jnp.concatenate(
                    two, axis=0
                ).astype(BF16)
    for fetch in fetches:
        fetch.wait()
    gridded = dot(weights_ref[...], rows_ref[...]).astype(BF16)
    grid_ref[...] = gridded
    strips_ref[...] = dot(pick_ref[...], gridded).astype(BF16)
    core = core_ref[0]
    for ref, k in ((up_ref, 0), (down_ref, 1), (far_ref, 3 - core), (by_ref, 2 + core)):
        ref[...] = strips_ref[strip_at(k), :]
    emb_ref[...] = dot(gridded, near_ref[0:width]).astype(BF16)


def tiles_of(part, two, one):
    for k in range(64):
        r, c = divmod(k, 4)
        yield part * 128 + k, two, pl.ds(r * 16, 16), pl.ds(c * LANE, LANE)
    for k in range(64):
        r, c = divmod(k, 2)
        yield part * 128 + 64 + k, one, pl.ds(r * 16, 16), pl.ds(c * LANE, LANE)


def inner_kernel(
    emb_ref, near_ref, shelf_far, cot_ref, field_ref, conv_ref, kern_ref, d_act_ref, w_two_ref, sem
):
    width, channels = near_ref.shape[0] - 80, near_ref.shape[1]
    spot = shelf(width, 0, w_two_ref.shape[0], channels)[3]
    (fetch,) = start(sem, (shelf_far.at[spot], w_two_ref))
    taps = near_ref[width : width + 64].astype(F32)
    last = TAPS * TAPS - 1
    for h in range(2):
        for cb in range(4):
            lanes = slice(cb * LANE, (cb + 1) * LANE)
            for g in range(0, last, 8):
                kern_ref[pl.ds(g * 8 + h * 4 + cb, 8, stride=8), :] = taps[g : g + 8, lanes]
            kern_ref[pl.ds(last * 8 + h * 4 + cb, 1), :] = taps[last : last + 1, lanes]
    for i in range(SIDE):
        own = emb_ref[pl.ds(i * SIDE, SIDE), :].astype(F32)
        x = i + HALO
        for g in range(0, SIDE, 8):
            for cb in range(4):
                value = own[g : g + 8, cb * LANE : (cb + 1) * LANE]
                if x < ROWS2:
                    field_ref[comb(x, HALO + g, PITCH, 0, cb), :] = value
                if x >= HALF:
                    field_ref[comb(x - HALF, HALO + g, PITCH, 1, cb), :] = value
    fetch.wait()
    step = d_act_ref.shape[1] // HALF
    for i in range(HALF):
        some = pl.ds(i * step, step)
        d_act_ref[:, some] = dot(cot_ref[...], w_two_ref[some, :], NT)
        sums = [jnp.zeros((8, LANE), F32)] * SIDE
        for x in range(max(i, HALO), min(i + TAPS, HALF + HALO)):
            taps = [kern_ref[block(x - i, b, TAPS), :] for b in range(TAPS)]
            for y in range(HALO, SIDE + HALO):
                here = field_ref[block(x, y, PITCH), :]
                for b in range(TAPS):
                    if 0 <= y - b < SIDE:
                        sums[y - b] = sums[y - b] + here * taps[b]
        for j in range(SIDE):
            conv_ref[block(i, j, SIDE), :] = sums[j]


OUTER = (0, 1, 2, 19, 20, 21)


def ring():
    at = 0
    for x in OUTER:
        for y in range(0, PITCH, 8):
            yield at, x, y
            at += 8
    for x in range(HALO, SIDE + HALO):
        for y in (0, PITCH - 8):
            yield at, x, y
            at += 8


RING = 8 * len(list(ring()))


def forward_kernel(
    core_ref, s0, s1, s2, s3, place_ref, near_ref, w_one_ref, own_ref, part_ref, kern_ref, d_act_ref, cot_ref,
    field_ref, normal_ref, inv_ref, scaled_ref, active_ref, d_hid_ref, theirs_ref,
    strips_ref, ring_ref, conv_ref,
):
    width, channels = near_ref.shape[0] - 80, near_ref.shape[1]
    take_strips(core_ref[0], (s0, s1, s2, s3), strips_ref)
    halo = dot(strips_ref[...], near_ref[0:width]).astype(BF16)
    ring_ref[...] = dot(place_ref[...], halo)
    field_ref[...] = own_ref[...]
    for at, x, y in ring():
        skip, count = (0, 8) if x in OUTER else (0, HALO) if y == 0 else (HALO, HALO)
        for cb in range(4):
            value = ring_ref[pl.ds(at + skip, count), pl.ds(cb * LANE, LANE)]
            if x < ROWS2:
                field_ref[pl.ds((x * PITCH + y + skip) * 8 + cb, count, stride=8), :] = value
            if x >= HALF:
                row = ((x - HALF) * PITCH + y + skip) * 8 + 4 + cb
                field_ref[pl.ds(row, count, stride=8), :] = value

    for i in range(HALF):
        sums = [part_ref[block(i, j, SIDE), :] for j in range(SIDE)]
        for a in range(TAPS):
            x = i + a
            whole = x < HALO or x >= HALF + HALO
            taps = [kern_ref[block(a, b, TAPS), :] for b in range(TAPS)]
            for y in range(FULL):
                if whole or y < HALO or y >= SIDE + HALO:
                    here = field_ref[block(x, y, PITCH), :]
                    for b in range(TAPS):
                        if 0 <= y - b < SIDE:
                            sums[y - b] = sums[y - b] + here * taps[b]
        for j in range(SIDE):
            conv_ref[block(i, j, SIDE), :] = sums[j]

    gain = near_ref[width + 64 :].astype(F32)
    for r in range(SIDE):
        h, i = divmod(r, HALF)
        parts = [
            jnp.concatenate([conv_ref[comb(i, 8 * g, SIDE, h, cb), :] for g in range(2)], axis=0)
            for cb in range(4)
        ]
        value = jnp.concatenate(parts, axis=1)
        centred = value - jnp.mean(value, axis=1, keepdims=True)
        inverse = lax.rsqrt(jnp.mean(centred * centred, axis=1, keepdims=True) + 1e-06)
        normal = centred * inverse
        rows = pl.ds(r * SIDE, SIDE)
        normal_ref[rows, :] = normal
        inv_ref[rows, :] = jnp.broadcast_to(inverse, (SIDE, LANE))
        scaled_ref[rows, :] = (normal * gain).astype(BF16)

    for k in range(w_one_ref.shape[1] // STEP):
        some = pl.ds(k * STEP, STEP)
        pre = dot(scaled_ref[...], w_one_ref[:, some])
        square = pre * pre
        tanh = jnp.tanh(pre * (ROOT + (ROOT * CUBE) * square))
        upper = 0.5 + 0.5 * tanh
        slope = upper + (0.5 * pre) * (1.0 - tanh * tanh) * (ROOT + (3.0 * ROOT * CUBE) * square)
        active_ref[:, some] = (pre * upper).astype(BF16)
        d_hid_ref[:, some] = (d_act_ref[:, some] * slope).astype(BF16)

    half = w_one_ref.shape[1] // 2
    away = pl.ds(pl.multiple_of((1 - core_ref[0]) * half, half), half)
    theirs_ref[:, 0:half] = active_ref[:, away]
    theirs_ref[:, half : 2 * half] = d_hid_ref[:, away]
    theirs_ref[:, 2 * half : 2 * half + channels] = scaled_ref[...]
    theirs_ref[:, 2 * half + channels :] = cot_ref[...]


def backward_kernel(
    core_ref, grid_ref, s0, s1, s2, s3, place_ref, field_ref, normal_ref, inv_ref, d_hid_ref, w_one_ref,
    near_ref, kern_ref, cot_ref,
    mine_ref, theirs_ref,
    d_scaled_ref, d_conv_ref, spread_ref, own_ref, ring_ref, taps_ref, strips_ref, small_ref,
):
    d_scaled_ref[...] = dot(d_hid_ref[...], w_one_ref[...], NT)
    total = jnp.zeros((SIDE, normal_ref.shape[1]), F32)
    gain = near_ref[near_ref.shape[0] - 16 :].astype(F32)
    for r in range(SIDE):
        h, i = divmod(r, HALF)
        rows = pl.ds(r * SIDE, SIDE)
        normal, d_scaled = normal_ref[rows, :], d_scaled_ref[rows, :]
        total = total + d_scaled * normal
        d_normal = d_scaled * gain
        mean = jnp.mean(d_normal, axis=1, keepdims=True)
        along = jnp.mean(d_normal * normal, axis=1, keepdims=True)
        d_conv = (d_normal - mean - normal * along) * inv_ref[rows, 0:1]
        for g in range(2):
            for cb in range(4):
                d_conv_ref[comb(i, 8 * g, SIDE, h, cb), :] = d_conv[
                    8 * g : 8 * g + 8, cb * LANE : (cb + 1) * LANE
                ]
    grad_gain = jnp.sum(total, axis=0, keepdims=True)

    spread_ref[...] = jnp.zeros_like(spread_ref)
    taps_ref[...] = jnp.zeros_like(taps_ref)

    def conv_row(i, carry):
        d_conv = [d_conv_ref[block(i, j, SIDE), :] for j in range(SIDE)]
        for a in range(TAPS):
            taps = [kern_ref[block(a, b, TAPS), :] for b in range(TAPS)]
            sums = [taps_ref[block(a, b, TAPS), :] for b in range(TAPS)]
            for y in range(FULL):
                here = field_ref[block(i + a, y, PITCH), :]
                value = spread_ref[block(i + a, y, PITCH), :]
                for b in range(TAPS):
                    if 0 <= y - b < SIDE:
                        value = value + d_conv[y - b] * taps[b]
                        sums[b] = sums[b] + here * d_conv[y - b]
                spread_ref[block(i + a, y, PITCH), :] = value
            for b in range(TAPS):
                taps_ref[block(a, b, TAPS), :] = sums[b]
        return carry

    lax.fori_loop(0, HALF, conv_row, 0)

    def part(x, y, cb):
        value = None
        if x < ROWS2:
            value = spread_ref[comb(x, y, PITCH, 0, cb), :]
        if x >= HALF:
            more = spread_ref[comb(x - HALF, y, PITCH, 1, cb), :]
            value = more if value is None else value + more
        return value

    for cb in range(4):
        lanes = pl.ds(cb * LANE, LANE)
        for at, x, y in ring():
            ring_ref[pl.ds(at, 8), lanes] = part(x, y, cb)
        for i in range(SIDE):
            for g in range(0, SIDE, 8):
                own_ref[pl.ds(i * SIDE + g, 8), lanes] = part(i + HALO, g + HALO, cb)
    take_strips(core_ref[0], (s0, s1, s2, s3), strips_ref)
    d_halo = dot(place_ref[...], ring_ref[...].astype(BF16), TN).astype(BF16)
    d_own = (own_ref[...] + cot_ref[...].astype(F32)).astype(BF16)
    grad_embed = dot(grid_ref[...], d_own, TN) + dot(strips_ref[...], d_halo, TN)

    half = mine_ref.shape[0]
    small_ref[...] = jnp.zeros_like(small_ref)
    for t in range(half):
        r, c = divmod(t, 4)
        small_ref[t * 16 : (t + 1) * 16] = grad_embed[r * 16 : (r + 1) * 16, c * LANE : (c + 1) * LANE]
    base = half * 16
    for t in range(TAPS * TAPS):
        both = taps_ref[t * 8 : (t + 1) * 8, :]
        small_ref[base + t * 4 : base + (t + 1) * 4] = both[:4] + both[4:]
    for c in range(4):
        at = base + TAPS * TAPS * 4 + c
        small_ref[at : at + 1] = grad_gain[:, c * LANE : (c + 1) * LANE]
    core = core_ref[0]
    for t in range(half):
        mine_ref[t] = small_ref[pl.ds(pl.multiple_of((core * half + t) * 16, 16), 16), :]
        theirs_ref[t] = small_ref[
            pl.ds(pl.multiple_of(((1 - core) * half + t) * 16, 16), 16), :
        ].astype(BF16)


def pair_kernel(core_ref, scaled_ref, active_ref, d_hid_ref, cot_ref, their_ref, out_ref, two_ref, one_ref):
    half, channels = active_ref.shape[1] // 2, cot_ref.shape[1]
    their_scaled = their_ref[:, 2 * half : 2 * half + channels]
    their_cot = their_ref[:, 2 * half + channels :]
    for k in range(half // STEP):
        some = pl.ds(pl.multiple_of(core_ref[0] * half + k * STEP, STEP), STEP)
        two_ref[...] = dot(active_ref[:, some], cot_ref[...], TN) + dot(
            their_ref[:, k * STEP : (k + 1) * STEP], their_cot, TN
        )
        one_ref[...] = dot(scaled_ref[...], d_hid_ref[:, some], TN) + dot(
            their_scaled, their_ref[:, half + k * STEP : half + (k + 1) * STEP], TN
        )
        for t, ref, rows, lanes in tiles_of(k, two_ref, one_ref):
            out_ref[t // 8, t % 8] = ref[rows, lanes].astype(BF16)


def join_kernel(mine_ref, small_ref, paired_far, out_far, tile_ref, sem):
    tile_ref[...] = (mine_ref[...] + small_ref[...].astype(F32)).astype(BF16)
    put = pltpu.make_async_copy(tile_ref, out_far.at[:, 8], sem.at[0])
    put.start()
    put.wait()


def sum_kernel(in_ref, out_ref):
    parts, tiles = in_ref.shape[:2]

    def add(d, sums):
        return [s + in_ref[d, t].astype(F32) for t, s in enumerate(sums)]

    sums = lax.fori_loop(0, parts, add, [jnp.zeros(in_ref.shape[2:], F32)] * tiles)
    sums = [s.astype(BF16) for s in sums]

    def spread(d, carry):
        for t in range(tiles):
            out_ref[d, t] = sums[t]
        return carry

    lax.fori_loop(0, parts, spread, 0)


def assemble_half(core, in_ref, one_far, two_far, one_ref, two_ref, sem):
    steps = one_ref.shape[0]
    puts = []
    for k in range(steps):
        for t, ref, rows, lanes in tiles_of(k, two_ref, one_ref):
            ref[k, rows, lanes] = in_ref[t // 8, t % 8].astype(F32)
        some = pl.ds(pl.multiple_of((core * steps + k) * STEP, STEP), STEP)
        puts += [
            pltpu.make_async_copy(one_ref.at[k], one_far.at[:, some], sem.at[2 * k]),
            pltpu.make_async_copy(two_ref.at[k], two_far.at[some, :], sem.at[2 * k + 1]),
        ]
        puts[-2].start()
        puts[-1].start()
    return puts


def first_kernel(
    core_ref, in_ref, emb_ref, active_ref, w_two_ref,
    one_far, two_far, feature_far, one_ref, two_ref, feature_ref, sem,
):
    puts = assemble_half(core_ref[0], in_ref, one_far, two_far, one_ref, two_ref, sem)
    feature_ref[...] = (emb_ref[...].astype(F32) + dot(active_ref[...], w_two_ref[...])).astype(BF16)
    puts.append(pltpu.make_async_copy(feature_ref, feature_far, sem.at[len(puts)]))
    puts[-1].start()
    for put in puts:
        put.wait()


def second_kernel(
    core_ref, in_ref, mine_ref, one_old, two_old,
    one_far, two_far, embed_far, taps_far, gain_far,
    one_ref, two_ref, rows_ref, embed_ref, taps_ref, gain_ref, sem,
):
    core = core_ref[0]
    puts = assemble_half(1 - core, in_ref, one_far, two_far, one_ref, two_ref, sem)
    count = taps_ref.shape[0]

    def place(first, last):
        for t in range(in_ref.shape[0]):
            r, c = divmod(t, 4)
            embed_ref[r * 16 : (r + 1) * 16, c * LANE : (c + 1) * LANE] = first[t, 8].astype(F32)
        for t in range(rows_ref.shape[0] // 16):
            rows_ref[t * 16 : (t + 1) * 16, :] = last[t, 8].astype(F32)

    @pl.when(core == 0)
    def _():
        place(mine_ref, in_ref)

    @pl.when(core == 1)
    def _():
        place(in_ref, mine_ref)

    for cb in range(4):
        lanes = pl.ds(cb * LANE, LANE)
        for g in range(0, count - 1, 8):
            taps_ref[pl.ds(g, 8), lanes] = rows_ref[pl.ds(g * 4 + cb, 8, stride=4), :]
        taps_ref[pl.ds(count - 1, 1), lanes] = rows_ref[pl.ds((count - 1) * 4 + cb, 1), :]
        gain_ref[:, lanes] = rows_ref[pl.ds(count * 4 + cb, 1), :]
    base = len(puts)
    for k, pair in enumerate(((embed_ref, embed_far), (taps_ref, taps_far), (gain_ref, gain_far))):
        puts.append(pltpu.make_async_copy(*pair, sem.at[base + k]))
        puts[-1].start()
    for put in puts:
        put.wait()


def turned(spin, x, y, last):
    row = jnp.where(spin == 0, x, jnp.where(spin == 1, last - y, jnp.where(spin == 2, last - x, y)))
    col = jnp.where(spin == 0, y, jnp.where(spin == 1, x, jnp.where(spin == 2, last - y, last - x)))
    return row, col


def selectors(spin):
    x = jnp.asarray([x for _, x, _ in ring() for _ in range(8)], jnp.int32)
    y = jnp.asarray([y + k for _, _, y in ring() for k in range(8)], jnp.int32)
    row, col = turned(spin, x, y, FULL - 1)
    end = SIDE + HALO
    in_row, in_col = (row >= HALO) & (row < end), (col >= HALO) & (col < end)
    strip = jnp.where(
        (row < HALO) & in_col, row * SIDE + col - HALO,
        jnp.where((row >= end) & in_col, STRIP + (row - end) * SIDE + col - HALO,
        jnp.where((col < HALO) & in_row, 2 * STRIP + col * SIDE + row - HALO,
        jnp.where((col >= end) & in_row, 3 * STRIP + (col - end) * SIDE + row - HALO, -1))),
    )
    strip = jnp.where(y < FULL, strip, -1)
    k = jnp.arange(4 * STRIP, dtype=jnp.int32)
    place = (strip[:, None] == k[None]).astype(BF16)

    q = jnp.arange(CELLS, dtype=jnp.int32)
    row, col = turned(spin, q // SIDE, q % SIDE, SIDE - 1)
    cut = SIDE - HALO
    by_row = jnp.where(row >= cut, (row - cut) * SIDE + col, jnp.where(row < HALO, STRIP + row * SIDE + col, -1))
    by_col = jnp.where(col >= cut, 2 * STRIP + (col - cut) * SIDE + row, jnp.where(col < HALO, 3 * STRIP + col * SIDE + row, -1))
    pick = ((k[:, None] == by_row[None]) | (k[:, None] == by_col[None])).astype(BF16)
    return place, pick


def exchange(up, down, far, by):
    beside = ("col", "core")
    tiles, faces = lax.axis_size(beside), lax.axis_size("face")
    pairs = [(i, (i + 1) % tiles) for i in range(1, tiles, 2)]
    far = lax.ppermute(far, beside, pairs + [(j, i) for i, j in pairs])
    up = lax.ppermute(up, "face", [(i, (i + 1) % faces) for i in range(faces)])
    down = lax.ppermute(down, "face", [((i + 1) % faces, i) for i in range(faces)])
    return up, down, far, swap(by)


def swap(value):
    return lax.ppermute(value, "core", [(0, 1), (1, 0)])


def on_device(
    obs_values, obs_tile, interp, tile_spin, w_embed, dw_kernel, norm_gain, w_one, w_two, cotangent
):
    tiles, chips = lax.axis_size(ALL), lax.axis_size(CHIPS)
    width, channels = w_embed.shape
    hidden = w_one.shape[1]
    slots = interp.shape[2]
    core = lax.axis_index("core").reshape(1)
    place, pick = selectors(tile_spin[0, 0])
    (leaving,) = call(
        route_kernel,
        [((tiles * 8, LANE), BF16)],
        [((1, obs_values.shape[0]), jnp.int32), (obs_values.shape, BF16)],
        60.5, core, obs_tile.reshape(1, -1), obs_values, far=(1, 2), copies=2,
    )
    arrived = lax.all_to_all(leaving.reshape(tiles, 8, LANE), ALL, 0, 0, tiled=True)
    stacked = ((CELLS, tiles * slots), BF16)
    near = ((width + 80, channels), BF16)
    (shelved,) = call(
        prepare_kernel, [((SHELF, channels), BF16)], [stacked, ((80, channels), F32), near, (w_two.shape, BF16)],
        60.5, interp[0], pick, w_embed, dw_kernel, norm_gain[None], w_two, far=(5,), far_outs=(0,), copies=5,
    )
    gridded, embedded, nearby, *strips = call(
        embed_kernel,
        [((CELLS, width), BF16), ((CELLS, channels), BF16), near] + [((STRIP, width), BF16)] * 4,
        [((tiles * 8, LANE), F32), ((tiles * slots, width), BF16), stacked, (pick.shape, BF16), ((4 * STRIP, width), BF16)],
        16, core, arrived.reshape(tiles * 8, LANE), shelved, far=(2,), copies=3,
    )
    strips = exchange(*strips)
    cells2 = ((ROWS2 * PITCH * 8, LANE), F32)
    kernel = ((TAPS * TAPS * 8, LANE), F32)
    blocks, cells = ((CELLS * 4, LANE), F32), ((CELLS, channels), F32)
    around = ((RING, channels), F32)
    step_sums = [((STEP, channels), F32), ((channels, STEP), F32)]
    field, conv, taps, d_active = call(
        inner_kernel, [cells2, blocks, kernel, ((CELLS, hidden), F32)], [((hidden, channels), BF16)], 20,
        embedded, nearby, shelved, cotangent, far=(2,), copies=1,
    )
    field, normal, inverse, scaled, active, d_hidden, theirs = call(
        forward_kernel,
        [
            cells2,
            cells,
            ((CELLS, LANE), F32),
            ((CELLS, channels), BF16),
            ((CELLS, hidden), BF16),
            ((CELLS, hidden), BF16),
            ((CELLS, hidden + 2 * channels), BF16),
        ],
        [((4 * STRIP, width), BF16), around, blocks],
        20,
        core, *strips, place, nearby, w_one, field, conv, taps, d_active, cotangent,
    )
    big = swap(theirs)

    mine, theirs = call(
        backward_kernel,
        [((chips, 16, LANE), F32), ((chips, 16, LANE), BF16)],
        [cells, blocks, cells2, cells, around, kernel, ((4 * STRIP, width), BF16), ((2 * chips * 16, LANE), F32)],
        20,
        core, gridded, *strips, place, field, normal, inverse, d_hidden, w_one, nearby, taps, cotangent,
    )
    small = swap(theirs)
    whole = ((chips, 9, 16, LANE), BF16)
    (paired,) = call(
        pair_kernel, [whole], step_sums, 20, core, scaled, active, d_hidden, cotangent, big
    )
    (paired,) = call(
        join_kernel, [whole], [((chips, 16, LANE), BF16)], 4,
        mine, small, paired, far=(2,), far_outs=(0,), copies=1, aliases={2: 0},
    )
    paired = lax.all_to_all(paired, CHIPS, 0, 0, tiled=True)
    (summed,) = call(sum_kernel, [whole], [], 4, paired)
    here = lax.all_to_all(summed, CHIPS, 0, 0, tiled=True)
    there = swap(here)

    large = [((channels, hidden), F32), ((hidden, channels), F32)]
    steps = hidden // STEP // 2
    buffers = [((steps, channels, STEP), F32), ((steps, STEP, channels), F32)]
    *grads, output = call(
        first_kernel, large + [((CELLS, channels), BF16)], buffers + [((CELLS, channels), BF16)], 16,
        core, here, embedded, active, w_two, far_outs=(0, 1, 2), copies=2 * steps + 1,
    )
    count = TAPS * TAPS
    minor = [((width, channels), F32), ((count, channels), F32), ((1, channels), F32)]
    grad_one, grad_two, grad_embed, grad_kernel, grad_gain = call(
        second_kernel, large + minor,
        buffers + [((-(-(count + 1) * 4 // 16) * 16, LANE), F32)] + minor, 16,
        core, there, here, *grads,
        far=(3, 4), far_outs=range(5), copies=2 * steps + 3, aliases={3: 0, 4: 1},
    )
    return output, grad_embed, grad_kernel, grad_gain[0], grad_one, grad_two


def solution(mesh):
    faces, tiles = mesh.shape["face"], mesh.shape["tile"]
    fine = jax.sharding.Mesh(mesh.devices.reshape(faces, tiles // 2, 2), ALL)
    split = P(ALL, None)
    in_specs = (split, split, P(ALL, None, None, None), split) + (P(),) * 5 + (split,)
    return jax.shard_map(
        on_device, mesh=fine, in_specs=in_specs, out_specs=(split,) + (P(),) * 5, check_vma=False
    )
```

```python
import jax
import jax.numpy as jnp
from jax import lax
from jax.experimental import pallas as pl
from jax.experimental.pallas import tpu as pltpu
from jax.sharding import PartitionSpec as P

F32 = jnp.float32
BF16 = jnp.bfloat16
SIDE = 16
CELLS = SIDE * SIDE
HALO = 3
TAPS = 7
FULL = SIDE + 2 * HALO
PITCH = 24
HALF = SIDE // 2
LANE = 128
ROWS2 = HALF + TAPS - 1
STRIP = HALO * SIDE
SHELF = 65536
STEP = 256
ALL = ("face", "col", "core")
CHIPS = ("face", "col")
ROOT = 0.7978845608028654
CUBE = 0.044715

NN = (((1,), (0,)), ((), ()))
NT = (((1,), (1,)), ((), ()))
TN = (((0,), (0,)), ((), ()))


def dot(a, b, dims=NN):
    return lax.dot_general(a, b, dims, preferred_element_type=F32)


def call(kernel, outs, scratch, limit, *args, far=(), far_outs=(), copies=0, aliases=None):
    vmem, scalar = pl.BlockSpec(memory_space=pltpu.VMEM), pl.BlockSpec(memory_space=pltpu.SMEM)
    away = pl.BlockSpec(memory_space=pltpu.HBM)
    return pl.pallas_call(
        kernel,
        out_shape=[jax.ShapeDtypeStruct(s, d) for s, d in outs],
        in_specs=[
            scalar if a.shape == (1,) else away if k in far else vmem for k, a in enumerate(args)
        ],
        out_specs=[away if k in far_outs else vmem for k in range(len(outs))],
        scratch_shapes=[pltpu.VMEM(s, d) for s, d in scratch]
        + [pltpu.SemaphoreType.DMA((copies,))] * bool(copies),
        input_output_aliases=aliases or {},
        compiler_params=pltpu.CompilerParams(vmem_limit_bytes=int(limit * 2**20)),
    )(*args)


def start(sem, *pairs):
    moves = [pltpu.make_async_copy(a, b, sem.at[k]) for k, (a, b) in enumerate(pairs)]
    for move in moves:
        move.start()
    return moves


def strip_at(k):
    return pl.ds(pl.multiple_of(k * STRIP, 16), STRIP)


def take_strips(core, odd, refs, strips_ref):
    for ref, k in zip(refs, (2 + core, 1 - odd, odd, 3 - core)):
        strips_ref[strip_at(k), :] = ref[...]


def block(i, j, pitch):
    return pl.ds(pl.multiple_of((i * pitch + j) * 8, 8), 8)


def comb(i, j, pitch, h, cb):
    return pl.ds((i * pitch + j) * 8 + h * 4 + cb, 8, stride=8)


def route_kernel(core_ref, odd_ref, row_far, obs_far, out_ref, row_ref, obs_ref, sem):
    fetch_row, fetch_obs = start(sem, (row_far, row_ref), (obs_far, obs_ref))
    fetch_row.wait()
    row = row_ref[...]
    count = row.shape[1]
    across = jnp.broadcast_to(row, (count, count)).astype(F32)
    earlier = lax.broadcasted_iota(jnp.int32, (count, count), 0) < lax.broadcasted_iota(
        jnp.int32, (count, count), 1
    )
    same = jnp.where((across.T == across) & earlier, 1.0, 0.0)
    rank = jnp.sum(same, axis=0, keepdims=True).astype(jnp.int32)
    place = row * 8 + rank
    lines = out_ref.shape[0]
    line = lax.broadcasted_iota(jnp.int32, (lines, count), 0)
    chosen = jnp.where((line - (line & 4)) == place, 1.0, 0.0).astype(BF16)
    fetch_obs.wait()
    moved = dot(chosen, obs_ref[...])
    first = (lax.broadcasted_iota(jnp.int32, (lines, LANE), 0) & 4) == 0
    out_ref[...] = jnp.where(first, moved[:, :LANE], moved[:, LANE:]).astype(BF16)


def shelf(width, slots, channels):
    rows = (CELLS, 4 * STRIP, width + 80)
    lanes = (slots, CELLS, channels)
    ends = [sum(rows[: k + 1]) for k in range(len(rows))]
    return [(pl.ds(e - r, r), pl.ds(0, n)) for e, r, n in zip(ends, rows, lanes)]


def prepare_kernel(
    spin_ref, interp_far, w_embed_far, dw_far, gain_far, w_two_far, cot_far, shelf_far, d_act_far,
    interp_ref, w_embed_ref, dw_ref, gain_ref, w_two_ref, cot_ref, d_act_ref, weights_ref, pick_ref, small_ref, near_ref, sem,
):
    tiles, slots = interp_ref.shape[:2]
    width, channels = w_embed_ref.shape
    spots = shelf(width, tiles * slots, channels)
    fetches = start(
        sem, (w_two_far, w_two_ref), (interp_far, interp_ref), (w_embed_far, w_embed_ref), (dw_far, dw_ref),
        (gain_far, gain_ref), (cot_far, cot_ref),
    )
    put_weights, put_pick, put_near = (
        pltpu.make_async_copy(a, shelf_far.at[spot], sem.at[6 + k])
        for k, (a, spot) in enumerate(zip((weights_ref, pick_ref, near_ref), spots))
    )
    q = lax.broadcasted_iota(jnp.int32, (1, CELLS), 1)
    by_row, by_col = leaving_strips(spin_ref[0], q // SIDE, q % SIDE)
    k = lax.broadcasted_iota(jnp.int32, pick_ref.shape, 0)
    pick_ref[...] = jnp.where((k == by_row) | (k == by_col), 1.0, 0.0).astype(BF16)
    put_pick.start()
    for fetch in fetches:
        fetch.wait()
    puts = []
    for k in range(0, w_two_ref.shape[0], 2 * STEP):
        some = pl.ds(k, 2 * STEP)
        d_act_ref[:, some] = dot(cot_ref[...], w_two_ref[some, :], NT)
        target = d_act_far.at[pl.ds(0, CELLS), some]
        puts.append(pltpu.make_async_copy(d_act_ref.at[:, some], target, sem.at[9 + len(puts)]))
        puts[-1].start()
    small_ref[...] = jnp.zeros_like(small_ref)
    small_ref[0 : TAPS * TAPS] = dw_ref[...].astype(F32)
    small_ref[64:] = jnp.broadcast_to(gain_ref[...], (16, channels))
    near_ref[0:width] = w_embed_ref[...]
    near_ref[width:] = small_ref[...].astype(BF16)
    put_near.start()
    weights = interp_ref[...].astype(F32)
    for k in range(slots):
        weights_ref[:, k * tiles : (k + 1) * tiles] = weights[:, k, :].T.astype(BF16)
    put_weights.start()
    for put in [put_pick, put_near, put_weights] + puts:
        put.wait()


def embed_kernel(
    core_ref, odd_ref, got_ref, shelf_far, grid_ref, emb_ref, near_ref, far_ref, one_ref, two_ref, by_ref,
    wide_ref, rows_ref, weights_ref, pick_ref, strips_ref, sem,
):
    width, channels = near_ref.shape[0] - 80, near_ref.shape[1]
    spots = shelf(width, weights_ref.shape[1], channels)
    targets = (weights_ref, pick_ref, near_ref)
    fetches = start(sem, *((shelf_far.at[spot], b) for spot, b in zip(spots, targets)))
    wide_ref[...] = got_ref[...].astype(F32)
    tiles = got_ref.shape[0] // 8
    for k in range(4):
        for half in range(2):
            for g in range(0, tiles, 16):
                two = [
                    wide_ref[pl.ds((g + e) * 8 + half * 4 + k, 8, stride=8), :] for e in (0, 8)
                ]
                rows_ref[pl.ds(k * tiles + g, 16), pl.ds(half * LANE, LANE)] = jnp.concatenate(
                    two, axis=0
                ).astype(BF16)
    for fetch in fetches:
        fetch.wait()
    gridded = dot(weights_ref[...], rows_ref[...]).astype(BF16)
    grid_ref[...] = gridded
    strips_ref[...] = dot(pick_ref[...], gridded).astype(BF16)
    core, odd = core_ref[0], odd_ref[0]
    for ref, k in ((far_ref, 3 - core), (one_ref, odd), (two_ref, 1 - odd), (by_ref, 2 + core)):
        ref[...] = strips_ref[strip_at(k), :]
    emb_ref[...] = dot(gridded, near_ref[0:width]).astype(BF16)


def tiles_of(part, two, one):
    for k in range(64):
        r, c = divmod(k, 4)
        yield part * 128 + k, two, pl.ds(r * 16, 16), pl.ds(c * LANE, LANE)
    for k in range(64):
        r, c = divmod(k, 2)
        yield part * 128 + 64 + k, one, pl.ds(r * 16, 16), pl.ds(c * LANE, LANE)


def inner_kernel(
    emb_ref, near_ref, d_act_far, field_ref, conv_ref, kern_ref, d_act_ref, sem
):
    width = near_ref.shape[0] - 80
    (fetch,) = start(sem, (d_act_far.at[pl.ds(0, CELLS), :], d_act_ref))
    taps = near_ref[width : width + 64].astype(F32)
    last = TAPS * TAPS - 1
    for h in range(2):
        for cb in range(4):
            lanes = slice(cb * LANE, (cb + 1) * LANE)
            for g in range(0, last, 8):
                kern_ref[pl.ds(g * 8 + h * 4 + cb, 8, stride=8), :] = taps[g : g + 8, lanes]
            kern_ref[pl.ds(last * 8 + h * 4 + cb, 1), :] = taps[last : last + 1, lanes]
    for i in range(SIDE):
        own = emb_ref[pl.ds(i * SIDE, SIDE), :].astype(F32)
        x = i + HALO
        for g in range(0, SIDE, 8):
            for cb in range(4):
                value = own[g : g + 8, cb * LANE : (cb + 1) * LANE]
                if x < ROWS2:
                    field_ref[comb(x, HALO + g, PITCH, 0, cb), :] = value
                if x >= HALF:
                    field_ref[comb(x - HALF, HALO + g, PITCH, 1, cb), :] = value
    for i in range(HALF):
        sums = [jnp.zeros((8, LANE), F32)] * SIDE
        for x in range(max(i, HALO), min(i + TAPS, HALF + HALO)):
            taps = [kern_ref[block(x - i, b, TAPS), :] for b in range(TAPS)]
            for y in range(HALO, SIDE + HALO):
                here = field_ref[block(x, y, PITCH), :]
                for b in range(TAPS):
                    if 0 <= y - b < SIDE:
                        sums[y - b] = sums[y - b] + here * taps[b]
        for j in range(SIDE):
            conv_ref[block(i, j, SIDE), :] = sums[j]
    fetch.wait()


OUTER = (0, 1, 2, 19, 20, 21)


def ring():
    at = 0
    for x in OUTER:
        for y in range(0, PITCH, 8):
            yield at, x, y
            at += 8
    for x in range(HALO, SIDE + HALO):
        for y in (0, PITCH - 8):
            yield at, x, y
            at += 8


RING = 8 * len(list(ring()))


def forward_kernel(
    core_ref, odd_ref, s0, s1, s2, s3, place_ref, near_ref, w_one_ref, own_ref, part_ref, kern_ref, d_act_ref, cot_ref,
    field_ref, normal_ref, inv_ref, scaled_ref, active_ref, d_hid_ref, theirs_ref,
    strips_ref, ring_ref, conv_ref,
):
    width, channels = near_ref.shape[0] - 80, near_ref.shape[1]
    take_strips(core_ref[0], odd_ref[0], (s0, s1, s2, s3), strips_ref)
    halo = dot(strips_ref[...], near_ref[0:width]).astype(BF16)
    ring_ref[...] = dot(place_ref[...], halo)
    field_ref[...] = own_ref[...]
    for at, x, y in ring():
        skip, count = (0, 8) if x in OUTER else (0, HALO) if y == 0 else (HALO, HALO)
        for cb in range(4):
            value = ring_ref[pl.ds(at + skip, count), pl.ds(cb * LANE, LANE)]
            if x < ROWS2:
                field_ref[pl.ds((x * PITCH + y + skip) * 8 + cb, count, stride=8), :] = value
            if x >= HALF:
                row = ((x - HALF) * PITCH + y + skip) * 8 + 4 + cb
                field_ref[pl.ds(row, count, stride=8), :] = value

    for i in range(HALF):
        sums = [part_ref[block(i, j, SIDE), :] for j in range(SIDE)]
        for a in range(TAPS):
            x = i + a
            whole = x < HALO or x >= HALF + HALO
            taps = [kern_ref[block(a, b, TAPS), :] for b in range(TAPS)]
            for y in range(FULL):
                if whole or y < HALO or y >= SIDE + HALO:
                    here = field_ref[block(x, y, PITCH), :]
                    for b in range(TAPS):
                        if 0 <= y - b < SIDE:
                            sums[y - b] = sums[y - b] + here * taps[b]
        for j in range(SIDE):
            conv_ref[block(i, j, SIDE), :] = sums[j]

    gain = near_ref[width + 64 :].astype(F32)
    for r in range(SIDE):
        h, i = divmod(r, HALF)
        parts = [
            jnp.concatenate([conv_ref[comb(i, 8 * g, SIDE, h, cb), :] for g in range(2)], axis=0)
            for cb in range(4)
        ]
        value = jnp.concatenate(parts, axis=1)
        centred = value - jnp.mean(value, axis=1, keepdims=True)
        inverse = lax.rsqrt(jnp.mean(centred * centred, axis=1, keepdims=True) + 1e-06)
        normal = centred * inverse
        rows = pl.ds(r * SIDE, SIDE)
        normal_ref[rows, :] = normal
        inv_ref[rows, :] = jnp.broadcast_to(inverse, (SIDE, LANE))
        scaled_ref[rows, :] = (normal * gain).astype(BF16)

    for k in range(w_one_ref.shape[1] // STEP):
        some = pl.ds(k * STEP, STEP)
        pre = dot(scaled_ref[...], w_one_ref[:, some])
        cubic = (ROOT * CUBE) * (pre * pre)
        upper = 0.5 + 0.5 * jnp.tanh(pre * (ROOT + cubic))
        active = pre * upper
        slope = upper + active * (1.0 - upper) * (2.0 * ROOT + 6.0 * cubic)
        active_ref[:, some] = active.astype(BF16)
        d_hid_ref[:, some] = (d_act_ref[:, some] * slope).astype(BF16)

    half = w_one_ref.shape[1] // 2
    away = pl.ds(pl.multiple_of((1 - core_ref[0]) * half, half), half)
    theirs_ref[:, 0:half] = active_ref[:, away]
    theirs_ref[:, half : 2 * half] = d_hid_ref[:, away]
    theirs_ref[:, 2 * half : 2 * half + channels] = scaled_ref[...]
    theirs_ref[:, 2 * half + channels :] = cot_ref[...]


def backward_kernel(
    core_ref, odd_ref, grid_ref, s0, s1, s2, s3, place_ref, field_ref, normal_ref, inv_ref, d_hid_ref, w_one_ref,
    near_ref, kern_ref, cot_ref,
    mine_ref, theirs_ref,
    d_scaled_ref, d_conv_ref, spread_ref, own_ref, ring_ref, taps_ref, strips_ref, small_ref,
):
    d_scaled_ref[...] = dot(d_hid_ref[...], w_one_ref[...], NT)
    total = jnp.zeros((SIDE, normal_ref.shape[1]), F32)
    gain = near_ref[near_ref.shape[0] - 16 :].astype(F32)
    for r in range(SIDE):
        h, i = divmod(r, HALF)
        rows = pl.ds(r * SIDE, SIDE)
        normal, d_scaled = normal_ref[rows, :], d_scaled_ref[rows, :]
        total = total + d_scaled * normal
        d_normal = d_scaled * gain
        mean = jnp.mean(d_normal, axis=1, keepdims=True)
        along = jnp.mean(d_normal * normal, axis=1, keepdims=True)
        d_conv = (d_normal - mean - normal * along) * inv_ref[rows, 0:1]
        for g in range(2):
            for cb in range(4):
                d_conv_ref[comb(i, 8 * g, SIDE, h, cb), :] = d_conv[
                    8 * g : 8 * g + 8, cb * LANE : (cb + 1) * LANE
                ]
    grad_gain = jnp.sum(total, axis=0, keepdims=True)

    spread_ref[...] = jnp.zeros_like(spread_ref)
    taps_ref[...] = jnp.zeros_like(taps_ref)

    def conv_row(i, carry):
        d_conv = [d_conv_ref[block(i, j, SIDE), :] for j in range(SIDE)]
        for a in range(TAPS):
            taps = [kern_ref[block(a, b, TAPS), :] for b in range(TAPS)]
            sums = [taps_ref[block(a, b, TAPS), :] for b in range(TAPS)]
            for y in range(FULL):
                here = field_ref[block(i + a, y, PITCH), :]
                value = spread_ref[block(i + a, y, PITCH), :]
                for b in range(TAPS):
                    if 0 <= y - b < SIDE:
                        value = value + d_conv[y - b] * taps[b]
                        sums[b] = sums[b] + here * d_conv[y - b]
                spread_ref[block(i + a, y, PITCH), :] = value
            for b in range(TAPS):
                taps_ref[block(a, b, TAPS), :] = sums[b]
        return carry

    lax.fori_loop(0, HALF, conv_row, 0)

    def part(x, y, cb):
        value = None
        if x < ROWS2:
            value = spread_ref[comb(x, y, PITCH, 0, cb), :]
        if x >= HALF:
            more = spread_ref[comb(x - HALF, y, PITCH, 1, cb), :]
            value = more if value is None else value + more
        return value

    for cb in range(4):
        lanes = pl.ds(cb * LANE, LANE)
        for at, x, y in ring():
            ring_ref[pl.ds(at, 8), lanes] = part(x, y, cb)
        for i in range(SIDE):
            for g in range(0, SIDE, 8):
                own_ref[pl.ds(i * SIDE + g, 8), lanes] = part(i + HALO, g + HALO, cb)
    take_strips(core_ref[0], odd_ref[0], (s0, s1, s2, s3), strips_ref)
    d_halo = dot(place_ref[...], ring_ref[...].astype(BF16), TN).astype(BF16)
    d_own = (own_ref[...] + cot_ref[...].astype(F32)).astype(BF16)
    grad_embed = dot(grid_ref[...], d_own, TN) + dot(strips_ref[...], d_halo, TN)

    half = mine_ref.shape[0]
    small_ref[...] = jnp.zeros_like(small_ref)
    for t in range(half):
        r, c = divmod(t, 4)
        small_ref[t * 16 : (t + 1) * 16] = grad_embed[r * 16 : (r + 1) * 16, c * LANE : (c + 1) * LANE]
    base = half * 16
    for t in range(TAPS * TAPS):
        both = taps_ref[t * 8 : (t + 1) * 8, :]
        small_ref[base + t * 4 : base + (t + 1) * 4] = both[:4] + both[4:]
    for c in range(4):
        at = base + TAPS * TAPS * 4 + c
        small_ref[at : at + 1] = grad_gain[:, c * LANE : (c + 1) * LANE]
    core = core_ref[0]
    for t in range(half):
        mine_ref[t] = small_ref[pl.ds(pl.multiple_of((core * half + t) * 16, 16), 16), :]
        theirs_ref[t] = small_ref[
            pl.ds(pl.multiple_of(((1 - core) * half + t) * 16, 16), 16), :
        ].astype(BF16)


def pair_kernel(core_ref, scaled_ref, active_ref, d_hid_ref, cot_ref, their_ref, out_ref, two_ref, one_ref):
    half, channels = active_ref.shape[1] // 2, cot_ref.shape[1]
    their_scaled = their_ref[:, 2 * half : 2 * half + channels]
    their_cot = their_ref[:, 2 * half + channels :]
    for k in range(half // STEP):
        some = pl.ds(pl.multiple_of(core_ref[0] * half + k * STEP, STEP), STEP)
        two_ref[...] = dot(active_ref[:, some], cot_ref[...], TN) + dot(
            their_ref[:, k * STEP : (k + 1) * STEP], their_cot, TN
        )
        one_ref[...] = dot(scaled_ref[...], d_hid_ref[:, some], TN) + dot(
            their_scaled, their_ref[:, half + k * STEP : half + (k + 1) * STEP], TN
        )
        for t, ref, rows, lanes in tiles_of(k, two_ref, one_ref):
            out_ref[t // 8, t % 8] = ref[rows, lanes].astype(BF16)


def join_kernel(mine_ref, small_ref, paired_far, out_far, tile_ref, sem):
    tile_ref[...] = (mine_ref[...] + small_ref[...].astype(F32)).astype(BF16)
    put = pltpu.make_async_copy(tile_ref, out_far.at[:, 8], sem.at[0])
    put.start()
    put.wait()


def sum_kernel(in_ref, out_ref):
    parts, tiles = in_ref.shape[:2]

    def add(d, sums):
        return [s + in_ref[d, t].astype(F32) for t, s in enumerate(sums)]

    sums = lax.fori_loop(0, parts, add, [jnp.zeros(in_ref.shape[2:], F32)] * tiles)
    sums = [s.astype(BF16) for s in sums]

    def spread(d, carry):
        for t in range(tiles):
            out_ref[d, t] = sums[t]
        return carry

    lax.fori_loop(0, parts, spread, 0)


def assemble_half(core, in_ref, one_far, two_far, one_ref, two_ref, sem):
    steps = one_ref.shape[0]
    puts = []
    for k in range(steps):
        for t, ref, rows, lanes in tiles_of(k, two_ref, one_ref):
            ref[k, rows, lanes] = in_ref[t // 8, t % 8].astype(F32)
        some = pl.ds(pl.multiple_of((core * steps + k) * STEP, STEP), STEP)
        puts += [
            pltpu.make_async_copy(one_ref.at[k], one_far.at[:, some], sem.at[2 * k]),
            pltpu.make_async_copy(two_ref.at[k], two_far.at[some, :], sem.at[2 * k + 1]),
        ]
        puts[-2].start()
        puts[-1].start()
    return puts


def first_kernel(
    core_ref, in_ref, emb_ref, active_ref, w_two_ref,
    one_far, two_far, feature_far, one_ref, two_ref, feature_ref, sem,
):
    puts = assemble_half(core_ref[0], in_ref, one_far, two_far, one_ref, two_ref, sem)
    feature_ref[...] = (emb_ref[...].astype(F32) + dot(active_ref[...], w_two_ref[...])).astype(BF16)
    puts.append(pltpu.make_async_copy(feature_ref, feature_far, sem.at[len(puts)]))
    puts[-1].start()
    for put in puts:
        put.wait()


def second_kernel(
    core_ref, in_ref, mine_ref, one_old, two_old,
    one_far, two_far, embed_far, taps_far, gain_far,
    one_ref, two_ref, rows_ref, embed_ref, taps_ref, gain_ref, sem,
):
    core = core_ref[0]
    count = taps_ref.shape[0]

    def place(first, last):
        for t in range(in_ref.shape[0]):
            r, c = divmod(t, 4)
            embed_ref[r * 16 : (r + 1) * 16, c * LANE : (c + 1) * LANE] = first[t, 8].astype(F32)
        for t in range(rows_ref.shape[0] // 16):
            rows_ref[t * 16 : (t + 1) * 16, :] = last[t, 8].astype(F32)

    @pl.when(core == 0)
    def _():
        place(mine_ref, in_ref)

    @pl.when(core == 1)
    def _():
        place(in_ref, mine_ref)

    for cb in range(4):
        lanes = pl.ds(cb * LANE, LANE)
        for g in range(0, count - 1, 8):
            taps_ref[pl.ds(g, 8), lanes] = rows_ref[pl.ds(g * 4 + cb, 8, stride=4), :]
        taps_ref[pl.ds(count - 1, 1), lanes] = rows_ref[pl.ds((count - 1) * 4 + cb, 1), :]
        gain_ref[:, lanes] = rows_ref[pl.ds(count * 4 + cb, 1), :]
    base = 2 * one_ref.shape[0]
    puts = []
    for k, pair in enumerate(((embed_ref, embed_far), (taps_ref, taps_far), (gain_ref, gain_far))):
        puts.append(pltpu.make_async_copy(*pair, sem.at[base + k]))
        puts[-1].start()
    puts += assemble_half(1 - core, in_ref, one_far, two_far, one_ref, two_ref, sem)
    for put in puts:
        put.wait()


def turned(spin, x, y, last):
    row = jnp.where(spin == 0, x, jnp.where(spin == 1, last - y, jnp.where(spin == 2, last - x, y)))
    col = jnp.where(spin == 0, y, jnp.where(spin == 1, x, jnp.where(spin == 2, last - y, last - x)))
    return row, col


def leaving_strips(spin, x, y):
    row, col = turned(spin, x, y, SIDE - 1)
    cut = SIDE - HALO
    by_row = jnp.where(row >= cut, (row - cut) * SIDE + col, jnp.where(row < HALO, STRIP + row * SIDE + col, -1))
    by_col = jnp.where(col >= cut, 2 * STRIP + (col - cut) * SIDE + row, jnp.where(col < HALO, 3 * STRIP + col * SIDE + row, -1))
    return by_row, by_col


def arriving_strips(spin):
    x = jnp.asarray([x for _, x, _ in ring() for _ in range(8)], jnp.int32)
    y = jnp.asarray([y + k for _, _, y in ring() for k in range(8)], jnp.int32)
    row, col = turned(spin, x, y, FULL - 1)
    end = SIDE + HALO
    in_row, in_col = (row >= HALO) & (row < end), (col >= HALO) & (col < end)
    strip = jnp.where(
        (row < HALO) & in_col, row * SIDE + col - HALO,
        jnp.where((row >= end) & in_col, STRIP + (row - end) * SIDE + col - HALO,
        jnp.where((col < HALO) & in_row, 2 * STRIP + col * SIDE + row - HALO,
        jnp.where((col >= end) & in_row, 3 * STRIP + (col - end) * SIDE + row - HALO, -1))),
    )
    strip = jnp.where(y < FULL, strip, -1)
    k = jnp.arange(4 * STRIP, dtype=jnp.int32)
    place = (strip[:, None] == k[None]).astype(BF16)

    return place


def exchange(far, one, two, by):
    def between(value, axes, first):
        size = lax.axis_size(axes)
        pairs = [(i, (i + 1) % size) for i in range(first, size, 2)]
        return lax.ppermute(value, axes, pairs + [(j, i) for i, j in pairs])

    beside = ("col", "core")
    return between(far, beside, 1), between(one, "face", 0), between(two, "face", 1), between(by, beside, 0)


def swap(value):
    return lax.ppermute(value, "core", [(0, 1), (1, 0)])


def on_device(
    obs_values, obs_tile, interp, tile_spin, w_embed, dw_kernel, norm_gain, w_one, w_two, cotangent
):
    tiles, chips = lax.axis_size(ALL), lax.axis_size(CHIPS)
    width, channels = w_embed.shape
    hidden = w_one.shape[1]
    slots = interp.shape[2]
    core, odd = lax.axis_index("core").reshape(1), (lax.axis_index("face") % 2).reshape(1)
    place = arriving_strips(tile_spin[0, 0])
    (leaving,) = call(
        route_kernel,
        [((tiles * 8, LANE), BF16)],
        [((1, obs_values.shape[0]), jnp.int32), (obs_values.shape, BF16)],
        60.5, core, odd, obs_tile.reshape(1, -1), obs_values, far=(2, 3), copies=2,
    )
    arrived = lax.all_to_all(leaving.reshape(tiles, 8, LANE), ALL, 0, 0, tiled=True)
    stacked = ((CELLS, tiles * slots), BF16)
    near = ((width + 80, channels), BF16)
    picks = ((4 * STRIP, CELLS), BF16)
    shelved, d_active = call(
        prepare_kernel,
        [((SHELF, channels), BF16), ((SHELF // 8, hidden), F32)],
        [
            (interp.shape[1:], BF16),
            (w_embed.shape, BF16),
            (dw_kernel.shape, BF16),
            ((1, channels), F32),
            (w_two.shape, BF16),
            (cotangent.shape, BF16),
            ((CELLS, hidden), F32),
            stacked,
            picks,
            ((80, channels), F32),
            near,
        ],
        60.5, tile_spin.reshape(1), interp[0], w_embed, dw_kernel, norm_gain.astype(F32)[None], w_two, cotangent,
        far=(1, 2, 3, 4, 5, 6), far_outs=(0, 1), copies=9 + hidden // (2 * STEP),
    )
    gridded, embedded, nearby, *strips = call(
        embed_kernel,
        [((CELLS, width), BF16), ((CELLS, channels), BF16), near] + [((STRIP, width), BF16)] * 4,
        [((tiles * 8, LANE), F32), ((tiles * slots, width), BF16), stacked, picks, ((4 * STRIP, width), BF16)],
        16, core, odd, arrived.reshape(tiles * 8, LANE), shelved, far=(3,), copies=3,
    )
    strips = exchange(*strips)
    cells2 = ((ROWS2 * PITCH * 8, LANE), F32)
    kernel = ((TAPS * TAPS * 8, LANE), F32)
    blocks, cells = ((CELLS * 4, LANE), F32), ((CELLS, channels), F32)
    around = ((RING, channels), F32)
    step_sums = [((STEP, channels), F32), ((channels, STEP), F32)]
    field, conv, taps, d_active = call(
        inner_kernel, [cells2, blocks, kernel, ((CELLS, hidden), F32)], [], 20,
        embedded, nearby, d_active, far=(2,), copies=1,
    )
    field, normal, inverse, scaled, active, d_hidden, theirs = call(
        forward_kernel,
        [
            cells2,
            cells,
            ((CELLS, LANE), F32),
            ((CELLS, channels), BF16),
            ((CELLS, hidden), BF16),
            ((CELLS, hidden), BF16),
            ((CELLS, hidden + 2 * channels), BF16),
        ],
        [((4 * STRIP, width), BF16), around, blocks],
        20,
        core, odd, *strips, place, nearby, w_one, field, conv, taps, d_active, cotangent,
    )
    big = swap(theirs)

    mine, theirs = call(
        backward_kernel,
        [((chips, 16, LANE), F32), ((chips, 16, LANE), BF16)],
        [cells, blocks, cells2, cells, around, kernel, ((4 * STRIP, width), BF16), ((2 * chips * 16, LANE), F32)],
        20,
        core, odd, gridded, *strips, place, field, normal, inverse, d_hidden, w_one, nearby, taps, cotangent,
    )
    small = swap(theirs)
    whole = ((chips, 9, 16, LANE), BF16)
    (paired,) = call(
        pair_kernel, [whole], step_sums, 20, core, scaled, active, d_hidden, cotangent, big
    )
    (paired,) = call(
        join_kernel, [whole], [((chips, 16, LANE), BF16)], 4,
        mine, small, paired, far=(2,), far_outs=(0,), copies=1, aliases={2: 0},
    )
    paired = lax.all_to_all(paired, CHIPS, 0, 0, tiled=True)
    (summed,) = call(sum_kernel, [whole], [], 4, paired)
    here = lax.all_to_all(summed, CHIPS, 0, 0, tiled=True)
    there = swap(here)

    large = [((channels, hidden), F32), ((hidden, channels), F32)]
    steps = hidden // STEP // 2
    buffers = [((steps, channels, STEP), F32), ((steps, STEP, channels), F32)]
    *grads, output = call(
        first_kernel, large + [((CELLS, channels), BF16)], buffers + [((CELLS, channels), BF16)], 16,
        core, here, embedded, active, w_two, far_outs=(0, 1, 2), copies=2 * steps + 1,
    )
    count = TAPS * TAPS
    minor = [((width, channels), F32), ((count, channels), F32), ((1, channels), F32)]
    grad_one, grad_two, grad_embed, grad_kernel, grad_gain = call(
        second_kernel, large + minor,
        buffers + [((-(-(count + 1) * 4 // 16) * 16, LANE), F32)] + minor, 16,
        core, there, here, *grads,
        far=(3, 4), far_outs=range(5), copies=2 * steps + 3, aliases={3: 0, 4: 1},
    )
    return output, grad_embed, grad_kernel, grad_gain[0], grad_one, grad_two


def solution(mesh):
    faces, tiles = mesh.shape["face"], mesh.shape["tile"]
    fine = jax.sharding.Mesh(mesh.devices.reshape(faces, tiles // 2, 2), ALL)
    split = P(ALL, None)
    in_specs = (split, split, P(ALL, None, None, None), split) + (P(),) * 5 + (split,)
    return jax.shard_map(
        on_device, mesh=fine, in_specs=in_specs, out_specs=(split,) + (P(),) * 5, check_vma=False
    )
```

```python
import jax
import jax.numpy as jnp
from jax import lax
from jax.experimental import pallas as pl
from jax.experimental.pallas import tpu as pltpu
from jax.sharding import PartitionSpec as P

F32 = jnp.float32
BF16 = jnp.bfloat16
SIDE = 16
CELLS = SIDE * SIDE
HALO = 3
TAPS = 7
FULL = SIDE + 2 * HALO
PITCH = 24
HALF = SIDE // 2
LANE = 128
ROWS2 = HALF + TAPS - 1
STRIP = HALO * SIDE
SHELF = 65536
STEP = 256
ALL = ("face", "col", "core")
CHIPS = ("face", "col")
ROOT = 0.7978845608028654
CUBE = 0.044715

NN = (((1,), (0,)), ((), ()))
NT = (((1,), (1,)), ((), ()))
TN = (((0,), (0,)), ((), ()))


def dot(a, b, dims=NN):
    return lax.dot_general(a, b, dims, preferred_element_type=F32)


def call(kernel, outs, scratch, limit, *args, far=(), far_outs=(), copies=0, aliases=None):
    vmem, scalar = pl.BlockSpec(memory_space=pltpu.VMEM), pl.BlockSpec(memory_space=pltpu.SMEM)
    away = pl.BlockSpec(memory_space=pltpu.HBM)
    return pl.pallas_call(
        kernel,
        out_shape=[jax.ShapeDtypeStruct(s, d) for s, d in outs],
        in_specs=[
            scalar if a.shape == (1,) else away if k in far else vmem for k, a in enumerate(args)
        ],
        out_specs=[away if k in far_outs else vmem for k in range(len(outs))],
        scratch_shapes=[pltpu.VMEM(s, d) for s, d in scratch]
        + [pltpu.SemaphoreType.DMA((copies,))] * bool(copies),
        input_output_aliases=aliases or {},
        compiler_params=pltpu.CompilerParams(vmem_limit_bytes=int(limit * 2**20)),
    )(*args)


def start(sem, *pairs):
    moves = [pltpu.make_async_copy(a, b, sem.at[k]) for k, (a, b) in enumerate(pairs)]
    for move in moves:
        move.start()
    return moves


def strip_at(k):
    return pl.ds(pl.multiple_of(k * STRIP, 16), STRIP)


def take_strips(core, odd, refs, strips_ref):
    for ref, k in zip(refs, (2 + core, 1 - odd, odd, 3 - core)):
        strips_ref[strip_at(k), :] = ref[...]


def block(i, j, pitch):
    return pl.ds(pl.multiple_of((i * pitch + j) * 8, 8), 8)


def comb(i, j, pitch, h, cb):
    return pl.ds((i * pitch + j) * 8 + h * 4 + cb, 8, stride=8)


def route_kernel(core_ref, odd_ref, row_far, obs_far, out_ref, row_ref, obs_ref, sem):
    fetch_row, fetch_obs = start(sem, (row_far, row_ref), (obs_far, obs_ref))
    fetch_row.wait()
    row = row_ref[...]
    count = row.shape[1]
    across = jnp.broadcast_to(row, (count, count)).astype(F32)
    earlier = lax.broadcasted_iota(jnp.int32, (count, count), 0) < lax.broadcasted_iota(
        jnp.int32, (count, count), 1
    )
    same = jnp.where((across.T == across) & earlier, 1.0, 0.0)
    rank = jnp.sum(same, axis=0, keepdims=True).astype(jnp.int32)
    place = row * 8 + rank
    lines = out_ref.shape[0]
    line = lax.broadcasted_iota(jnp.int32, (lines, count), 0)
    chosen = jnp.where((line - (line & 4)) == place, 1.0, 0.0).astype(BF16)
    fetch_obs.wait()
    moved = dot(chosen, obs_ref[...])
    first = (lax.broadcasted_iota(jnp.int32, (lines, LANE), 0) & 4) == 0
    out_ref[...] = jnp.where(first, moved[:, :LANE], moved[:, LANE:]).astype(BF16)


OUTER = (0, 1, 2, 19, 20, 21)


def ring():
    at = 0
    for x in OUTER:
        for y in range(0, PITCH, 8):
            yield at, x, y
            at += 8
    for x in range(HALO, SIDE + HALO):
        for y in (0, PITCH - 8):
            yield at, x, y
            at += 8


RING = 8 * len(list(ring()))


def shelf(width, slots, channels):
    rows = (CELLS, 4 * STRIP, width + 80, RING)
    lanes = (slots, CELLS, channels, CELLS)
    ends = [sum(rows[: k + 1]) for k in range(len(rows))]
    return [(pl.ds(e - r, r), pl.ds(0, n)) for e, r, n in zip(ends, rows, lanes)]


def prepare_kernel(
    spin_ref, interp_far, w_embed_far, dw_far, gain_far, w_two_far, cot_far, shelf_far, d_act_far,
    interp_ref, w_embed_ref, dw_ref, gain_ref, w_two_ref, cot_ref, d_act_ref, weights_ref, pick_ref, small_ref, near_ref,
    place_ref, sem,
):
    tiles, slots = interp_ref.shape[:2]
    width, channels = w_embed_ref.shape
    spots = shelf(width, tiles * slots, channels)
    fetches = start(
        sem, (interp_far, interp_ref), (cot_far, cot_ref), (w_embed_far, w_embed_ref), (dw_far, dw_ref),
        (gain_far, gain_ref), (w_two_far, w_two_ref),
    )
    put_weights, put_pick, put_near, put_place = (
        pltpu.make_async_copy(a, shelf_far.at[spot], sem.at[6 + k])
        for k, (a, spot) in enumerate(zip((weights_ref, pick_ref, near_ref, place_ref), spots))
    )
    spin = spin_ref[0]
    q = lax.broadcasted_iota(jnp.int32, (1, CELLS), 1)
    by_row, by_col = leaving_strips(spin, q // SIDE, q % SIDE)
    k = lax.broadcasted_iota(jnp.int32, pick_ref.shape, 0)
    pick_ref[...] = jnp.where((k == by_row) | (k == by_col), 1.0, 0.0).astype(BF16)
    put_pick.start()
    fetches[0].wait()
    weights = interp_ref[...].astype(F32)
    for k in range(slots):
        weights_ref[:, k * tiles : (k + 1) * tiles] = weights[:, k, :].T.astype(BF16)
    put_weights.start()
    p = lax.broadcasted_iota(jnp.int32, (RING, 1), 0)
    outer = len(OUTER) * PITCH
    o, r = (p * 171) >> 12, p - outer
    x = jnp.where(p < outer, jnp.where(o < HALO, o, o + SIDE), HALO + (r >> 4))
    y = jnp.where(p < outer, p - o * PITCH, (r & 15) + (r & 8))
    strip = arriving_strips(spin, x, y)
    k = lax.broadcasted_iota(jnp.int32, place_ref.shape, 1)
    place_ref[...] = jnp.where(strip == k, 1.0, 0.0).astype(BF16)
    put_place.start()
    for fetch in fetches[1:]:
        fetch.wait()
    small_ref[...] = jnp.zeros_like(small_ref)
    small_ref[0 : TAPS * TAPS] = dw_ref[...].astype(F32)
    gain = gain_ref[...].astype(F32)
    for c in range(channels // LANE):
        small_ref[64:, c * LANE : (c + 1) * LANE] = jnp.broadcast_to(gain[c : c + 1], (16, LANE))
    near_ref[0:width] = w_embed_ref[...]
    near_ref[width:] = small_ref[...].astype(BF16)
    put_near.start()
    puts = []
    for k in range(0, w_two_ref.shape[0], 2 * STEP):
        some = pl.ds(k, 2 * STEP)
        d_act_ref[:, some] = dot(cot_ref[...], w_two_ref[some, :], NT)
        target = d_act_far.at[pl.ds(0, CELLS), some]
        puts.append(pltpu.make_async_copy(d_act_ref.at[:, some], target, sem.at[10 + len(puts)]))
        puts[-1].start()
    for put in [put_pick, put_near, put_weights, put_place] + puts:
        put.wait()


def embed_kernel(
    core_ref, odd_ref, got_ref, shelf_far, grid_ref, emb_ref, near_ref, place_ref, far_ref, one_ref, two_ref, by_ref,
    wide_ref, rows_ref, weights_ref, pick_ref, strips_ref, sem,
):
    width, channels = near_ref.shape[0] - 80, near_ref.shape[1]
    spots = shelf(width, weights_ref.shape[1], channels)
    targets = (weights_ref, pick_ref, near_ref, place_ref)
    fetches = start(sem, *((shelf_far.at[spot], b) for spot, b in zip(spots, targets)))
    wide_ref[...] = got_ref[...].astype(F32)
    tiles = got_ref.shape[0] // 8
    for k in range(4):
        for half in range(2):
            for g in range(0, tiles, 16):
                two = [
                    wide_ref[pl.ds((g + e) * 8 + half * 4 + k, 8, stride=8), :] for e in (0, 8)
                ]
                rows_ref[pl.ds(k * tiles + g, 16), pl.ds(half * LANE, LANE)] = jnp.concatenate(
                    two, axis=0
                ).astype(BF16)
    for fetch in fetches:
        fetch.wait()
    gridded = dot(weights_ref[...], rows_ref[...]).astype(BF16)
    grid_ref[...] = gridded
    strips_ref[...] = dot(pick_ref[...], gridded).astype(BF16)
    core, odd = core_ref[0], odd_ref[0]
    for ref, k in ((far_ref, 3 - core), (one_ref, odd), (two_ref, 1 - odd), (by_ref, 2 + core)):
        ref[...] = strips_ref[strip_at(k), :]
    emb_ref[...] = dot(gridded, near_ref[0:width]).astype(BF16)


def tiles_of(part, two, one):
    for k in range(64):
        r, c = divmod(k, 4)
        yield part * 128 + k, two, pl.ds(r * 16, 16), pl.ds(c * LANE, LANE)
    for k in range(64):
        r, c = divmod(k, 2)
        yield part * 128 + 64 + k, one, pl.ds(r * 16, 16), pl.ds(c * LANE, LANE)


def inner_kernel(
    emb_ref, near_ref, d_act_far, field_ref, conv_ref, kern_ref, d_act_ref, sem
):
    width = near_ref.shape[0] - 80
    (fetch,) = start(sem, (d_act_far.at[pl.ds(0, CELLS), :], d_act_ref))
    taps = near_ref[width : width + 64].astype(F32)
    last = TAPS * TAPS - 1
    for h in range(2):
        for cb in range(4):
            lanes = slice(cb * LANE, (cb + 1) * LANE)
            for g in range(0, last, 8):
                kern_ref[pl.ds(g * 8 + h * 4 + cb, 8, stride=8), :] = taps[g : g + 8, lanes]
            kern_ref[pl.ds(last * 8 + h * 4 + cb, 1), :] = taps[last : last + 1, lanes]
    for i in range(SIDE):
        own = emb_ref[pl.ds(i * SIDE, SIDE), :].astype(F32)
        x = i + HALO
        for g in range(0, SIDE, 8):
            for cb in range(4):
                value = own[g : g + 8, cb * LANE : (cb + 1) * LANE]
                if x < ROWS2:
                    field_ref[comb(x, HALO + g, PITCH, 0, cb), :] = value
                if x >= HALF:
                    field_ref[comb(x - HALF, HALO + g, PITCH, 1, cb), :] = value
    for i in range(HALF):
        sums = [jnp.zeros((8, LANE), F32)] * SIDE
        for x in range(max(i, HALO), min(i + TAPS, HALF + HALO)):
            taps = [kern_ref[block(x - i, b, TAPS), :] for b in range(TAPS)]
            for y in range(HALO, SIDE + HALO):
                here = field_ref[block(x, y, PITCH), :]
                for b in range(TAPS):
                    if 0 <= y - b < SIDE:
                        sums[y - b] = sums[y - b] + here * taps[b]
        for j in range(SIDE):
            conv_ref[block(i, j, SIDE), :] = sums[j]
    fetch.wait()


def forward_kernel(
    core_ref, odd_ref, s0, s1, s2, s3, place_ref, near_ref, w_one_ref, own_ref, part_ref, kern_ref, d_act_ref, cot_ref,
    field_ref, normal_ref, inv_ref, scaled_ref, active_ref, d_hid_ref, theirs_ref,
    strips_ref, ring_ref, conv_ref,
):
    width, channels = near_ref.shape[0] - 80, near_ref.shape[1]
    take_strips(core_ref[0], odd_ref[0], (s0, s1, s2, s3), strips_ref)
    halo = dot(strips_ref[...], near_ref[0:width]).astype(BF16)
    ring_ref[...] = dot(place_ref[:, : 4 * STRIP], halo)
    field_ref[...] = own_ref[...]
    for at, x, y in ring():
        skip, count = (0, 8) if x in OUTER else (0, HALO) if y == 0 else (HALO, HALO)
        for cb in range(4):
            value = ring_ref[pl.ds(at + skip, count), pl.ds(cb * LANE, LANE)]
            if x < ROWS2:
                field_ref[pl.ds((x * PITCH + y + skip) * 8 + cb, count, stride=8), :] = value
            if x >= HALF:
                row = ((x - HALF) * PITCH + y + skip) * 8 + 4 + cb
                field_ref[pl.ds(row, count, stride=8), :] = value

    for i in range(HALF):
        sums = [part_ref[block(i, j, SIDE), :] for j in range(SIDE)]
        for a in range(TAPS):
            x = i + a
            whole = x < HALO or x >= HALF + HALO
            taps = [kern_ref[block(a, b, TAPS), :] for b in range(TAPS)]
            for y in range(FULL):
                if whole or y < HALO or y >= SIDE + HALO:
                    here = field_ref[block(x, y, PITCH), :]
                    for b in range(TAPS):
                        if 0 <= y - b < SIDE:
                            sums[y - b] = sums[y - b] + here * taps[b]
        for j in range(SIDE):
            conv_ref[block(i, j, SIDE), :] = sums[j]

    gain = near_ref[width + 64 :].astype(F32)
    for r in range(SIDE):
        h, i = divmod(r, HALF)
        parts = [
            jnp.concatenate([conv_ref[comb(i, 8 * g, SIDE, h, cb), :] for g in range(2)], axis=0)
            for cb in range(4)
        ]
        value = jnp.concatenate(parts, axis=1)
        centred = value - jnp.mean(value, axis=1, keepdims=True)
        inverse = lax.rsqrt(jnp.mean(centred * centred, axis=1, keepdims=True) + 1e-06)
        normal = centred * inverse
        rows = pl.ds(r * SIDE, SIDE)
        normal_ref[rows, :] = normal
        inv_ref[rows, :] = jnp.broadcast_to(inverse, (SIDE, LANE))
        scaled_ref[rows, :] = (normal * gain).astype(BF16)

    for k in range(w_one_ref.shape[1] // STEP):
        some = pl.ds(k * STEP, STEP)
        pre = dot(scaled_ref[...], w_one_ref[:, some])
        cubic = (ROOT * CUBE) * (pre * pre)
        upper = 0.5 + 0.5 * jnp.tanh(pre * (ROOT + cubic))
        active = pre * upper
        slope = upper + active * (1.0 - upper) * (2.0 * ROOT + 6.0 * cubic)
        active_ref[:, some] = active.astype(BF16)
        d_hid_ref[:, some] = (d_act_ref[:, some] * slope).astype(BF16)

    half = w_one_ref.shape[1] // 2
    away = pl.ds(pl.multiple_of((1 - core_ref[0]) * half, half), half)
    theirs_ref[:, 0:half] = active_ref[:, away]
    theirs_ref[:, half : 2 * half] = d_hid_ref[:, away]
    theirs_ref[:, 2 * half : 2 * half + channels] = scaled_ref[...]
    theirs_ref[:, 2 * half + channels :] = cot_ref[...]


def backward_kernel(
    core_ref, odd_ref, grid_ref, s0, s1, s2, s3, place_ref, field_ref, normal_ref, inv_ref, d_hid_ref, w_one_ref,
    near_ref, kern_ref, cot_ref,
    mine_ref, theirs_ref,
    d_scaled_ref, d_conv_ref, spread_ref, own_ref, ring_ref, taps_ref, strips_ref, small_ref,
):
    d_scaled_ref[...] = dot(d_hid_ref[...], w_one_ref[...], NT)
    total = jnp.zeros((SIDE, normal_ref.shape[1]), F32)
    gain = near_ref[near_ref.shape[0] - 16 :].astype(F32)
    for r in range(SIDE):
        h, i = divmod(r, HALF)
        rows = pl.ds(r * SIDE, SIDE)
        normal, d_scaled = normal_ref[rows, :], d_scaled_ref[rows, :]
        total = total + d_scaled * normal
        d_normal = d_scaled * gain
        mean = jnp.mean(d_normal, axis=1, keepdims=True)
        along = jnp.mean(d_normal * normal, axis=1, keepdims=True)
        d_conv = (d_normal - mean - normal * along) * inv_ref[rows, 0:1]
        for g in range(2):
            for cb in range(4):
                d_conv_ref[comb(i, 8 * g, SIDE, h, cb), :] = d_conv[
                    8 * g : 8 * g + 8, cb * LANE : (cb + 1) * LANE
                ]
    grad_gain = jnp.sum(total, axis=0, keepdims=True)

    spread_ref[...] = jnp.zeros_like(spread_ref)
    taps_ref[...] = jnp.zeros_like(taps_ref)

    def conv_row(i, carry):
        d_conv = [d_conv_ref[block(i, j, SIDE), :] for j in range(SIDE)]
        for a in range(TAPS):
            taps = [kern_ref[block(a, b, TAPS), :] for b in range(TAPS)]
            sums = [taps_ref[block(a, b, TAPS), :] for b in range(TAPS)]
            for y in range(FULL):
                here = field_ref[block(i + a, y, PITCH), :]
                value = spread_ref[block(i + a, y, PITCH), :]
                for b in range(TAPS):
                    if 0 <= y - b < SIDE:
                        value = value + d_conv[y - b] * taps[b]
                        sums[b] = sums[b] + here * d_conv[y - b]
                spread_ref[block(i + a, y, PITCH), :] = value
            for b in range(TAPS):
                taps_ref[block(a, b, TAPS), :] = sums[b]
        return carry

    lax.fori_loop(0, HALF, conv_row, 0)

    def part(x, y, cb):
        value = None
        if x < ROWS2:
            value = spread_ref[comb(x, y, PITCH, 0, cb), :]
        if x >= HALF:
            more = spread_ref[comb(x - HALF, y, PITCH, 1, cb), :]
            value = more if value is None else value + more
        return value

    for cb in range(4):
        lanes = pl.ds(cb * LANE, LANE)
        for at, x, y in ring():
            ring_ref[pl.ds(at, 8), lanes] = part(x, y, cb)
        for i in range(SIDE):
            for g in range(0, SIDE, 8):
                own_ref[pl.ds(i * SIDE + g, 8), lanes] = part(i + HALO, g + HALO, cb)
    take_strips(core_ref[0], odd_ref[0], (s0, s1, s2, s3), strips_ref)
    d_halo = dot(place_ref[:, : 4 * STRIP], ring_ref[...].astype(BF16), TN).astype(BF16)
    d_own = (own_ref[...] + cot_ref[...].astype(F32)).astype(BF16)
    grad_embed = dot(grid_ref[...], d_own, TN) + dot(strips_ref[...], d_halo, TN)

    half = mine_ref.shape[0]
    small_ref[...] = jnp.zeros_like(small_ref)
    for t in range(half):
        r, c = divmod(t, 4)
        small_ref[t * 16 : (t + 1) * 16] = grad_embed[r * 16 : (r + 1) * 16, c * LANE : (c + 1) * LANE]
    base = half * 16
    for t in range(TAPS * TAPS):
        both = taps_ref[t * 8 : (t + 1) * 8, :]
        small_ref[base + t * 4 : base + (t + 1) * 4] = both[:4] + both[4:]
    for c in range(4):
        at = base + TAPS * TAPS * 4 + c
        small_ref[at : at + 1] = grad_gain[:, c * LANE : (c + 1) * LANE]
    core = core_ref[0]
    for t in range(half):
        mine_ref[t] = small_ref[pl.ds(pl.multiple_of((core * half + t) * 16, 16), 16), :]
        theirs_ref[t] = small_ref[
            pl.ds(pl.multiple_of(((1 - core) * half + t) * 16, 16), 16), :
        ].astype(BF16)


def pair_kernel(core_ref, scaled_ref, active_ref, d_hid_ref, cot_ref, their_ref, out_ref, two_ref, one_ref):
    half, channels = active_ref.shape[1] // 2, cot_ref.shape[1]
    their_scaled = their_ref[:, 2 * half : 2 * half + channels]
    their_cot = their_ref[:, 2 * half + channels :]
    for k in range(half // STEP):
        some = pl.ds(pl.multiple_of(core_ref[0] * half + k * STEP, STEP), STEP)
        two_ref[...] = dot(active_ref[:, some], cot_ref[...], TN) + dot(
            their_ref[:, k * STEP : (k + 1) * STEP], their_cot, TN
        )
        one_ref[...] = dot(scaled_ref[...], d_hid_ref[:, some], TN) + dot(
            their_scaled, their_ref[:, half + k * STEP : half + (k + 1) * STEP], TN
        )
        for t, ref, rows, lanes in tiles_of(k, two_ref, one_ref):
            out_ref[t // 8, t % 8] = ref[rows, lanes].astype(BF16)


def join_kernel(mine_ref, small_ref, paired_far, out_far, tile_ref, sem):
    tile_ref[...] = (mine_ref[...] + small_ref[...].astype(F32)).astype(BF16)
    put = pltpu.make_async_copy(tile_ref, out_far.at[:, 8], sem.at[0])
    put.start()
    put.wait()


def sum_kernel(in_ref, out_ref):
    parts, tiles = in_ref.shape[:2]

    def add(d, sums):
        return [s + in_ref[d, t].astype(F32) for t, s in enumerate(sums)]

    sums = lax.fori_loop(0, parts, add, [jnp.zeros(in_ref.shape[2:], F32)] * tiles, unroll=4)
    sums = [s.astype(BF16) for s in sums]

    def spread(d, carry):
        for t in range(tiles):
            out_ref[d, t] = sums[t]
        return carry

    lax.fori_loop(0, parts, spread, 0, unroll=4)


def assemble_half(core, in_ref, one_far, two_far, one_ref, two_ref, sem):
    steps = one_ref.shape[0]
    puts = []
    for k in range(steps):
        for t, ref, rows, lanes in tiles_of(k, two_ref, one_ref):
            ref[k, rows, lanes] = in_ref[t // 8, t % 8].astype(F32)
        some = pl.ds(pl.multiple_of((core * steps + k) * STEP, STEP), STEP)
        puts += [
            pltpu.make_async_copy(one_ref.at[k], one_far.at[:, some], sem.at[2 * k]),
            pltpu.make_async_copy(two_ref.at[k], two_far.at[some, :], sem.at[2 * k + 1]),
        ]
        puts[-2].start()
        puts[-1].start()
    return puts


def first_kernel(
    core_ref, in_ref, emb_ref, active_ref, w_two_ref,
    one_far, two_far, feature_far, one_ref, two_ref, feature_ref, sem,
):
    puts = assemble_half(core_ref[0], in_ref, one_far, two_far, one_ref, two_ref, sem)
    feature_ref[...] = (emb_ref[...].astype(F32) + dot(active_ref[...], w_two_ref[...])).astype(BF16)
    puts.append(pltpu.make_async_copy(feature_ref, feature_far, sem.at[len(puts)]))
    puts[-1].start()
    for put in puts:
        put.wait()


def second_kernel(
    core_ref, in_ref, mine_ref, one_old, two_old,
    one_far, two_far, embed_far, taps_far, gain_far,
    one_ref, two_ref, rows_ref, embed_ref, taps_ref, gain_ref, sem,
):
    core = core_ref[0]
    count = taps_ref.shape[0]

    def place(first, last):
        for t in range(in_ref.shape[0]):
            r, c = divmod(t, 4)
            embed_ref[r * 16 : (r + 1) * 16, c * LANE : (c + 1) * LANE] = first[t, 8].astype(F32)
        for t in range(rows_ref.shape[0] // 16):
            rows_ref[t * 16 : (t + 1) * 16, :] = last[t, 8].astype(F32)

    @pl.when(core == 0)
    def _():
        place(mine_ref, in_ref)

    @pl.when(core == 1)
    def _():
        place(in_ref, mine_ref)

    for cb in range(4):
        lanes = pl.ds(cb * LANE, LANE)
        for g in range(0, count - 1, 8):
            taps_ref[pl.ds(g, 8), lanes] = rows_ref[pl.ds(g * 4 + cb, 8, stride=4), :]
        taps_ref[pl.ds(count - 1, 1), lanes] = rows_ref[pl.ds((count - 1) * 4 + cb, 1), :]
        gain_ref[:, lanes] = rows_ref[pl.ds(count * 4 + cb, 1), :]
    base = 2 * one_ref.shape[0]
    puts = []
    for k, pair in enumerate(((embed_ref, embed_far), (taps_ref, taps_far), (gain_ref, gain_far))):
        puts.append(pltpu.make_async_copy(*pair, sem.at[base + k]))
        puts[-1].start()
    puts += assemble_half(1 - core, in_ref, one_far, two_far, one_ref, two_ref, sem)
    for put in puts:
        put.wait()


def turned(spin, x, y, last):
    row = jnp.where(spin == 0, x, jnp.where(spin == 1, last - y, jnp.where(spin == 2, last - x, y)))
    col = jnp.where(spin == 0, y, jnp.where(spin == 1, x, jnp.where(spin == 2, last - y, last - x)))
    return row, col


def leaving_strips(spin, x, y):
    row, col = turned(spin, x, y, SIDE - 1)
    cut = SIDE - HALO
    by_row = jnp.where(row >= cut, (row - cut) * SIDE + col, jnp.where(row < HALO, STRIP + row * SIDE + col, -1))
    by_col = jnp.where(col >= cut, 2 * STRIP + (col - cut) * SIDE + row, jnp.where(col < HALO, 3 * STRIP + col * SIDE + row, -1))
    return by_row, by_col


def arriving_strips(spin, x, y):
    row, col = turned(spin, x, y, FULL - 1)
    end = SIDE + HALO
    in_row, in_col = (row >= HALO) & (row < end), (col >= HALO) & (col < end)
    strip = jnp.where(
        (row < HALO) & in_col, row * SIDE + col - HALO,
        jnp.where((row >= end) & in_col, STRIP + (row - end) * SIDE + col - HALO,
        jnp.where((col < HALO) & in_row, 2 * STRIP + col * SIDE + row - HALO,
        jnp.where((col >= end) & in_row, 3 * STRIP + (col - end) * SIDE + row - HALO, -1))),
    )
    return jnp.where(y < FULL, strip, -1)


def exchange(far, one, two, by):
    def between(value, axes, first):
        size = lax.axis_size(axes)
        pairs = [(i, (i + 1) % size) for i in range(first, size, 2)]
        return lax.ppermute(value, axes, pairs + [(j, i) for i, j in pairs])

    beside = ("col", "core")
    return between(far, beside, 1), between(one, "face", 0), between(two, "face", 1), between(by, beside, 0)


def swap(value):
    return lax.ppermute(value, "core", [(0, 1), (1, 0)])


def on_device(
    obs_values, obs_tile, interp, tile_spin, w_embed, dw_kernel, norm_gain, w_one, w_two, cotangent
):
    tiles, chips = lax.axis_size(ALL), lax.axis_size(CHIPS)
    width, channels = w_embed.shape
    hidden = w_one.shape[1]
    slots = interp.shape[2]
    core, odd = lax.axis_index("core").reshape(1), (lax.axis_index("face") % 2).reshape(1)
    (leaving,) = call(
        route_kernel,
        [((tiles * 8, LANE), BF16)],
        [((1, obs_values.shape[0]), jnp.int32), (obs_values.shape, BF16)],
        60.5, core, odd, obs_tile.reshape(1, -1), obs_values, far=(2, 3), copies=2,
    )
    arrived = lax.all_to_all(leaving.reshape(tiles, 8, LANE), ALL, 0, 0, tiled=True)
    stacked = ((CELLS, tiles * slots), BF16)
    near = ((width + 80, channels), BF16)
    picks, places = ((4 * STRIP, CELLS), BF16), ((RING, CELLS), BF16)
    shelved, d_active = call(
        prepare_kernel,
        [((SHELF, channels), BF16), ((SHELF // 8, hidden), F32)],
        [
            (interp.shape[1:], BF16),
            (w_embed.shape, BF16),
            (dw_kernel.shape, BF16),
            ((channels // LANE, LANE), BF16),
            (w_two.shape, BF16),
            (cotangent.shape, BF16),
            ((CELLS, hidden), F32),
            stacked,
            picks,
            ((80, channels), F32),
            near,
            places,
        ],
        60.5, tile_spin.reshape(1), interp[0], w_embed, dw_kernel, norm_gain.reshape(-1, LANE), w_two, cotangent,
        far=(1, 2, 3, 4, 5, 6), far_outs=(0, 1), copies=10 + hidden // (2 * STEP),
    )
    gridded, embedded, nearby, place, *strips = call(
        embed_kernel,
        [((CELLS, width), BF16), ((CELLS, channels), BF16), near, places] + [((STRIP, width), BF16)] * 4,
        [((tiles * 8, LANE), F32), ((tiles * slots, width), BF16), stacked, picks, ((4 * STRIP, width), BF16)],
        16, core, odd, arrived.reshape(tiles * 8, LANE), shelved, far=(3,), copies=4,
    )
    strips = exchange(*strips)
    cells2 = ((ROWS2 * PITCH * 8, LANE), F32)
    kernel = ((TAPS * TAPS * 8, LANE), F32)
    blocks, cells = ((CELLS * 4, LANE), F32), ((CELLS, channels), F32)
    around = ((RING, channels), F32)
    step_sums = [((STEP, channels), F32), ((channels, STEP), F32)]
    field, conv, taps, d_active = call(
        inner_kernel, [cells2, blocks, kernel, ((CELLS, hidden), F32)], [], 20,
        embedded, nearby, d_active, far=(2,), copies=1,
    )
    field, normal, inverse, scaled, active, d_hidden, theirs = call(
        forward_kernel,
        [
            cells2,
            cells,
            ((CELLS, LANE), F32),
            ((CELLS, channels), BF16),
            ((CELLS, hidden), BF16),
            ((CELLS, hidden), BF16),
            ((CELLS, hidden + 2 * channels), BF16),
        ],
        [((4 * STRIP, width), BF16), around, blocks],
        20,
        core, odd, *strips, place, nearby, w_one, field, conv, taps, d_active, cotangent,
    )
    big = swap(theirs)

    mine, theirs = call(
        backward_kernel,
        [((chips, 16, LANE), F32), ((chips, 16, LANE), BF16)],
        [cells, blocks, cells2, cells, around, kernel, ((4 * STRIP, width), BF16), ((2 * chips * 16, LANE), F32)],
        20,
        core, odd, gridded, *strips, place, field, normal, inverse, d_hidden, w_one, nearby, taps, cotangent,
    )
    small = swap(theirs)
    whole = ((chips, 9, 16, LANE), BF16)
    (paired,) = call(
        pair_kernel, [whole], step_sums, 20, core, scaled, active, d_hidden, cotangent, big
    )
    (paired,) = call(
        join_kernel, [whole], [((chips, 16, LANE), BF16)], 4,
        mine, small, paired, far=(2,), far_outs=(0,), copies=1, aliases={2: 0},
    )
    paired = lax.all_to_all(paired, CHIPS, 0, 0, tiled=True)
    (summed,) = call(sum_kernel, [whole], [], 4, paired)
    here = lax.all_to_all(summed, CHIPS, 0, 0, tiled=True)
    there = swap(here)

    large = [((channels, hidden), F32), ((hidden, channels), F32)]
    steps = hidden // STEP // 2
    buffers = [((steps, channels, STEP), F32), ((steps, STEP, channels), F32)]
    *grads, output = call(
        first_kernel, large + [((CELLS, channels), BF16)], buffers + [((CELLS, channels), BF16)], 16,
        core, here, embedded, active, w_two, far_outs=(0, 1, 2), copies=2 * steps + 1,
    )
    count = TAPS * TAPS
    minor = [((width, channels), F32), ((count, channels), F32), ((1, channels), F32)]
    grad_one, grad_two, grad_embed, grad_kernel, grad_gain = call(
        second_kernel, large + minor,
        buffers + [((-(-(count + 1) * 4 // 16) * 16, LANE), F32)] + minor, 16,
        core, there, here, *grads,
        far=(3, 4), far_outs=range(5), copies=2 * steps + 3, aliases={3: 0, 4: 1},
    )
    return output, grad_embed, grad_kernel, grad_gain[0], grad_one, grad_two


def solution(mesh):
    faces, tiles = mesh.shape["face"], mesh.shape["tile"]
    fine = jax.sharding.Mesh(mesh.devices.reshape(faces, tiles // 2, 2), ALL)
    split = P(ALL, None)
    in_specs = (split, split, P(ALL, None, None, None), split) + (P(),) * 5 + (split,)
    return jax.shard_map(
        on_device, mesh=fine, in_specs=in_specs, out_specs=(split,) + (P(),) * 5, check_vma=False
    )
```

```python
import jax
import jax.numpy as jnp
from jax import lax
from jax.experimental import pallas as pl
from jax.experimental.pallas import tpu as pltpu
from jax.sharding import PartitionSpec as P

F32 = jnp.float32
BF16 = jnp.bfloat16
SIDE = 16
CELLS = SIDE * SIDE
HALO = 3
TAPS = 7
FULL = SIDE + 2 * HALO
PITCH = 24
HALF = SIDE // 2
LANE = 128
ROWS2 = HALF + TAPS - 1
STRIP = HALO * SIDE
SHELF = 65536
STEP = 256
ALL = ("face", "col", "core")
CHIPS = ("face", "col")
ROOT = 0.7978845608028654
CUBE = 0.044715

NN = (((1,), (0,)), ((), ()))
NT = (((1,), (1,)), ((), ()))
TN = (((0,), (0,)), ((), ()))


def dot(a, b, dims=NN):
    return lax.dot_general(a, b, dims, preferred_element_type=F32)


def call(kernel, outs, scratch, limit, *args, far=(), far_outs=(), copies=0, aliases=None):
    vmem, scalar = pl.BlockSpec(memory_space=pltpu.VMEM), pl.BlockSpec(memory_space=pltpu.SMEM)
    away = pl.BlockSpec(memory_space=pltpu.HBM)
    return pl.pallas_call(
        kernel,
        out_shape=[jax.ShapeDtypeStruct(s, d) for s, d in outs],
        in_specs=[
            scalar if a.shape == (1,) else away if k in far else vmem for k, a in enumerate(args)
        ],
        out_specs=[away if k in far_outs else vmem for k in range(len(outs))],
        scratch_shapes=[pltpu.VMEM(s, d) for s, d in scratch]
        + [pltpu.SemaphoreType.DMA((copies,))] * bool(copies),
        input_output_aliases=aliases or {},
        compiler_params=pltpu.CompilerParams(vmem_limit_bytes=int(limit * 2**20)),
    )(*args)


def start(sem, *pairs):
    moves = [pltpu.make_async_copy(a, b, sem.at[k]) for k, (a, b) in enumerate(pairs)]
    for move in moves:
        move.start()
    return moves


def strip_at(k):
    return pl.ds(pl.multiple_of(k * STRIP, 16), STRIP)


def take_strips(core, odd, refs, strips_ref):
    for ref, k in zip(refs, (2 + core, 1 - odd, odd, 3 - core)):
        strips_ref[strip_at(k), :] = ref[...]


def block(i, j, pitch):
    return pl.ds(pl.multiple_of((i * pitch + j) * 8, 8), 8)


def comb(i, j, pitch, h, cb):
    return pl.ds((i * pitch + j) * 8 + h * 4 + cb, 8, stride=8)


def route_kernel(core_ref, odd_ref, row_far, obs_far, out_ref, row_ref, obs_ref, sem):
    fetch_row, fetch_obs = start(sem, (row_far, row_ref), (obs_far, obs_ref))
    fetch_row.wait()
    row = row_ref[...]
    count = row.shape[1]
    across = jnp.broadcast_to(row, (count, count)).astype(F32)
    earlier = lax.broadcasted_iota(jnp.int32, (count, count), 0) < lax.broadcasted_iota(
        jnp.int32, (count, count), 1
    )
    same = jnp.where((across.T == across) & earlier, 1.0, 0.0)
    rank = jnp.sum(same, axis=0, keepdims=True).astype(jnp.int32)
    place = row * 8 + rank
    lines = out_ref.shape[0]
    line = lax.broadcasted_iota(jnp.int32, (lines, count), 0)
    chosen = jnp.where((line - (line & 4)) == place, 1.0, 0.0).astype(BF16)
    fetch_obs.wait()
    moved = dot(chosen, obs_ref[...])
    first = (lax.broadcasted_iota(jnp.int32, (lines, LANE), 0) & 4) == 0
    out_ref[...] = jnp.where(first, moved[:, :LANE], moved[:, LANE:]).astype(BF16)


OUTER = (0, 1, 2, 19, 20, 21)


def ring():
    at = 0
    for x in OUTER:
        for y in range(0, PITCH, 8):
            yield at, x, y
            at += 8
    for x in range(HALO, SIDE + HALO):
        for y in (0, PITCH - 8):
            yield at, x, y
            at += 8


RING = 8 * len(list(ring()))


def shelf(width, slots, channels):
    rows = (CELLS, 4 * STRIP, width + 80, RING)
    lanes = (slots, CELLS, channels, CELLS)
    ends = [sum(rows[: k + 1]) for k in range(len(rows))]
    return [(pl.ds(e - r, r), pl.ds(0, n)) for e, r, n in zip(ends, rows, lanes)]


def prepare_kernel(
    spin_ref, interp_far, w_embed_far, small_far, w_two_far, cot_far, shelf_far, d_act_far,
    interp_ref, w_two_ref, cot_ref, d_act_ref, weights_ref, pick_ref, near_ref, place_ref, sem,
):
    tiles, slots = interp_ref.shape[:2]
    width, channels = w_embed_far.shape
    spots = shelf(width, tiles * slots, channels)
    fetches = start(
        sem, (interp_far, interp_ref), (w_embed_far, near_ref.at[pl.ds(0, width)]),
        (small_far, near_ref.at[pl.ds(width, 80)]), (cot_far, cot_ref), (w_two_far, w_two_ref),
    )
    put_weights, put_pick, put_near, put_place = (
        pltpu.make_async_copy(a, shelf_far.at[spot], sem.at[5 + k])
        for k, (a, spot) in enumerate(zip((weights_ref, pick_ref, near_ref, place_ref), spots))
    )
    spin = spin_ref[0]
    q = lax.broadcasted_iota(jnp.int32, (1, CELLS), 1)
    by_row, by_col = leaving_strips(spin, q // SIDE, q % SIDE)
    k = lax.broadcasted_iota(jnp.int32, pick_ref.shape, 0)
    pick_ref[...] = jnp.where((k == by_row) | (k == by_col), 1.0, 0.0).astype(BF16)
    put_pick.start()
    fetches[0].wait()
    weights = interp_ref[...].astype(F32)
    for k in range(slots):
        weights_ref[:, k * tiles : (k + 1) * tiles] = weights[:, k, :].T.astype(BF16)
    put_weights.start()
    p = lax.broadcasted_iota(jnp.int32, (RING, 1), 0)
    outer = len(OUTER) * PITCH
    o, r = (p * 171) >> 12, p - outer
    x = jnp.where(p < outer, jnp.where(o < HALO, o, o + SIDE), HALO + (r >> 4))
    y = jnp.where(p < outer, p - o * PITCH, (r & 15) + (r & 8))
    strip = arriving_strips(spin, x, y)
    k = lax.broadcasted_iota(jnp.int32, place_ref.shape, 1)
    place_ref[...] = jnp.where(strip == k, 1.0, 0.0).astype(BF16)
    put_place.start()
    for fetch in fetches[1:3]:
        fetch.wait()
    put_near.start()
    for fetch in fetches[3:]:
        fetch.wait()
    puts = []
    for k in range(0, w_two_ref.shape[0], 2 * STEP):
        some = pl.ds(k, 2 * STEP)
        d_act_ref[:, some] = dot(cot_ref[...], w_two_ref[some, :], NT)
        target = d_act_far.at[pl.ds(0, CELLS), some]
        puts.append(pltpu.make_async_copy(d_act_ref.at[:, some], target, sem.at[9 + len(puts)]))
        puts[-1].start()
    for put in [put_pick, put_near, put_weights, put_place] + puts:
        put.wait()


def embed_kernel(
    core_ref, odd_ref, got_ref, shelf_far, grid_ref, emb_ref, near_ref, place_ref, far_ref, one_ref, two_ref, by_ref,
    wide_ref, rows_ref, weights_ref, pick_ref, strips_ref, sem,
):
    width, channels = near_ref.shape[0] - 80, near_ref.shape[1]
    spots = shelf(width, weights_ref.shape[1], channels)
    targets = (weights_ref, pick_ref, near_ref, place_ref)
    fetches = start(sem, *((shelf_far.at[spot], b) for spot, b in zip(spots, targets)))
    wide_ref[...] = got_ref[...].astype(F32)
    tiles = got_ref.shape[0] // 8
    for k in range(4):
        for half in range(2):
            for g in range(0, tiles, 16):
                two = [
                    wide_ref[pl.ds((g + e) * 8 + half * 4 + k, 8, stride=8), :] for e in (0, 8)
                ]
                rows_ref[pl.ds(k * tiles + g, 16), pl.ds(half * LANE, LANE)] = jnp.concatenate(
                    two, axis=0
                ).astype(BF16)
    for fetch in fetches:
        fetch.wait()
    gridded = dot(weights_ref[...], rows_ref[...]).astype(BF16)
    grid_ref[...] = gridded
    strips_ref[...] = dot(pick_ref[...], gridded).astype(BF16)
    core, odd = core_ref[0], odd_ref[0]
    for ref, k in ((far_ref, 3 - core), (one_ref, odd), (two_ref, 1 - odd), (by_ref, 2 + core)):
        ref[...] = strips_ref[strip_at(k), :]
    emb_ref[...] = dot(gridded, near_ref[0:width]).astype(BF16)


def tiles_of(part, two, one):
    for k in range(64):
        r, c = divmod(k, 4)
        yield part * 128 + k, two, pl.ds(r * 16, 16), pl.ds(c * LANE, LANE)
    for k in range(64):
        r, c = divmod(k, 2)
        yield part * 128 + 64 + k, one, pl.ds(r * 16, 16), pl.ds(c * LANE, LANE)


def inner_kernel(
    emb_ref, near_ref, d_act_far, field_ref, conv_ref, kern_ref, d_act_ref, sem
):
    width = near_ref.shape[0] - 80
    (fetch,) = start(sem, (d_act_far.at[pl.ds(0, CELLS), :], d_act_ref))
    taps = near_ref[width : width + 64].astype(F32)
    last = TAPS * TAPS - 1
    for h in range(2):
        for cb in range(4):
            lanes = slice(cb * LANE, (cb + 1) * LANE)
            for g in range(0, last, 8):
                kern_ref[pl.ds(g * 8 + h * 4 + cb, 8, stride=8), :] = taps[g : g + 8, lanes]
            kern_ref[pl.ds(last * 8 + h * 4 + cb, 1), :] = taps[last : last + 1, lanes]
    for i in range(SIDE):
        own = emb_ref[pl.ds(i * SIDE, SIDE), :].astype(F32)
        x = i + HALO
        for g in range(0, SIDE, 8):
            for cb in range(4):
                value = own[g : g + 8, cb * LANE : (cb + 1) * LANE]
                if x < ROWS2:
                    field_ref[comb(x, HALO + g, PITCH, 0, cb), :] = value
                if x >= HALF:
                    field_ref[comb(x - HALF, HALO + g, PITCH, 1, cb), :] = value
    for i in range(HALF):
        sums = [jnp.zeros((8, LANE), F32)] * SIDE
        for x in range(max(i, HALO), min(i + TAPS, HALF + HALO)):
            taps = [kern_ref[block(x - i, b, TAPS), :] for b in range(TAPS)]
            for y in range(HALO, SIDE + HALO):
                here = field_ref[block(x, y, PITCH), :]
                for b in range(TAPS):
                    if 0 <= y - b < SIDE:
                        sums[y - b] = sums[y - b] + here * taps[b]
        for j in range(SIDE):
            conv_ref[block(i, j, SIDE), :] = sums[j]
    fetch.wait()


def forward_kernel(
    core_ref, odd_ref, s0, s1, s2, s3, place_ref, near_ref, w_one_ref, own_ref, part_ref, kern_ref, d_act_ref, cot_ref,
    field_ref, normal_ref, inv_ref, scaled_ref, active_ref, d_hid_ref, theirs_ref,
    strips_ref, ring_ref, conv_ref,
):
    width, channels = near_ref.shape[0] - 80, near_ref.shape[1]
    take_strips(core_ref[0], odd_ref[0], (s0, s1, s2, s3), strips_ref)
    halo = dot(strips_ref[...], near_ref[0:width]).astype(BF16)
    ring_ref[...] = dot(place_ref[:, : 4 * STRIP], halo)
    field_ref[...] = own_ref[...]
    for at, x, y in ring():
        skip, count = (0, 8) if x in OUTER else (0, HALO) if y == 0 else (HALO, HALO)
        for cb in range(4):
            value = ring_ref[pl.ds(at + skip, count), pl.ds(cb * LANE, LANE)]
            if x < ROWS2:
                field_ref[pl.ds((x * PITCH + y + skip) * 8 + cb, count, stride=8), :] = value
            if x >= HALF:
                row = ((x - HALF) * PITCH + y + skip) * 8 + 4 + cb
                field_ref[pl.ds(row, count, stride=8), :] = value

    for i in range(HALF):
        sums = [part_ref[block(i, j, SIDE), :] for j in range(SIDE)]
        for a in range(TAPS):
            x = i + a
            whole = x < HALO or x >= HALF + HALO
            taps = [kern_ref[block(a, b, TAPS), :] for b in range(TAPS)]
            for y in range(FULL):
                if whole or y < HALO or y >= SIDE + HALO:
                    here = field_ref[block(x, y, PITCH), :]
                    for b in range(TAPS):
                        if 0 <= y - b < SIDE:
                            sums[y - b] = sums[y - b] + here * taps[b]
        for j in range(SIDE):
            conv_ref[block(i, j, SIDE), :] = sums[j]

    gain = near_ref[width + 64 :].astype(F32)
    for r in range(SIDE):
        h, i = divmod(r, HALF)
        parts = [
            jnp.concatenate([conv_ref[comb(i, 8 * g, SIDE, h, cb), :] for g in range(2)], axis=0)
            for cb in range(4)
        ]
        value = jnp.concatenate(parts, axis=1)
        centred = value - jnp.mean(value, axis=1, keepdims=True)
        inverse = lax.rsqrt(jnp.mean(centred * centred, axis=1, keepdims=True) + 1e-06)
        normal = centred * inverse
        rows = pl.ds(r * SIDE, SIDE)
        normal_ref[rows, :] = normal
        inv_ref[rows, :] = jnp.broadcast_to(inverse, (SIDE, LANE))
        scaled_ref[rows, :] = (normal * gain).astype(BF16)

    for k in range(w_one_ref.shape[1] // STEP):
        some = pl.ds(k * STEP, STEP)
        pre = dot(scaled_ref[...], w_one_ref[:, some])
        cubic = (ROOT * CUBE) * (pre * pre)
        upper = 0.5 + 0.5 * jnp.tanh(pre * (ROOT + cubic))
        active = pre * upper
        slope = upper + active * (1.0 - upper) * (2.0 * ROOT + 6.0 * cubic)
        active_ref[:, some] = active.astype(BF16)
        d_hid_ref[:, some] = (d_act_ref[:, some] * slope).astype(BF16)

    half = w_one_ref.shape[1] // 2
    away = pl.ds(pl.multiple_of((1 - core_ref[0]) * half, half), half)
    theirs_ref[:, 0:half] = active_ref[:, away]
    theirs_ref[:, half : 2 * half] = d_hid_ref[:, away]
    theirs_ref[:, 2 * half : 2 * half + channels] = scaled_ref[...]
    theirs_ref[:, 2 * half + channels :] = cot_ref[...]


def backward_kernel(
    core_ref, odd_ref, grid_ref, s0, s1, s2, s3, place_ref, field_ref, normal_ref, inv_ref, d_hid_ref, w_one_ref,
    near_ref, kern_ref, cot_ref,
    mine_ref, theirs_ref,
    d_scaled_ref, d_conv_ref, spread_ref, own_ref, ring_ref, taps_ref, strips_ref, small_ref,
):
    d_scaled_ref[...] = dot(d_hid_ref[...], w_one_ref[...], NT)
    total = jnp.zeros((SIDE, normal_ref.shape[1]), F32)
    gain = near_ref[near_ref.shape[0] - 16 :].astype(F32)
    for r in range(SIDE):
        h, i = divmod(r, HALF)
        rows = pl.ds(r * SIDE, SIDE)
        normal, d_scaled = normal_ref[rows, :], d_scaled_ref[rows, :]
        total = total + d_scaled * normal
        d_normal = d_scaled * gain
        mean = jnp.mean(d_normal, axis=1, keepdims=True)
        along = jnp.mean(d_normal * normal, axis=1, keepdims=True)
        d_conv = (d_normal - mean - normal * along) * inv_ref[rows, 0:1]
        for g in range(2):
            for cb in range(4):
                d_conv_ref[comb(i, 8 * g, SIDE, h, cb), :] = d_conv[
                    8 * g : 8 * g + 8, cb * LANE : (cb + 1) * LANE
                ]
    grad_gain = jnp.sum(total, axis=0, keepdims=True)

    spread_ref[...] = jnp.zeros_like(spread_ref)
    taps_ref[...] = jnp.zeros_like(taps_ref)

    def conv_row(i, carry):
        d_conv = [d_conv_ref[block(i, j, SIDE), :] for j in range(SIDE)]
        for a in range(TAPS):
            taps = [kern_ref[block(a, b, TAPS), :] for b in range(TAPS)]
            sums = [taps_ref[block(a, b, TAPS), :] for b in range(TAPS)]
            for y in range(FULL):
                here = field_ref[block(i + a, y, PITCH), :]
                value = spread_ref[block(i + a, y, PITCH), :]
                for b in range(TAPS):
                    if 0 <= y - b < SIDE:
                        value = value + d_conv[y - b] * taps[b]
                        sums[b] = sums[b] + here * d_conv[y - b]
                spread_ref[block(i + a, y, PITCH), :] = value
            for b in range(TAPS):
                taps_ref[block(a, b, TAPS), :] = sums[b]
        return carry

    lax.fori_loop(0, HALF, conv_row, 0)

    def part(x, y, cb):
        value = None
        if x < ROWS2:
            value = spread_ref[comb(x, y, PITCH, 0, cb), :]
        if x >= HALF:
            more = spread_ref[comb(x - HALF, y, PITCH, 1, cb), :]
            value = more if value is None else value + more
        return value

    for cb in range(4):
        lanes = pl.ds(cb * LANE, LANE)
        for at, x, y in ring():
            ring_ref[pl.ds(at, 8), lanes] = part(x, y, cb)
        for i in range(SIDE):
            for g in range(0, SIDE, 8):
                own_ref[pl.ds(i * SIDE + g, 8), lanes] = part(i + HALO, g + HALO, cb)
    take_strips(core_ref[0], odd_ref[0], (s0, s1, s2, s3), strips_ref)
    d_halo = dot(place_ref[:, : 4 * STRIP], ring_ref[...].astype(BF16), TN).astype(BF16)
    d_own = (own_ref[...] + cot_ref[...].astype(F32)).astype(BF16)
    grad_embed = dot(grid_ref[...], d_own, TN) + dot(strips_ref[...], d_halo, TN)

    half = mine_ref.shape[0]
    small_ref[...] = jnp.zeros_like(small_ref)
    for t in range(half):
        r, c = divmod(t, 4)
        small_ref[t * 16 : (t + 1) * 16] = grad_embed[r * 16 : (r + 1) * 16, c * LANE : (c + 1) * LANE]
    base = half * 16
    for t in range(TAPS * TAPS):
        both = taps_ref[t * 8 : (t + 1) * 8, :]
        small_ref[base + t * 4 : base + (t + 1) * 4] = both[:4] + both[4:]
    for c in range(4):
        at = base + TAPS * TAPS * 4 + c
        small_ref[at : at + 1] = grad_gain[:, c * LANE : (c + 1) * LANE]
    core = core_ref[0]
    for t in range(half):
        mine_ref[t] = small_ref[pl.ds(pl.multiple_of((core * half + t) * 16, 16), 16), :]
        theirs_ref[t] = small_ref[
            pl.ds(pl.multiple_of(((1 - core) * half + t) * 16, 16), 16), :
        ].astype(BF16)


def pair_kernel(core_ref, scaled_ref, active_ref, d_hid_ref, cot_ref, their_ref, out_ref, two_ref, one_ref):
    half, channels = active_ref.shape[1] // 2, cot_ref.shape[1]
    their_scaled = their_ref[:, 2 * half : 2 * half + channels]
    their_cot = their_ref[:, 2 * half + channels :]
    mine = pl.ds(pl.multiple_of(core_ref[0] * half, half), half)
    one_ref[...] = dot(scaled_ref[...], d_hid_ref[:, mine], TN) + dot(
        their_scaled, their_ref[:, half : 2 * half], TN
    )
    for k in range(half // STEP):
        some = pl.ds(pl.multiple_of(core_ref[0] * half + k * STEP, STEP), STEP)
        two_ref[...] = dot(active_ref[:, some], cot_ref[...], TN) + dot(
            their_ref[:, k * STEP : (k + 1) * STEP], their_cot, TN
        )
        for t, ref, rows, lanes in tiles_of(k, two_ref, one_ref.at[:, k * STEP : (k + 1) * STEP]):
            out_ref[t // 8, t % 8] = ref[rows, lanes].astype(BF16)


def join_kernel(mine_ref, small_ref, paired_far, out_far, tile_ref, sem):
    tile_ref[...] = (mine_ref[...] + small_ref[...].astype(F32)).astype(BF16)
    put = pltpu.make_async_copy(tile_ref, out_far.at[:, 8], sem.at[0])
    put.start()
    put.wait()


def sum_kernel(in_ref, out_ref):
    parts, tiles = in_ref.shape[:2]

    def add(d, sums):
        return [s + in_ref[d, t].astype(F32) for t, s in enumerate(sums)]

    sums = lax.fori_loop(0, parts, add, [jnp.zeros(in_ref.shape[2:], F32)] * tiles, unroll=4)
    sums = [s.astype(BF16) for s in sums]

    def spread(d, carry):
        for t in range(tiles):
            out_ref[d, t] = sums[t]
        return carry

    lax.fori_loop(0, parts, spread, 0, unroll=4)


def assemble_half(core, in_ref, one_far, two_far, one_ref, two_ref, sem):
    steps = one_ref.shape[0]
    puts = []
    for k in range(steps):
        for t, ref, rows, lanes in tiles_of(k, two_ref, one_ref):
            ref[k, rows, lanes] = in_ref[t // 8, t % 8].astype(F32)
        some = pl.ds(pl.multiple_of((core * steps + k) * STEP, STEP), STEP)
        puts += [
            pltpu.make_async_copy(one_ref.at[k], one_far.at[:, some], sem.at[2 * k]),
            pltpu.make_async_copy(two_ref.at[k], two_far.at[some, :], sem.at[2 * k + 1]),
        ]
        puts[-2].start()
        puts[-1].start()
    return puts


def first_kernel(
    core_ref, in_ref, emb_ref, active_ref, w_two_ref,
    one_far, two_far, feature_far, one_ref, two_ref, feature_ref, sem,
):
    puts = assemble_half(core_ref[0], in_ref, one_far, two_far, one_ref, two_ref, sem)
    feature_ref[...] = (emb_ref[...].astype(F32) + dot(active_ref[...], w_two_ref[...])).astype(BF16)
    puts.append(pltpu.make_async_copy(feature_ref, feature_far, sem.at[len(puts)]))
    puts[-1].start()
    for put in puts:
        put.wait()


def second_kernel(
    core_ref, in_ref, mine_ref, one_old, two_old,
    one_far, two_far, embed_far, taps_far, gain_far,
    one_ref, two_ref, rows_ref, embed_ref, taps_ref, gain_ref, sem,
):
    core = core_ref[0]
    count = taps_ref.shape[0]

    def place(first, last):
        for t in range(in_ref.shape[0]):
            r, c = divmod(t, 4)
            embed_ref[r * 16 : (r + 1) * 16, c * LANE : (c + 1) * LANE] = first[t, 8].astype(F32)
        for t in range(rows_ref.shape[0] // 16):
            rows_ref[t * 16 : (t + 1) * 16, :] = last[t, 8].astype(F32)

    @pl.when(core == 0)
    def _():
        place(mine_ref, in_ref)

    @pl.when(core == 1)
    def _():
        place(in_ref, mine_ref)

    for cb in range(4):
        lanes = pl.ds(cb * LANE, LANE)
        for g in range(0, count - 1, 8):
            taps_ref[pl.ds(g, 8), lanes] = rows_ref[pl.ds(g * 4 + cb, 8, stride=4), :]
        taps_ref[pl.ds(count - 1, 1), lanes] = rows_ref[pl.ds((count - 1) * 4 + cb, 1), :]
        gain_ref[:, lanes] = rows_ref[pl.ds(count * 4 + cb, 1), :]
    base = 2 * one_ref.shape[0]
    puts = []
    for k, pair in enumerate(((embed_ref, embed_far), (taps_ref, taps_far), (gain_ref, gain_far))):
        puts.append(pltpu.make_async_copy(*pair, sem.at[base + k]))
        puts[-1].start()
    puts += assemble_half(1 - core, in_ref, one_far, two_far, one_ref, two_ref, sem)
    for put in puts:
        put.wait()


def turned(spin, x, y, last):
    row = jnp.where(spin == 0, x, jnp.where(spin == 1, last - y, jnp.where(spin == 2, last - x, y)))
    col = jnp.where(spin == 0, y, jnp.where(spin == 1, x, jnp.where(spin == 2, last - y, last - x)))
    return row, col


def leaving_strips(spin, x, y):
    row, col = turned(spin, x, y, SIDE - 1)
    cut = SIDE - HALO
    by_row = jnp.where(row >= cut, (row - cut) * SIDE + col, jnp.where(row < HALO, STRIP + row * SIDE + col, -1))
    by_col = jnp.where(col >= cut, 2 * STRIP + (col - cut) * SIDE + row, jnp.where(col < HALO, 3 * STRIP + col * SIDE + row, -1))
    return by_row, by_col


def arriving_strips(spin, x, y):
    row, col = turned(spin, x, y, FULL - 1)
    end = SIDE + HALO
    in_row, in_col = (row >= HALO) & (row < end), (col >= HALO) & (col < end)
    strip = jnp.where(
        (row < HALO) & in_col, row * SIDE + col - HALO,
        jnp.where((row >= end) & in_col, STRIP + (row - end) * SIDE + col - HALO,
        jnp.where((col < HALO) & in_row, 2 * STRIP + col * SIDE + row - HALO,
        jnp.where((col >= end) & in_row, 3 * STRIP + (col - end) * SIDE + row - HALO, -1))),
    )
    return jnp.where(y < FULL, strip, -1)


def exchange(far, one, two, by):
    def between(value, axes, first):
        size = lax.axis_size(axes)
        pairs = [(i, (i + 1) % size) for i in range(first, size, 2)]
        return lax.ppermute(value, axes, pairs + [(j, i) for i, j in pairs])

    beside = ("col", "core")
    return between(far, beside, 1), between(one, "face", 0), between(two, "face", 1), between(by, beside, 0)


def swap(value):
    return lax.ppermute(value, "core", [(0, 1), (1, 0)])


def on_device(
    obs_values, obs_tile, interp, tile_spin, w_embed, dw_kernel, norm_gain, w_one, w_two, cotangent
):
    tiles, chips = lax.axis_size(ALL), lax.axis_size(CHIPS)
    width, channels = w_embed.shape
    hidden = w_one.shape[1]
    slots = interp.shape[2]
    core, odd = lax.axis_index("core").reshape(1), (lax.axis_index("face") % 2).reshape(1)
    (leaving,) = call(
        route_kernel,
        [((tiles * 8, LANE), BF16)],
        [((1, obs_values.shape[0]), jnp.int32), (obs_values.shape, BF16)],
        60.5, core, odd, obs_tile.reshape(1, -1), obs_values, far=(2, 3), copies=2,
    )
    arrived = lax.all_to_all(leaving.reshape(tiles, 8, LANE), ALL, 0, 0, tiled=True)
    stacked = ((CELLS, tiles * slots), BF16)
    near = ((width + 80, channels), BF16)
    taps_gain = jnp.concatenate(
        [dw_kernel, jnp.zeros((64 - TAPS * TAPS, channels), BF16), jnp.broadcast_to(norm_gain, (16, channels))]
    )
    picks, places = ((4 * STRIP, CELLS), BF16), ((RING, CELLS), BF16)
    shelved, d_active = call(
        prepare_kernel,
        [((SHELF, channels), BF16), ((SHELF // 8, hidden), F32)],
        [
            (interp.shape[1:], BF16),
            (w_two.shape, BF16),
            (cotangent.shape, BF16),
            ((CELLS, hidden), F32),
            stacked,
            picks,
            near,
            places,
        ],
        60.5, tile_spin.reshape(1), interp[0], w_embed, taps_gain, w_two, cotangent,
        far=(1, 2, 3, 4, 5), far_outs=(0, 1), copies=9 + hidden // (2 * STEP),
    )
    gridded, embedded, nearby, place, *strips = call(
        embed_kernel,
        [((CELLS, width), BF16), ((CELLS, channels), BF16), near, places] + [((STRIP, width), BF16)] * 4,
        [((tiles * 8, LANE), F32), ((tiles * slots, width), BF16), stacked, picks, ((4 * STRIP, width), BF16)],
        16, core, odd, arrived.reshape(tiles * 8, LANE), shelved, far=(3,), copies=4,
    )
    strips = exchange(*strips)
    cells2 = ((ROWS2 * PITCH * 8, LANE), F32)
    kernel = ((TAPS * TAPS * 8, LANE), F32)
    blocks, cells = ((CELLS * 4, LANE), F32), ((CELLS, channels), F32)
    around = ((RING, channels), F32)
    step_sums = [((STEP, channels), F32), ((channels, hidden // 2), F32)]
    field, conv, taps, d_active = call(
        inner_kernel, [cells2, blocks, kernel, ((CELLS, hidden), F32)], [], 20,
        embedded, nearby, d_active, far=(2,), copies=1,
    )
    field, normal, inverse, scaled, active, d_hidden, theirs = call(
        forward_kernel,
        [
            cells2,
            cells,
            ((CELLS, LANE), F32),
            ((CELLS, channels), BF16),
            ((CELLS, hidden), BF16),
            ((CELLS, hidden), BF16),
            ((CELLS, hidden + 2 * channels), BF16),
        ],
        [((4 * STRIP, width), BF16), around, blocks],
        20,
        core, odd, *strips, place, nearby, w_one, field, conv, taps, d_active, cotangent,
    )
    big = swap(theirs)

    mine, theirs = call(
        backward_kernel,
        [((chips, 16, LANE), F32), ((chips, 16, LANE), BF16)],
        [cells, blocks, cells2, cells, around, kernel, ((4 * STRIP, width), BF16), ((2 * chips * 16, LANE), F32)],
        20,
        core, odd, gridded, *strips, place, field, normal, inverse, d_hidden, w_one, nearby, taps, cotangent,
    )
    small = swap(theirs)
    whole = ((chips, 9, 16, LANE), BF16)
    (paired,) = call(
        pair_kernel, [whole], step_sums, 20, core, scaled, active, d_hidden, cotangent, big
    )
    (paired,) = call(
        join_kernel, [whole], [((chips, 16, LANE), BF16)], 4,
        mine, small, paired, far=(2,), far_outs=(0,), copies=1, aliases={2: 0},
    )
    paired = lax.all_to_all(paired, CHIPS, 0, 0, tiled=True)
    (summed,) = call(sum_kernel, [whole], [], 4, paired)
    here = lax.all_to_all(summed, CHIPS, 0, 0, tiled=True)
    there = swap(here)

    large = [((channels, hidden), F32), ((hidden, channels), F32)]
    steps = hidden // STEP // 2
    buffers = [((steps, channels, STEP), F32), ((steps, STEP, channels), F32)]
    *grads, output = call(
        first_kernel, large + [((CELLS, channels), BF16)], buffers + [((CELLS, channels), BF16)], 16,
        core, here, embedded, active, w_two, far_outs=(0, 1, 2), copies=2 * steps + 1,
    )
    count = TAPS * TAPS
    minor = [((width, channels), F32), ((count, channels), F32), ((1, channels), F32)]
    grad_one, grad_two, grad_embed, grad_kernel, grad_gain = call(
        second_kernel, large + minor,
        buffers + [((-(-(count + 1) * 4 // 16) * 16, LANE), F32)] + minor, 16,
        core, there, here, *grads,
        far=(3, 4), far_outs=range(5), copies=2 * steps + 3, aliases={3: 0, 4: 1},
    )
    return output, grad_embed, grad_kernel, grad_gain[0], grad_one, grad_two


def solution(mesh):
    faces, tiles = mesh.shape["face"], mesh.shape["tile"]
    fine = jax.sharding.Mesh(mesh.devices.reshape(faces, tiles // 2, 2), ALL)
    split = P(ALL, None)
    in_specs = (split, split, P(ALL, None, None, None), split) + (P(),) * 5 + (split,)
    return jax.shard_map(
        on_device, mesh=fine, in_specs=in_specs, out_specs=(split,) + (P(),) * 5, check_vma=False
    )
```

```python
import jax
import jax.numpy as jnp
from jax import lax
from jax.experimental import pallas as pl
from jax.experimental.pallas import tpu as pltpu
from jax.sharding import PartitionSpec as P

F32 = jnp.float32
BF16 = jnp.bfloat16
SIDE = 16
CELLS = SIDE * SIDE
HALO = 3
TAPS = 7
FULL = SIDE + 2 * HALO
PITCH = 24
HALF = SIDE // 2
LANE = 128
ROWS2 = HALF + TAPS - 1
STRIP = HALO * SIDE
SHELF = 65536
STEP = 256
ALL = ("face", "col", "core")
CHIPS = ("face", "col")
ROOT = 0.7978845608028654
CUBE = 0.044715

NN = (((1,), (0,)), ((), ()))
NT = (((1,), (1,)), ((), ()))
TN = (((0,), (0,)), ((), ()))


def dot(a, b, dims=NN):
    return lax.dot_general(a, b, dims, preferred_element_type=F32)


def call(kernel, outs, scratch, limit, *args, far=(), far_outs=(), copies=0, aliases=None):
    vmem, scalar = pl.BlockSpec(memory_space=pltpu.VMEM), pl.BlockSpec(memory_space=pltpu.SMEM)
    away = pl.BlockSpec(memory_space=pltpu.HBM)
    return pl.pallas_call(
        kernel,
        out_shape=[jax.ShapeDtypeStruct(s, d) for s, d in outs],
        in_specs=[
            scalar if a.shape == (1,) else away if k in far else vmem for k, a in enumerate(args)
        ],
        out_specs=[away if k in far_outs else vmem for k in range(len(outs))],
        scratch_shapes=[pltpu.VMEM(s, d) for s, d in scratch]
        + [pltpu.SemaphoreType.DMA((copies,))] * bool(copies),
        input_output_aliases=aliases or {},
        compiler_params=pltpu.CompilerParams(vmem_limit_bytes=int(limit * 2**20)),
    )(*args)


def start(sem, *pairs):
    moves = [pltpu.make_async_copy(a, b, sem.at[k]) for k, (a, b) in enumerate(pairs)]
    for move in moves:
        move.start()
    return moves


def strip_at(k):
    return pl.ds(pl.multiple_of(k * STRIP, 16), STRIP)


def take_strips(core, odd, refs, strips_ref):
    for ref, k in zip(refs, (2 + core, 1 - odd, odd, 3 - core)):
        strips_ref[strip_at(k), :] = ref[...]


def block(i, j, pitch):
    return pl.ds(pl.multiple_of((i * pitch + j) * 8, 8), 8)


def comb(i, j, pitch, h, cb):
    return pl.ds((i * pitch + j) * 8 + h * 4 + cb, 8, stride=8)


def route_kernel(core_ref, odd_ref, row_far, obs_far, out_ref, row_ref, obs_ref, sem):
    fetch_row, fetch_obs = start(sem, (row_far, row_ref), (obs_far, obs_ref))
    fetch_row.wait()
    row = row_ref[...]
    count = row.shape[1]
    across = jnp.broadcast_to(row, (count, count)).astype(F32)
    earlier = lax.broadcasted_iota(jnp.int32, (count, count), 0) < lax.broadcasted_iota(
        jnp.int32, (count, count), 1
    )
    same = jnp.where((across.T == across) & earlier, 1.0, 0.0)
    rank = jnp.sum(same, axis=0, keepdims=True).astype(jnp.int32)
    place = row * 8 + rank
    lines = out_ref.shape[0]
    line = lax.broadcasted_iota(jnp.int32, (lines, count), 0)
    chosen = jnp.where((line - (line & 4)) == place, 1.0, 0.0).astype(BF16)
    fetch_obs.wait()
    moved = dot(chosen, obs_ref[...])
    first = (lax.broadcasted_iota(jnp.int32, (lines, LANE), 0) & 4) == 0
    out_ref[...] = jnp.where(first, moved[:, :LANE], moved[:, LANE:]).astype(BF16)


OUTER = (0, 1, 2, 19, 20, 21)


def ring():
    at = 0
    for x in OUTER:
        for y in range(0, PITCH, 8):
            yield at, x, y
            at += 8
    for x in range(HALO, SIDE + HALO):
        for y in (0, PITCH - 8):
            yield at, x, y
            at += 8


RING = 8 * len(list(ring()))


def shelf(width, slots, channels):
    rows = (CELLS, 4 * STRIP, width + 80, RING)
    lanes = (slots, CELLS, channels, CELLS)
    ends = [sum(rows[: k + 1]) for k in range(len(rows))]
    return [(pl.ds(e - r, r), pl.ds(0, n)) for e, r, n in zip(ends, rows, lanes)]


def prepare_kernel(
    spin_ref, interp_far, w_embed_far, small_far, w_two_far, cot_far, shelf_far, d_act_far,
    interp_ref, w_two_ref, cot_ref, d_act_ref, weights_ref, pick_ref, near_ref, place_ref, sem,
):
    tiles, slots = interp_ref.shape[:2]
    width, channels = w_embed_far.shape
    spots = shelf(width, tiles * slots, channels)
    fetches = start(
        sem, (interp_far, interp_ref), (w_embed_far, near_ref.at[pl.ds(0, width)]),
        (small_far, near_ref.at[pl.ds(width, 80)]), (cot_far, cot_ref), (w_two_far, w_two_ref),
    )
    put_weights, put_pick, put_near, put_place = (
        pltpu.make_async_copy(a, shelf_far.at[spot], sem.at[5 + k])
        for k, (a, spot) in enumerate(zip((weights_ref, pick_ref, near_ref, place_ref), spots))
    )
    spin = spin_ref[0]
    q = lax.broadcasted_iota(jnp.int32, (1, CELLS), 1)
    by_row, by_col = leaving_strips(spin, q // SIDE, q % SIDE)
    k = lax.broadcasted_iota(jnp.int32, pick_ref.shape, 0)
    pick_ref[...] = jnp.where((k == by_row) | (k == by_col), 1.0, 0.0).astype(BF16)
    put_pick.start()
    fetches[0].wait()
    weights = interp_ref[...].astype(F32)
    for k in range(slots):
        weights_ref[:, k * tiles : (k + 1) * tiles] = weights[:, k, :].T.astype(BF16)
    put_weights.start()
    p = lax.broadcasted_iota(jnp.int32, (RING, 1), 0)
    outer = len(OUTER) * PITCH
    o, r = (p * 171) >> 12, p - outer
    x = jnp.where(p < outer, jnp.where(o < HALO, o, o + SIDE), HALO + (r >> 4))
    y = jnp.where(p < outer, p - o * PITCH, (r & 15) + (r & 8))
    strip = arriving_strips(spin, x, y)
    k = lax.broadcasted_iota(jnp.int32, place_ref.shape, 1)
    place_ref[...] = jnp.where(strip == k, 1.0, 0.0).astype(BF16)
    put_place.start()
    for fetch in fetches[1:3]:
        fetch.wait()
    put_near.start()
    for fetch in fetches[3:]:
        fetch.wait()
    puts = []
    for k in range(0, w_two_ref.shape[0], 2 * STEP):
        some = pl.ds(k, 2 * STEP)
        d_act_ref[:, some] = dot(cot_ref[...], w_two_ref[some, :], NT)
        target = d_act_far.at[pl.ds(0, CELLS), some]
        puts.append(pltpu.make_async_copy(d_act_ref.at[:, some], target, sem.at[9 + len(puts)]))
        puts[-1].start()
    for put in [put_pick, put_near, put_weights, put_place] + puts:
        put.wait()


def embed_kernel(
    core_ref, odd_ref, got_ref, shelf_far, grid_ref, near_ref, place_ref, far_ref, one_ref, two_ref, by_ref,
    wide_ref, rows_ref, weights_ref, pick_ref, strips_ref, sem,
):
    width, channels = near_ref.shape[0] - 80, near_ref.shape[1]
    spots = shelf(width, weights_ref.shape[1], channels)
    targets = (weights_ref, pick_ref, near_ref, place_ref)
    fetches = start(sem, *((shelf_far.at[spot], b) for spot, b in zip(spots, targets)))
    wide_ref[...] = got_ref[...].astype(F32)
    tiles = got_ref.shape[0] // 8
    for k in range(4):
        for half in range(2):
            for g in range(0, tiles, 16):
                two = [
                    wide_ref[pl.ds((g + e) * 8 + half * 4 + k, 8, stride=8), :] for e in (0, 8)
                ]
                rows_ref[pl.ds(k * tiles + g, 16), pl.ds(half * LANE, LANE)] = jnp.concatenate(
                    two, axis=0
                ).astype(BF16)
    fetches[0].wait()
    gridded = dot(weights_ref[...], rows_ref[...]).astype(BF16)
    grid_ref[...] = gridded
    fetches[1].wait()
    strips_ref[...] = dot(pick_ref[...], gridded).astype(BF16)
    core, odd = core_ref[0], odd_ref[0]
    for ref, k in ((far_ref, 3 - core), (one_ref, odd), (two_ref, 1 - odd), (by_ref, 2 + core)):
        ref[...] = strips_ref[strip_at(k), :]
    for fetch in fetches[2:]:
        fetch.wait()


def tiles_of(part, two, one):
    for k in range(64):
        r, c = divmod(k, 4)
        yield part * 128 + k, two, pl.ds(r * 16, 16), pl.ds(c * LANE, LANE)
    for k in range(64):
        r, c = divmod(k, 2)
        yield part * 128 + 64 + k, one, pl.ds(r * 16, 16), pl.ds(c * LANE, LANE)


def inner_kernel(
    grid_ref, near_ref, d_act_far, emb_ref, field_ref, conv_ref, kern_ref, d_act_ref, sem
):
    width = near_ref.shape[0] - 80
    (fetch,) = start(sem, (d_act_far.at[pl.ds(0, CELLS), :], d_act_ref))
    emb_ref[...] = dot(grid_ref[...], near_ref[0:width]).astype(BF16)
    taps = near_ref[width : width + 64].astype(F32)
    last = TAPS * TAPS - 1
    for h in range(2):
        for cb in range(4):
            lanes = slice(cb * LANE, (cb + 1) * LANE)
            for g in range(0, last, 8):
                kern_ref[pl.ds(g * 8 + h * 4 + cb, 8, stride=8), :] = taps[g : g + 8, lanes]
            kern_ref[pl.ds(last * 8 + h * 4 + cb, 1), :] = taps[last : last + 1, lanes]
    for i in range(SIDE):
        own = emb_ref[pl.ds(i * SIDE, SIDE), :].astype(F32)
        x = i + HALO
        for g in range(0, SIDE, 8):
            for cb in range(4):
                value = own[g : g + 8, cb * LANE : (cb + 1) * LANE]
                if x < ROWS2:
                    field_ref[comb(x, HALO + g, PITCH, 0, cb), :] = value
                if x >= HALF:
                    field_ref[comb(x - HALF, HALO + g, PITCH, 1, cb), :] = value
    for i in range(HALF):
        sums = [jnp.zeros((8, LANE), F32)] * SIDE
        for x in range(max(i, HALO), min(i + TAPS, HALF + HALO)):
            taps = [kern_ref[block(x - i, b, TAPS), :] for b in range(TAPS)]
            for y in range(HALO, SIDE + HALO):
                here = field_ref[block(x, y, PITCH), :]
                for b in range(TAPS):
                    if 0 <= y - b < SIDE:
                        sums[y - b] = sums[y - b] + here * taps[b]
        for j in range(SIDE):
            conv_ref[block(i, j, SIDE), :] = sums[j]
    fetch.wait()


def forward_kernel(
    core_ref, odd_ref, s0, s1, s2, s3, place_ref, near_ref, w_one_ref, own_ref, part_ref, kern_ref, d_act_ref, cot_ref,
    field_ref, normal_ref, inv_ref, scaled_ref, active_ref, d_hid_ref, theirs_ref,
    strips_ref, ring_ref, conv_ref,
):
    width, channels = near_ref.shape[0] - 80, near_ref.shape[1]
    take_strips(core_ref[0], odd_ref[0], (s0, s1, s2, s3), strips_ref)
    halo = dot(strips_ref[...], near_ref[0:width]).astype(BF16)
    ring_ref[...] = dot(place_ref[:, : 4 * STRIP], halo)
    field_ref[...] = own_ref[...]
    for at, x, y in ring():
        skip, count = (0, 8) if x in OUTER else (0, HALO) if y == 0 else (HALO, HALO)
        for cb in range(4):
            value = ring_ref[pl.ds(at + skip, count), pl.ds(cb * LANE, LANE)]
            if x < ROWS2:
                field_ref[pl.ds((x * PITCH + y + skip) * 8 + cb, count, stride=8), :] = value
            if x >= HALF:
                row = ((x - HALF) * PITCH + y + skip) * 8 + 4 + cb
                field_ref[pl.ds(row, count, stride=8), :] = value

    for i in range(HALF):
        sums = [part_ref[block(i, j, SIDE), :] for j in range(SIDE)]
        for a in range(TAPS):
            x = i + a
            whole = x < HALO or x >= HALF + HALO
            taps = [kern_ref[block(a, b, TAPS), :] for b in range(TAPS)]
            for y in range(FULL):
                if whole or y < HALO or y >= SIDE + HALO:
                    here = field_ref[block(x, y, PITCH), :]
                    for b in range(TAPS):
                        if 0 <= y - b < SIDE:
                            sums[y - b] = sums[y - b] + here * taps[b]
        for j in range(SIDE):
            conv_ref[block(i, j, SIDE), :] = sums[j]

    gain = near_ref[width + 64 :].astype(F32)
    for r in range(SIDE):
        h, i = divmod(r, HALF)
        parts = [
            jnp.concatenate([conv_ref[comb(i, 8 * g, SIDE, h, cb), :] for g in range(2)], axis=0)
            for cb in range(4)
        ]
        value = jnp.concatenate(parts, axis=1)
        centred = value - jnp.mean(value, axis=1, keepdims=True)
        inverse = lax.rsqrt(jnp.mean(centred * centred, axis=1, keepdims=True) + 1e-06)
        normal = centred * inverse
        rows = pl.ds(r * SIDE, SIDE)
        normal_ref[rows, :] = normal
        inv_ref[rows, :] = jnp.broadcast_to(inverse, (SIDE, LANE))
        scaled_ref[rows, :] = (normal * gain).astype(BF16)

    for k in range(w_one_ref.shape[1] // STEP):
        some = pl.ds(k * STEP, STEP)
        pre = dot(scaled_ref[...], w_one_ref[:, some])
        cubic = (ROOT * CUBE) * (pre * pre)
        upper = 0.5 + 0.5 * jnp.tanh(pre * (ROOT + cubic))
        active = pre * upper
        slope = upper + active * (1.0 - upper) * (2.0 * ROOT + 6.0 * cubic)
        active_ref[:, some] = active.astype(BF16)
        d_hid_ref[:, some] = (d_act_ref[:, some] * slope).astype(BF16)

    half = w_one_ref.shape[1] // 2
    away = pl.ds(pl.multiple_of((1 - core_ref[0]) * half, half), half)
    theirs_ref[:, 0:half] = active_ref[:, away]
    theirs_ref[:, half : 2 * half] = d_hid_ref[:, away]
    theirs_ref[:, 2 * half : 2 * half + channels] = scaled_ref[...]
    theirs_ref[:, 2 * half + channels :] = cot_ref[...]


def backward_kernel(
    core_ref, odd_ref, grid_ref, s0, s1, s2, s3, place_ref, field_ref, normal_ref, inv_ref, d_hid_ref, w_one_ref,
    near_ref, kern_ref, cot_ref,
    mine_ref, theirs_ref,
    d_scaled_ref, d_conv_ref, spread_ref, own_ref, ring_ref, taps_ref, strips_ref, small_ref,
):
    d_scaled_ref[...] = dot(d_hid_ref[...], w_one_ref[...], NT)
    total = jnp.zeros((SIDE, normal_ref.shape[1]), F32)
    gain = near_ref[near_ref.shape[0] - 16 :].astype(F32)
    for r in range(SIDE):
        h, i = divmod(r, HALF)
        rows = pl.ds(r * SIDE, SIDE)
        normal, d_scaled = normal_ref[rows, :], d_scaled_ref[rows, :]
        total = total + d_scaled * normal
        d_normal = d_scaled * gain
        mean = jnp.mean(d_normal, axis=1, keepdims=True)
        along = jnp.mean(d_normal * normal, axis=1, keepdims=True)
        d_conv = (d_normal - mean - normal * along) * inv_ref[rows, 0:1]
        for g in range(2):
            for cb in range(4):
                d_conv_ref[comb(i, 8 * g, SIDE, h, cb), :] = d_conv[
                    8 * g : 8 * g + 8, cb * LANE : (cb + 1) * LANE
                ]
    grad_gain = jnp.sum(total, axis=0, keepdims=True)

    spread_ref[...] = jnp.zeros_like(spread_ref)
    taps_ref[...] = jnp.zeros_like(taps_ref)

    def conv_row(i, carry):
        d_conv = [d_conv_ref[block(i, j, SIDE), :] for j in range(SIDE)]
        for a in range(TAPS):
            taps = [kern_ref[block(a, b, TAPS), :] for b in range(TAPS)]
            sums = [taps_ref[block(a, b, TAPS), :] for b in range(TAPS)]
            for y in range(FULL):
                here = field_ref[block(i + a, y, PITCH), :]
                value = spread_ref[block(i + a, y, PITCH), :]
                for b in range(TAPS):
                    if 0 <= y - b < SIDE:
                        value = value + d_conv[y - b] * taps[b]
                        sums[b] = sums[b] + here * d_conv[y - b]
                spread_ref[block(i + a, y, PITCH), :] = value
            for b in range(TAPS):
                taps_ref[block(a, b, TAPS), :] = sums[b]
        return carry

    lax.fori_loop(0, HALF, conv_row, 0)

    def part(x, y, cb):
        value = None
        if x < ROWS2:
            value = spread_ref[comb(x, y, PITCH, 0, cb), :]
        if x >= HALF:
            more = spread_ref[comb(x - HALF, y, PITCH, 1, cb), :]
            value = more if value is None else value + more
        return value

    for cb in range(4):
        lanes = pl.ds(cb * LANE, LANE)
        for at, x, y in ring():
            ring_ref[pl.ds(at, 8), lanes] = part(x, y, cb)
        for i in range(SIDE):
            for g in range(0, SIDE, 8):
                own_ref[pl.ds(i * SIDE + g, 8), lanes] = part(i + HALO, g + HALO, cb)
    take_strips(core_ref[0], odd_ref[0], (s0, s1, s2, s3), strips_ref)
    d_halo = dot(place_ref[:, : 4 * STRIP], ring_ref[...].astype(BF16), TN).astype(BF16)
    d_own = (own_ref[...] + cot_ref[...].astype(F32)).astype(BF16)
    grad_embed = dot(grid_ref[...], d_own, TN) + dot(strips_ref[...], d_halo, TN)

    half = mine_ref.shape[0]
    small_ref[...] = jnp.zeros_like(small_ref)
    for t in range(half):
        r, c = divmod(t, 4)
        small_ref[t * 16 : (t + 1) * 16] = grad_embed[r * 16 : (r + 1) * 16, c * LANE : (c + 1) * LANE]
    base = half * 16
    for t in range(TAPS * TAPS):
        both = taps_ref[t * 8 : (t + 1) * 8, :]
        small_ref[base + t * 4 : base + (t + 1) * 4] = both[:4] + both[4:]
    for c in range(4):
        at = base + TAPS * TAPS * 4 + c
        small_ref[at : at + 1] = grad_gain[:, c * LANE : (c + 1) * LANE]
    core = core_ref[0]
    for t in range(half):
        mine_ref[t] = small_ref[pl.ds(pl.multiple_of((core * half + t) * 16, 16), 16), :]
        theirs_ref[t] = small_ref[
            pl.ds(pl.multiple_of(((1 - core) * half + t) * 16, 16), 16), :
        ].astype(BF16)


def pair_kernel(core_ref, scaled_ref, active_ref, d_hid_ref, cot_ref, their_ref, out_ref, two_ref, one_ref):
    half, channels = active_ref.shape[1] // 2, cot_ref.shape[1]
    their_scaled = their_ref[:, 2 * half : 2 * half + channels]
    their_cot = their_ref[:, 2 * half + channels :]
    mine = pl.ds(pl.multiple_of(core_ref[0] * half, half), half)
    one_ref[...] = dot(scaled_ref[...], d_hid_ref[:, mine], TN) + dot(
        their_scaled, their_ref[:, half : 2 * half], TN
    )
    for k in range(half // STEP):
        some = pl.ds(pl.multiple_of(core_ref[0] * half + k * STEP, STEP), STEP)
        two_ref[...] = dot(active_ref[:, some], cot_ref[...], TN) + dot(
            their_ref[:, k * STEP : (k + 1) * STEP], their_cot, TN
        )
        for t, ref, rows, lanes in tiles_of(k, two_ref, one_ref.at[:, k * STEP : (k + 1) * STEP]):
            out_ref[t // 8, t % 8] = ref[rows, lanes].astype(BF16)


def join_kernel(mine_ref, small_ref, paired_far, out_far, tile_ref, sem):
    tile_ref[...] = (mine_ref[...] + small_ref[...].astype(F32)).astype(BF16)
    put = pltpu.make_async_copy(tile_ref, out_far.at[:, 8], sem.at[0])
    put.start()
    put.wait()


def sum_kernel(in_ref, out_ref):
    parts, tiles = in_ref.shape[:2]

    def add(d, sums):
        return [s + in_ref[d, t].astype(F32) for t, s in enumerate(sums)]

    sums = lax.fori_loop(0, parts, add, [jnp.zeros(in_ref.shape[2:], F32)] * tiles, unroll=4)
    sums = [s.astype(BF16) for s in sums]

    def spread(d, carry):
        for t in range(tiles):
            out_ref[d, t] = sums[t]
        return carry

    lax.fori_loop(0, parts, spread, 0, unroll=4)


def assemble_half(core, in_ref, one_far, two_far, one_ref, two_ref, sem):
    steps = one_ref.shape[0]
    puts = []
    for k in range(steps):
        for t, ref, rows, lanes in tiles_of(k, two_ref, one_ref):
            ref[k, rows, lanes] = in_ref[t // 8, t % 8].astype(F32)
        some = pl.ds(pl.multiple_of((core * steps + k) * STEP, STEP), STEP)
        puts += [
            pltpu.make_async_copy(one_ref.at[k], one_far.at[:, some], sem.at[2 * k]),
            pltpu.make_async_copy(two_ref.at[k], two_far.at[some, :], sem.at[2 * k + 1]),
        ]
        puts[-2].start()
        puts[-1].start()
    return puts


def first_kernel(
    core_ref, in_ref, emb_ref, active_ref, w_two_ref,
    one_far, two_far, feature_far, one_ref, two_ref, feature_ref, sem,
):
    puts = assemble_half(core_ref[0], in_ref, one_far, two_far, one_ref, two_ref, sem)
    feature_ref[...] = (emb_ref[...].astype(F32) + dot(active_ref[...], w_two_ref[...])).astype(BF16)
    puts.append(pltpu.make_async_copy(feature_ref, feature_far, sem.at[len(puts)]))
    puts[-1].start()
    for put in puts:
        put.wait()


def second_kernel(
    core_ref, in_ref, mine_ref, one_old, two_old,
    one_far, two_far, embed_far, taps_far, gain_far,
    one_ref, two_ref, rows_ref, embed_ref, taps_ref, gain_ref, sem,
):
    core = core_ref[0]
    count = taps_ref.shape[0]

    def place(first, last):
        for t in range(in_ref.shape[0]):
            r, c = divmod(t, 4)
            embed_ref[r * 16 : (r + 1) * 16, c * LANE : (c + 1) * LANE] = first[t, 8].astype(F32)
        for t in range(rows_ref.shape[0] // 16):
            rows_ref[t * 16 : (t + 1) * 16, :] = last[t, 8].astype(F32)

    @pl.when(core == 0)
    def _():
        place(mine_ref, in_ref)

    @pl.when(core == 1)
    def _():
        place(in_ref, mine_ref)

    for cb in range(4):
        lanes = pl.ds(cb * LANE, LANE)
        for g in range(0, count - 1, 8):
            taps_ref[pl.ds(g, 8), lanes] = rows_ref[pl.ds(g * 4 + cb, 8, stride=4), :]
        taps_ref[pl.ds(count - 1, 1), lanes] = rows_ref[pl.ds((count - 1) * 4 + cb, 1), :]
        gain_ref[:, lanes] = rows_ref[pl.ds(count * 4 + cb, 1), :]
    base = 2 * one_ref.shape[0]
    puts = []
    for k, pair in enumerate(((embed_ref, embed_far), (taps_ref, taps_far), (gain_ref, gain_far))):
        puts.append(pltpu.make_async_copy(*pair, sem.at[base + k]))
        puts[-1].start()
    puts += assemble_half(1 - core, in_ref, one_far, two_far, one_ref, two_ref, sem)
    for put in puts:
        put.wait()


def turned(spin, x, y, last):
    row = jnp.where(spin == 0, x, jnp.where(spin == 1, last - y, jnp.where(spin == 2, last - x, y)))
    col = jnp.where(spin == 0, y, jnp.where(spin == 1, x, jnp.where(spin == 2, last - y, last - x)))
    return row, col


def leaving_strips(spin, x, y):
    row, col = turned(spin, x, y, SIDE - 1)
    cut = SIDE - HALO
    by_row = jnp.where(row >= cut, (row - cut) * SIDE + col, jnp.where(row < HALO, STRIP + row * SIDE + col, -1))
    by_col = jnp.where(col >= cut, 2 * STRIP + (col - cut) * SIDE + row, jnp.where(col < HALO, 3 * STRIP + col * SIDE + row, -1))
    return by_row, by_col


def arriving_strips(spin, x, y):
    row, col = turned(spin, x, y, FULL - 1)
    end = SIDE + HALO
    in_row, in_col = (row >= HALO) & (row < end), (col >= HALO) & (col < end)
    strip = jnp.where(
        (row < HALO) & in_col, row * SIDE + col - HALO,
        jnp.where((row >= end) & in_col, STRIP + (row - end) * SIDE + col - HALO,
        jnp.where((col < HALO) & in_row, 2 * STRIP + col * SIDE + row - HALO,
        jnp.where((col >= end) & in_row, 3 * STRIP + (col - end) * SIDE + row - HALO, -1))),
    )
    return jnp.where(y < FULL, strip, -1)


def exchange(far, one, two, by):
    def between(value, axes, first):
        size = lax.axis_size(axes)
        pairs = [(i, (i + 1) % size) for i in range(first, size, 2)]
        return lax.ppermute(value, axes, pairs + [(j, i) for i, j in pairs])

    beside = ("col", "core")
    return between(far, beside, 1), between(one, "face", 0), between(two, "face", 1), between(by, beside, 0)


def swap(value):
    return lax.ppermute(value, "core", [(0, 1), (1, 0)])


def on_device(
    obs_values, obs_tile, interp, tile_spin, w_embed, dw_kernel, norm_gain, w_one, w_two, cotangent
):
    tiles, chips = lax.axis_size(ALL), lax.axis_size(CHIPS)
    width, channels = w_embed.shape
    hidden = w_one.shape[1]
    slots = interp.shape[2]
    core, odd = lax.axis_index("core").reshape(1), (lax.axis_index("face") % 2).reshape(1)
    (leaving,) = call(
        route_kernel,
        [((tiles * 8, LANE), BF16)],
        [((1, obs_values.shape[0]), jnp.int32), (obs_values.shape, BF16)],
        60.5, core, odd, obs_tile.reshape(1, -1), obs_values, far=(2, 3), copies=2,
    )
    arrived = lax.all_to_all(leaving.reshape(tiles, 8, LANE), ALL, 0, 0, tiled=True)
    stacked = ((CELLS, tiles * slots), BF16)
    near = ((width + 80, channels), BF16)
    taps_gain = jnp.concatenate(
        [dw_kernel, jnp.zeros((64 - TAPS * TAPS, channels), BF16), jnp.broadcast_to(norm_gain, (16, channels))]
    )
    picks, places = ((4 * STRIP, CELLS), BF16), ((RING, CELLS), BF16)
    shelved, d_active = call(
        prepare_kernel,
        [((SHELF, channels), BF16), ((SHELF // 8, hidden), F32)],
        [
            (interp.shape[1:], BF16),
            (w_two.shape, BF16),
            (cotangent.shape, BF16),
            ((CELLS, hidden), F32),
            stacked,
            picks,
            near,
            places,
        ],
        60.5, tile_spin.reshape(1), interp[0], w_embed, taps_gain, w_two, cotangent,
        far=(1, 2, 3, 4, 5), far_outs=(0, 1), copies=9 + hidden // (2 * STEP),
    )
    gridded, nearby, place, *strips = call(
        embed_kernel,
        [((CELLS, width), BF16), near, places] + [((STRIP, width), BF16)] * 4,
        [((tiles * 8, LANE), F32), ((tiles * slots, width), BF16), stacked, picks, ((4 * STRIP, width), BF16)],
        16, core, odd, arrived.reshape(tiles * 8, LANE), shelved, far=(3,), copies=4,
    )
    strips = exchange(*strips)
    cells2 = ((ROWS2 * PITCH * 8, LANE), F32)
    kernel = ((TAPS * TAPS * 8, LANE), F32)
    blocks, cells = ((CELLS * 4, LANE), F32), ((CELLS, channels), F32)
    around = ((RING, channels), F32)
    step_sums = [((STEP, channels), F32), ((channels, hidden // 2), F32)]
    embedded, field, conv, taps, d_active = call(
        inner_kernel, [((CELLS, channels), BF16), cells2, blocks, kernel, ((CELLS, hidden), F32)], [], 20,
        gridded, nearby, d_active, far=(2,), copies=1,
    )
    field, normal, inverse, scaled, active, d_hidden, theirs = call(
        forward_kernel,
        [
            cells2,
            cells,
            ((CELLS, LANE), F32),
            ((CELLS, channels), BF16),
            ((CELLS, hidden), BF16),
            ((CELLS, hidden), BF16),
            ((CELLS, hidden + 2 * channels), BF16),
        ],
        [((4 * STRIP, width), BF16), around, blocks],
        20,
        core, odd, *strips, place, nearby, w_one, field, conv, taps, d_active, cotangent,
    )
    big = swap(theirs)

    mine, theirs = call(
        backward_kernel,
        [((chips, 16, LANE), F32), ((chips, 16, LANE), BF16)],
        [cells, blocks, cells2, cells, around, kernel, ((4 * STRIP, width), BF16), ((2 * chips * 16, LANE), F32)],
        20,
        core, odd, gridded, *strips, place, field, normal, inverse, d_hidden, w_one, nearby, taps, cotangent,
    )
    small = swap(theirs)
    whole = ((chips, 9, 16, LANE), BF16)
    (paired,) = call(
        pair_kernel, [whole], step_sums, 20, core, scaled, active, d_hidden, cotangent, big
    )
    (paired,) = call(
        join_kernel, [whole], [((chips, 16, LANE), BF16)], 4,
        mine, small, paired, far=(2,), far_outs=(0,), copies=1, aliases={2: 0},
    )
    paired = lax.all_to_all(paired, CHIPS, 0, 0, tiled=True)
    (summed,) = call(sum_kernel, [whole], [], 4, paired)
    here = lax.all_to_all(summed, CHIPS, 0, 0, tiled=True)
    there = swap(here)

    large = [((channels, hidden), F32), ((hidden, channels), F32)]
    steps = hidden // STEP // 2
    buffers = [((steps, channels, STEP), F32), ((steps, STEP, channels), F32)]
    *grads, output = call(
        first_kernel, large + [((CELLS, channels), BF16)], buffers + [((CELLS, channels), BF16)], 16,
        core, here, embedded, active, w_two, far_outs=(0, 1, 2), copies=2 * steps + 1,
    )
    count = TAPS * TAPS
    minor = [((width, channels), F32), ((count, channels), F32), ((1, channels), F32)]
    grad_one, grad_two, grad_embed, grad_kernel, grad_gain = call(
        second_kernel, large + minor,
        buffers + [((-(-(count + 1) * 4 // 16) * 16, LANE), F32)] + minor, 16,
        core, there, here, *grads,
        far=(3, 4), far_outs=range(5), copies=2 * steps + 3, aliases={3: 0, 4: 1},
    )
    return output, grad_embed, grad_kernel, grad_gain[0], grad_one, grad_two


def solution(mesh):
    faces, tiles = mesh.shape["face"], mesh.shape["tile"]
    fine = jax.sharding.Mesh(mesh.devices.reshape(faces, tiles // 2, 2), ALL)
    split = P(ALL, None)
    in_specs = (split, split, P(ALL, None, None, None), split) + (P(),) * 5 + (split,)
    return jax.shard_map(
        on_device, mesh=fine, in_specs=in_specs, out_specs=(split,) + (P(),) * 5, check_vma=False
    )
```

```python
import jax
import jax.numpy as jnp
from jax import lax
from jax.experimental import pallas as pl
from jax.experimental.pallas import tpu as pltpu
from jax.sharding import PartitionSpec as P

F32 = jnp.float32
BF16 = jnp.bfloat16
SIDE = 16
CELLS = SIDE * SIDE
HALO = 3
TAPS = 7
FULL = SIDE + 2 * HALO
PITCH = 24
HALF = SIDE // 2
LANE = 128
ROWS2 = HALF + TAPS - 1
STRIP = HALO * SIDE
SHELF = 65536
STEP = 256
ALL = ("face", "col", "core")
CHIPS = ("face", "col")
ROOT = 0.7978845608028654
CUBE = 0.044715

NN = (((1,), (0,)), ((), ()))
NT = (((1,), (1,)), ((), ()))
TN = (((0,), (0,)), ((), ()))


def dot(a, b, dims=NN):
    return lax.dot_general(a, b, dims, preferred_element_type=F32)


def call(kernel, outs, scratch, limit, *args, far=(), far_outs=(), copies=0, aliases=None):
    vmem, scalar = pl.BlockSpec(memory_space=pltpu.VMEM), pl.BlockSpec(memory_space=pltpu.SMEM)
    away = pl.BlockSpec(memory_space=pltpu.HBM)
    return pl.pallas_call(
        kernel,
        out_shape=[jax.ShapeDtypeStruct(s, d) for s, d in outs],
        in_specs=[
            scalar if a.shape == (1,) else away if k in far else vmem for k, a in enumerate(args)
        ],
        out_specs=[away if k in far_outs else vmem for k in range(len(outs))],
        scratch_shapes=[pltpu.VMEM(s, d) for s, d in scratch]
        + [pltpu.SemaphoreType.DMA((copies,))] * bool(copies),
        input_output_aliases=aliases or {},
        compiler_params=pltpu.CompilerParams(vmem_limit_bytes=int(limit * 2**20)),
    )(*args)


def start(sem, *pairs):
    moves = [pltpu.make_async_copy(a, b, sem.at[k]) for k, (a, b) in enumerate(pairs)]
    for move in moves:
        move.start()
    return moves


def strip_at(k):
    return pl.ds(pl.multiple_of(k * STRIP, 16), STRIP)


def take_strips(core, odd, refs, strips_ref):
    for ref, k in zip(refs, (2 + core, 1 - odd, odd, 3 - core)):
        strips_ref[strip_at(k), :] = ref[...]


def block(i, j, pitch):
    return pl.ds(pl.multiple_of((i * pitch + j) * 8, 8), 8)


def comb(i, j, pitch, h, cb):
    return pl.ds((i * pitch + j) * 8 + h * 4 + cb, 8, stride=8)


def route_kernel(core_ref, odd_ref, row_far, obs_far, out_ref, row_ref, obs_ref, sem):
    fetch_row, fetch_obs = start(sem, (row_far, row_ref), (obs_far, obs_ref))
    count, lines = row_ref.shape[1], out_ref.shape[0]
    line = lax.broadcasted_iota(jnp.int32, (lines, count), 0)
    line = line - (line & 4)
    fetch_row.wait()
    row = row_ref[...]
    across = jnp.broadcast_to(row, (count, count)).astype(F32)
    earlier = lax.broadcasted_iota(jnp.int32, (count, count), 0) < lax.broadcasted_iota(
        jnp.int32, (count, count), 1
    )
    same = jnp.where((across.T == across) & earlier, 1.0, 0.0)
    rank = jnp.sum(same, axis=0, keepdims=True).astype(jnp.int32)
    place = row * 8 + rank
    chosen = jnp.where(line == place, 1.0, 0.0).astype(BF16)
    fetch_obs.wait()
    moved = dot(chosen, obs_ref[...])
    first = (lax.broadcasted_iota(jnp.int32, (lines, LANE), 0) & 4) == 0
    out_ref[...] = jnp.where(first, moved[:, :LANE], moved[:, LANE:]).astype(BF16)


OUTER = (0, 1, 2, 19, 20, 21)


def ring():
    at = 0
    for x in OUTER:
        for y in range(0, PITCH, 8):
            yield at, x, y
            at += 8
    for x in range(HALO, SIDE + HALO):
        for y in (0, PITCH - 8):
            yield at, x, y
            at += 8


RING = 8 * len(list(ring()))


def shelf(width, slots, channels):
    rows = (CELLS, 4 * STRIP, width + 80, RING)
    lanes = (slots, CELLS, channels, CELLS)
    ends = [sum(rows[: k + 1]) for k in range(len(rows))]
    return [(pl.ds(e - r, r), pl.ds(0, n)) for e, r, n in zip(ends, rows, lanes)]


def prepare_kernel(
    spin_ref, interp_far, w_embed_far, small_far, w_two_far, cot_far, shelf_far, d_act_far,
    interp_ref, w_two_ref, cot_ref, d_act_ref, weights_ref, pick_ref, near_ref, place_ref, sem,
):
    tiles, slots = interp_ref.shape[:2]
    width, channels = w_embed_far.shape
    spots = shelf(width, tiles * slots, channels)
    fetches = start(
        sem, (interp_far, interp_ref), (w_embed_far, near_ref.at[pl.ds(0, width)]),
        (small_far, near_ref.at[pl.ds(width, 80)]), (cot_far, cot_ref), (w_two_far, w_two_ref),
    )
    put_weights, put_pick, put_near, put_place = (
        pltpu.make_async_copy(a, shelf_far.at[spot], sem.at[5 + k])
        for k, (a, spot) in enumerate(zip((weights_ref, pick_ref, near_ref, place_ref), spots))
    )
    spin = spin_ref[0]
    q = lax.broadcasted_iota(jnp.int32, (1, CELLS), 1)
    by_row, by_col = leaving_strips(spin, q // SIDE, q % SIDE)
    k = lax.broadcasted_iota(jnp.int32, pick_ref.shape, 0)
    pick_ref[...] = jnp.where((k == by_row) | (k == by_col), 1.0, 0.0).astype(BF16)
    put_pick.start()
    fetches[0].wait()
    weights = interp_ref[...].astype(F32)
    for k in range(slots):
        weights_ref[:, k * tiles : (k + 1) * tiles] = weights[:, k, :].T.astype(BF16)
    put_weights.start()
    p = lax.broadcasted_iota(jnp.int32, (RING, 1), 0)
    outer = len(OUTER) * PITCH
    o, r = (p * 171) >> 12, p - outer
    x = jnp.where(p < outer, jnp.where(o < HALO, o, o + SIDE), HALO + (r >> 4))
    y = jnp.where(p < outer, p - o * PITCH, (r & 15) + (r & 8))
    strip = arriving_strips(spin, x, y)
    k = lax.broadcasted_iota(jnp.int32, place_ref.shape, 1)
    place_ref[...] = jnp.where(strip == k, 1.0, 0.0).astype(BF16)
    put_place.start()
    for fetch in fetches[1:3]:
        fetch.wait()
    put_near.start()
    for fetch in fetches[3:]:
        fetch.wait()
    puts = []
    for k in range(0, w_two_ref.shape[0], 2 * STEP):
        some = pl.ds(k, 2 * STEP)
        d_act_ref[:, some] = dot(cot_ref[...], w_two_ref[some, :], NT)
        target = d_act_far.at[pl.ds(0, CELLS), some]
        puts.append(pltpu.make_async_copy(d_act_ref.at[:, some], target, sem.at[9 + len(puts)]))
        puts[-1].start()
    for put in [put_pick, put_near, put_weights, put_place] + puts:
        put.wait()


def embed_kernel(
    core_ref, odd_ref, got_ref, shelf_far, grid_ref, near_ref, place_ref, far_ref, one_ref, two_ref, by_ref,
    wide_ref, rows_ref, weights_ref, pick_ref, strips_ref, sem,
):
    width, channels = near_ref.shape[0] - 80, near_ref.shape[1]
    spots = shelf(width, weights_ref.shape[1], channels)
    targets = (weights_ref, pick_ref, near_ref, place_ref)
    fetches = start(sem, *((shelf_far.at[spot], b) for spot, b in zip(spots, targets)))
    wide_ref[...] = got_ref[...].astype(F32)
    tiles = got_ref.shape[0] // 8
    for k in range(4):
        for half in range(2):
            for g in range(0, tiles, 16):
                two = [
                    wide_ref[pl.ds((g + e) * 8 + half * 4 + k, 8, stride=8), :] for e in (0, 8)
                ]
                rows_ref[pl.ds(k * tiles + g, 16), pl.ds(half * LANE, LANE)] = jnp.concatenate(
                    two, axis=0
                ).astype(BF16)
    fetches[0].wait()
    gridded = dot(weights_ref[...], rows_ref[...]).astype(BF16)
    grid_ref[...] = gridded
    fetches[1].wait()
    strips_ref[...] = dot(pick_ref[...], gridded).astype(BF16)
    core, odd = core_ref[0], odd_ref[0]
    for ref, k in ((far_ref, 3 - core), (one_ref, odd), (two_ref, 1 - odd), (by_ref, 2 + core)):
        ref[...] = strips_ref[strip_at(k), :]
    for fetch in fetches[2:]:
        fetch.wait()


def tiles_of(part, two, one):
    for k in range(64):
        r, c = divmod(k, 4)
        yield part * 128 + k, two, pl.ds(r * 16, 16), pl.ds(c * LANE, LANE)
    for k in range(64):
        r, c = divmod(k, 2)
        yield part * 128 + 64 + k, one, pl.ds(r * 16, 16), pl.ds(c * LANE, LANE)


def inner_kernel(
    grid_ref, near_ref, d_act_far, emb_ref, field_ref, conv_ref, kern_ref, d_act_ref, sem
):
    width = near_ref.shape[0] - 80
    (fetch,) = start(sem, (d_act_far.at[pl.ds(0, CELLS), :], d_act_ref))
    emb_ref[...] = dot(grid_ref[...], near_ref[0:width]).astype(BF16)
    taps = near_ref[width : width + 64].astype(F32)
    last = TAPS * TAPS - 1
    for h in range(2):
        for cb in range(4):
            lanes = slice(cb * LANE, (cb + 1) * LANE)
            for g in range(0, last, 8):
                kern_ref[pl.ds(g * 8 + h * 4 + cb, 8, stride=8), :] = taps[g : g + 8, lanes]
            kern_ref[pl.ds(last * 8 + h * 4 + cb, 1), :] = taps[last : last + 1, lanes]
    for i in range(SIDE):
        own = emb_ref[pl.ds(i * SIDE, SIDE), :].astype(F32)
        x = i + HALO
        for g in range(0, SIDE, 8):
            for cb in range(4):
                value = own[g : g + 8, cb * LANE : (cb + 1) * LANE]
                if x < ROWS2:
                    field_ref[comb(x, HALO + g, PITCH, 0, cb), :] = value
                if x >= HALF:
                    field_ref[comb(x - HALF, HALO + g, PITCH, 1, cb), :] = value
    for i in range(HALF):
        sums = [jnp.zeros((8, LANE), F32)] * SIDE
        for x in range(max(i, HALO), min(i + TAPS, HALF + HALO)):
            taps = [kern_ref[block(x - i, b, TAPS), :] for b in range(TAPS)]
            for y in range(HALO, SIDE + HALO):
                here = field_ref[block(x, y, PITCH), :]
                for b in range(TAPS):
                    if 0 <= y - b < SIDE:
                        sums[y - b] = sums[y - b] + here * taps[b]
        for j in range(SIDE):
            conv_ref[block(i, j, SIDE), :] = sums[j]
    fetch.wait()


def forward_kernel(
    core_ref, odd_ref, s0, s1, s2, s3, place_ref, near_ref, w_one_ref, own_ref, part_ref, kern_ref, d_act_ref, cot_ref,
    field_ref, normal_ref, inv_ref, scaled_ref, active_ref, d_hid_ref, theirs_ref,
    strips_ref, ring_ref, conv_ref,
):
    width, channels = near_ref.shape[0] - 80, near_ref.shape[1]
    take_strips(core_ref[0], odd_ref[0], (s0, s1, s2, s3), strips_ref)
    halo = dot(strips_ref[...], near_ref[0:width]).astype(BF16)
    ring_ref[...] = dot(place_ref[:, : 4 * STRIP], halo)
    for x in range(ROWS2):
        own = pl.ds((x * PITCH + HALO) * 8, SIDE * 8)
        field_ref[own, :] = own_ref[own, :]
    for at, x, y in ring():
        skip, count = (0, 8) if x in OUTER else (0, HALO) if y == 0 else (HALO, HALO)
        for cb in range(4):
            value = ring_ref[pl.ds(at + skip, count), pl.ds(cb * LANE, LANE)]
            if x < ROWS2:
                field_ref[pl.ds((x * PITCH + y + skip) * 8 + cb, count, stride=8), :] = value
            if x >= HALF:
                row = ((x - HALF) * PITCH + y + skip) * 8 + 4 + cb
                field_ref[pl.ds(row, count, stride=8), :] = value

    for i in range(HALF):
        sums = [part_ref[block(i, j, SIDE), :] for j in range(SIDE)]
        for a in range(TAPS):
            x = i + a
            whole = x < HALO or x >= HALF + HALO
            taps = [kern_ref[block(a, b, TAPS), :] for b in range(TAPS)]
            for y in range(FULL):
                if whole or y < HALO or y >= SIDE + HALO:
                    here = field_ref[block(x, y, PITCH), :]
                    for b in range(TAPS):
                        if 0 <= y - b < SIDE:
                            sums[y - b] = sums[y - b] + here * taps[b]
        for j in range(SIDE):
            conv_ref[block(i, j, SIDE), :] = sums[j]

    gain = near_ref[width + 64 :].astype(F32)
    for r in range(SIDE):
        h, i = divmod(r, HALF)
        parts = [
            jnp.concatenate([conv_ref[comb(i, 8 * g, SIDE, h, cb), :] for g in range(2)], axis=0)
            for cb in range(4)
        ]
        value = jnp.concatenate(parts, axis=1)
        centred = value - jnp.mean(value, axis=1, keepdims=True)
        inverse = lax.rsqrt(jnp.mean(centred * centred, axis=1, keepdims=True) + 1e-06)
        normal = centred * inverse
        rows = pl.ds(r * SIDE, SIDE)
        normal_ref[rows, :] = normal
        inv_ref[rows, :] = jnp.broadcast_to(inverse, (SIDE, LANE))
        scaled_ref[rows, :] = (normal * gain).astype(BF16)

    for k in range(w_one_ref.shape[1] // STEP):
        some = pl.ds(k * STEP, STEP)
        pre = dot(scaled_ref[...], w_one_ref[:, some])
        cubic = (ROOT * CUBE) * (pre * pre)
        upper = 0.5 + 0.5 * jnp.tanh(pre * (ROOT + cubic))
        active = pre * upper
        slope = upper + active * (1.0 - upper) * (2.0 * ROOT + 6.0 * cubic)
        active_ref[:, some] = active.astype(BF16)
        d_hid_ref[:, some] = (d_act_ref[:, some] * slope).astype(BF16)

    half = w_one_ref.shape[1] // 2
    away = pl.ds(pl.multiple_of((1 - core_ref[0]) * half, half), half)
    theirs_ref[:, 0:half] = active_ref[:, away]
    theirs_ref[:, half : 2 * half] = d_hid_ref[:, away]
    theirs_ref[:, 2 * half : 2 * half + channels] = scaled_ref[...]
    theirs_ref[:, 2 * half + channels :] = cot_ref[...]


def backward_kernel(
    core_ref, odd_ref, grid_ref, s0, s1, s2, s3, place_ref, field_ref, normal_ref, inv_ref, d_hid_ref, w_one_ref,
    near_ref, kern_ref, cot_ref,
    mine_ref, theirs_ref,
    d_scaled_ref, d_conv_ref, spread_ref, own_ref, ring_ref, taps_ref, strips_ref, small_ref,
):
    d_scaled_ref[...] = dot(d_hid_ref[...], w_one_ref[...], NT)
    total = jnp.zeros((SIDE, normal_ref.shape[1]), F32)
    gain = near_ref[near_ref.shape[0] - 16 :].astype(F32)
    for r in range(SIDE):
        h, i = divmod(r, HALF)
        rows = pl.ds(r * SIDE, SIDE)
        normal, d_scaled = normal_ref[rows, :], d_scaled_ref[rows, :]
        total = total + d_scaled * normal
        d_normal = d_scaled * gain
        mean = jnp.mean(d_normal, axis=1, keepdims=True)
        along = jnp.mean(d_normal * normal, axis=1, keepdims=True)
        d_conv = (d_normal - mean - normal * along) * inv_ref[rows, 0:1]
        for g in range(2):
            for cb in range(4):
                d_conv_ref[comb(i, 8 * g, SIDE, h, cb), :] = d_conv[
                    8 * g : 8 * g + 8, cb * LANE : (cb + 1) * LANE
                ]
    grad_gain = jnp.sum(total, axis=0, keepdims=True)

    spread_ref[...] = jnp.zeros_like(spread_ref)
    taps_ref[...] = jnp.zeros_like(taps_ref)

    def conv_row(i, carry):
        d_conv = [d_conv_ref[block(i, j, SIDE), :] for j in range(SIDE)]
        for a in range(TAPS):
            taps = [kern_ref[block(a, b, TAPS), :] for b in range(TAPS)]
            sums = [taps_ref[block(a, b, TAPS), :] for b in range(TAPS)]
            for y in range(FULL):
                here = field_ref[block(i + a, y, PITCH), :]
                value = spread_ref[block(i + a, y, PITCH), :]
                for b in range(TAPS):
                    if 0 <= y - b < SIDE:
                        value = value + d_conv[y - b] * taps[b]
                        sums[b] = sums[b] + here * d_conv[y - b]
                spread_ref[block(i + a, y, PITCH), :] = value
            for b in range(TAPS):
                taps_ref[block(a, b, TAPS), :] = sums[b]
        return carry

    lax.fori_loop(0, HALF, conv_row, 0)

    def part(x, y, cb):
        value = None
        if x < ROWS2:
            value = spread_ref[comb(x, y, PITCH, 0, cb), :]
        if x >= HALF:
            more = spread_ref[comb(x - HALF, y, PITCH, 1, cb), :]
            value = more if value is None else value + more
        return value

    for cb in range(4):
        lanes = pl.ds(cb * LANE, LANE)
        for at, x, y in ring():
            ring_ref[pl.ds(at, 8), lanes] = part(x, y, cb)
        for i in range(SIDE):
            for g in range(0, SIDE, 8):
                own_ref[pl.ds(i * SIDE + g, 8), lanes] = part(i + HALO, g + HALO, cb)
    take_strips(core_ref[0], odd_ref[0], (s0, s1, s2, s3), strips_ref)
    d_halo = dot(place_ref[:, : 4 * STRIP], ring_ref[...].astype(BF16), TN).astype(BF16)
    d_own = (own_ref[...] + cot_ref[...].astype(F32)).astype(BF16)
    grad_embed = dot(grid_ref[...], d_own, TN) + dot(strips_ref[...], d_halo, TN)

    half = mine_ref.shape[0]
    small_ref[...] = jnp.zeros_like(small_ref)
    for t in range(half):
        r, c = divmod(t, 4)
        small_ref[t * 16 : (t + 1) * 16] = grad_embed[r * 16 : (r + 1) * 16, c * LANE : (c + 1) * LANE]
    base = half * 16
    for t in range(TAPS * TAPS):
        both = taps_ref[t * 8 : (t + 1) * 8, :]
        small_ref[base + t * 4 : base + (t + 1) * 4] = both[:4] + both[4:]
    for c in range(4):
        at = base + TAPS * TAPS * 4 + c
        small_ref[at : at + 1] = grad_gain[:, c * LANE : (c + 1) * LANE]
    core = core_ref[0]
    for t in range(half):
        mine_ref[t] = small_ref[pl.ds(pl.multiple_of((core * half + t) * 16, 16), 16), :]
        theirs_ref[t] = small_ref[
            pl.ds(pl.multiple_of(((1 - core) * half + t) * 16, 16), 16), :
        ].astype(BF16)


def pair_kernel(core_ref, scaled_ref, active_ref, d_hid_ref, cot_ref, their_ref, out_ref, two_ref, one_ref):
    half, channels = active_ref.shape[1] // 2, cot_ref.shape[1]
    their_scaled = their_ref[:, 2 * half : 2 * half + channels]
    their_cot = their_ref[:, 2 * half + channels :]
    mine = pl.ds(pl.multiple_of(core_ref[0] * half, half), half)
    one_ref[...] = dot(scaled_ref[...], d_hid_ref[:, mine], TN) + dot(
        their_scaled, their_ref[:, half : 2 * half], TN
    )
    for k in range(half // STEP):
        some = pl.ds(pl.multiple_of(core_ref[0] * half + k * STEP, STEP), STEP)
        two_ref[...] = dot(active_ref[:, some], cot_ref[...], TN) + dot(
            their_ref[:, k * STEP : (k + 1) * STEP], their_cot, TN
        )
        for t, ref, rows, lanes in tiles_of(k, two_ref, one_ref.at[:, k * STEP : (k + 1) * STEP]):
            out_ref[t // 8, t % 8] = ref[rows, lanes].astype(BF16)


def join_kernel(mine_ref, small_ref, paired_far, out_far, tile_ref, sem):
    tile_ref[...] = (mine_ref[...] + small_ref[...].astype(F32)).astype(BF16)
    put = pltpu.make_async_copy(tile_ref, out_far.at[:, 8], sem.at[0])
    put.start()
    put.wait()


def sum_kernel(in_ref, out_ref):
    parts, tiles = in_ref.shape[:2]

    def add(d, sums):
        return [s + in_ref[d, t].astype(F32) for t, s in enumerate(sums)]

    sums = lax.fori_loop(0, parts, add, [jnp.zeros(in_ref.shape[2:], F32)] * tiles, unroll=8)
    sums = [s.astype(BF16) for s in sums]

    def spread(d, carry):
        for t in range(tiles):
            out_ref[d, t] = sums[t]
        return carry

    lax.fori_loop(0, parts, spread, 0, unroll=8)


def assemble_half(core, in_ref, one_far, two_far, one_ref, two_ref, sem):
    steps = one_ref.shape[0]
    puts = []
    for k in range(steps):
        for t, ref, rows, lanes in tiles_of(k, two_ref, one_ref):
            ref[k, rows, lanes] = in_ref[t // 8, t % 8].astype(F32)
        some = pl.ds(pl.multiple_of((core * steps + k) * STEP, STEP), STEP)
        puts += [
            pltpu.make_async_copy(one_ref.at[k], one_far.at[:, some], sem.at[2 * k]),
            pltpu.make_async_copy(two_ref.at[k], two_far.at[some, :], sem.at[2 * k + 1]),
        ]
        puts[-2].start()
        puts[-1].start()
    return puts


def first_kernel(
    core_ref, in_ref, emb_ref, active_ref, w_two_ref,
    one_far, two_far, feature_far, one_ref, two_ref, feature_ref, sem,
):
    puts = assemble_half(core_ref[0], in_ref, one_far, two_far, one_ref, two_ref, sem)
    feature_ref[...] = (emb_ref[...].astype(F32) + dot(active_ref[...], w_two_ref[...])).astype(BF16)
    puts.append(pltpu.make_async_copy(feature_ref, feature_far, sem.at[len(puts)]))
    puts[-1].start()
    for put in puts:
        put.wait()


def second_kernel(
    core_ref, in_ref, mine_ref, one_old, two_old,
    one_far, two_far, embed_far, taps_far, gain_far,
    one_ref, two_ref, rows_ref, embed_ref, taps_ref, gain_ref, sem,
):
    core = core_ref[0]
    count = taps_ref.shape[0]

    def place(first, last):
        for t in range(in_ref.shape[0]):
            r, c = divmod(t, 4)
            embed_ref[r * 16 : (r + 1) * 16, c * LANE : (c + 1) * LANE] = first[t, 8].astype(F32)
        for t in range(rows_ref.shape[0] // 16):
            rows_ref[t * 16 : (t + 1) * 16, :] = last[t, 8].astype(F32)

    @pl.when(core == 0)
    def _():
        place(mine_ref, in_ref)

    @pl.when(core == 1)
    def _():
        place(in_ref, mine_ref)

    for cb in range(4):
        lanes = pl.ds(cb * LANE, LANE)
        for g in range(0, count - 1, 8):
            taps_ref[pl.ds(g, 8), lanes] = rows_ref[pl.ds(g * 4 + cb, 8, stride=4), :]
        taps_ref[pl.ds(count - 1, 1), lanes] = rows_ref[pl.ds((count - 1) * 4 + cb, 1), :]
        gain_ref[:, lanes] = rows_ref[pl.ds(count * 4 + cb, 1), :]
    base = 2 * one_ref.shape[0]
    puts = []
    for k, pair in enumerate(((embed_ref, embed_far), (taps_ref, taps_far), (gain_ref, gain_far))):
        puts.append(pltpu.make_async_copy(*pair, sem.at[base + k]))
        puts[-1].start()
    puts += assemble_half(1 - core, in_ref, one_far, two_far, one_ref, two_ref, sem)
    for put in puts:
        put.wait()


def turned(spin, x, y, last):
    row = jnp.where(spin == 0, x, jnp.where(spin == 1, last - y, jnp.where(spin == 2, last - x, y)))
    col = jnp.where(spin == 0, y, jnp.where(spin == 1, x, jnp.where(spin == 2, last - y, last - x)))
    return row, col


def leaving_strips(spin, x, y):
    row, col = turned(spin, x, y, SIDE - 1)
    cut = SIDE - HALO
    by_row = jnp.where(row >= cut, (row - cut) * SIDE + col, jnp.where(row < HALO, STRIP + row * SIDE + col, -1))
    by_col = jnp.where(col >= cut, 2 * STRIP + (col - cut) * SIDE + row, jnp.where(col < HALO, 3 * STRIP + col * SIDE + row, -1))
    return by_row, by_col


def arriving_strips(spin, x, y):
    row, col = turned(spin, x, y, FULL - 1)
    end = SIDE + HALO
    in_row, in_col = (row >= HALO) & (row < end), (col >= HALO) & (col < end)
    strip = jnp.where(
        (row < HALO) & in_col, row * SIDE + col - HALO,
        jnp.where((row >= end) & in_col, STRIP + (row - end) * SIDE + col - HALO,
        jnp.where((col < HALO) & in_row, 2 * STRIP + col * SIDE + row - HALO,
        jnp.where((col >= end) & in_row, 3 * STRIP + (col - end) * SIDE + row - HALO, -1))),
    )
    return jnp.where(y < FULL, strip, -1)


def exchange(far, one, two, by):
    def between(value, axes, first):
        size = lax.axis_size(axes)
        pairs = [(i, (i + 1) % size) for i in range(first, size, 2)]
        return lax.ppermute(value, axes, pairs + [(j, i) for i, j in pairs])

    beside = ("col", "core")
    return between(far, beside, 1), between(one, "face", 0), between(two, "face", 1), between(by, beside, 0)


def swap(value):
    return lax.ppermute(value, "core", [(0, 1), (1, 0)])


def on_device(
    obs_values, obs_tile, interp, tile_spin, w_embed, dw_kernel, norm_gain, w_one, w_two, cotangent
):
    tiles, chips = lax.axis_size(ALL), lax.axis_size(CHIPS)
    width, channels = w_embed.shape
    hidden = w_one.shape[1]
    slots = interp.shape[2]
    core, odd = lax.axis_index("core").reshape(1), (lax.axis_index("face") % 2).reshape(1)
    (leaving,) = call(
        route_kernel,
        [((tiles * 8, LANE), BF16)],
        [((1, obs_values.shape[0]), jnp.int32), (obs_values.shape, BF16)],
        60.5, core, odd, obs_tile.reshape(1, -1), obs_values, far=(2, 3), copies=2,
    )
    arrived = lax.all_to_all(leaving.reshape(tiles, 8, LANE), ALL, 0, 0, tiled=True)
    stacked = ((CELLS, tiles * slots), BF16)
    near = ((width + 80, channels), BF16)
    taps_gain = jnp.concatenate(
        [dw_kernel, jnp.zeros((64 - TAPS * TAPS, channels), BF16), jnp.broadcast_to(norm_gain, (16, channels))]
    )
    picks, places = ((4 * STRIP, CELLS), BF16), ((RING, CELLS), BF16)
    shelved, d_active = call(
        prepare_kernel,
        [((SHELF, channels), BF16), ((SHELF // 8, hidden), F32)],
        [
            (interp.shape[1:], BF16),
            (w_two.shape, BF16),
            (cotangent.shape, BF16),
            ((CELLS, hidden), F32),
            stacked,
            picks,
            near,
            places,
        ],
        60.5, tile_spin.reshape(1), interp[0], w_embed, taps_gain, w_two, cotangent,
        far=(1, 2, 3, 4, 5), far_outs=(0, 1), copies=9 + hidden // (2 * STEP),
    )
    gridded, nearby, place, *strips = call(
        embed_kernel,
        [((CELLS, width), BF16), near, places] + [((STRIP, width), BF16)] * 4,
        [((tiles * 8, LANE), F32), ((tiles * slots, width), BF16), stacked, picks, ((4 * STRIP, width), BF16)],
        16, core, odd, arrived.reshape(tiles * 8, LANE), shelved, far=(3,), copies=4,
    )
    strips = exchange(*strips)
    cells2 = ((ROWS2 * PITCH * 8, LANE), F32)
    kernel = ((TAPS * TAPS * 8, LANE), F32)
    blocks, cells = ((CELLS * 4, LANE), F32), ((CELLS, channels), F32)
    around = ((RING, channels), F32)
    step_sums = [((STEP, channels), F32), ((channels, hidden // 2), F32)]
    embedded, field, conv, taps, d_active = call(
        inner_kernel, [((CELLS, channels), BF16), cells2, blocks, kernel, ((CELLS, hidden), F32)], [], 20,
        gridded, nearby, d_active, far=(2,), copies=1,
    )
    field, normal, inverse, scaled, active, d_hidden, theirs = call(
        forward_kernel,
        [
            cells2,
            cells,
            ((CELLS, LANE), F32),
            ((CELLS, channels), BF16),
            ((CELLS, hidden), BF16),
            ((CELLS, hidden), BF16),
            ((CELLS, hidden + 2 * channels), BF16),
        ],
        [((4 * STRIP, width), BF16), around, blocks],
        20,
        core, odd, *strips, place, nearby, w_one, field, conv, taps, d_active, cotangent,
    )
    big = swap(theirs)

    mine, theirs = call(
        backward_kernel,
        [((chips, 16, LANE), F32), ((chips, 16, LANE), BF16)],
        [cells, blocks, cells2, cells, around, kernel, ((4 * STRIP, width), BF16), ((2 * chips * 16, LANE), F32)],
        20,
        core, odd, gridded, *strips, place, field, normal, inverse, d_hidden, w_one, nearby, taps, cotangent,
    )
    small = swap(theirs)
    whole = ((chips, 9, 16, LANE), BF16)
    (paired,) = call(
        pair_kernel, [whole], step_sums, 20, core, scaled, active, d_hidden, cotangent, big
    )
    (paired,) = call(
        join_kernel, [whole], [((chips, 16, LANE), BF16)], 4,
        mine, small, paired, far=(2,), far_outs=(0,), copies=1, aliases={2: 0},
    )
    paired = lax.all_to_all(paired, CHIPS, 0, 0, tiled=True)
    (summed,) = call(sum_kernel, [whole], [], 4, paired)
    here = lax.all_to_all(summed, CHIPS, 0, 0, tiled=True)
    there = swap(here)

    large = [((channels, hidden), F32), ((hidden, channels), F32)]
    steps = hidden // STEP // 2
    buffers = [((steps, channels, STEP), F32), ((steps, STEP, channels), F32)]
    *grads, output = call(
        first_kernel, large + [((CELLS, channels), BF16)], buffers + [((CELLS, channels), BF16)], 16,
        core, here, embedded, active, w_two, far_outs=(0, 1, 2), copies=2 * steps + 1,
    )
    count = TAPS * TAPS
    minor = [((width, channels), F32), ((count, channels), F32), ((1, channels), F32)]
    grad_one, grad_two, grad_embed, grad_kernel, grad_gain = call(
        second_kernel, large + minor,
        buffers + [((-(-(count + 1) * 4 // 16) * 16, LANE), F32)] + minor, 16,
        core, there, here, *grads,
        far=(3, 4), far_outs=range(5), copies=2 * steps + 3, aliases={3: 0, 4: 1},
    )
    return output, grad_embed, grad_kernel, grad_gain[0], grad_one, grad_two


def solution(mesh):
    faces, tiles = mesh.shape["face"], mesh.shape["tile"]
    fine = jax.sharding.Mesh(mesh.devices.reshape(faces, tiles // 2, 2), ALL)
    split = P(ALL, None)
    in_specs = (split, split, P(ALL, None, None, None), split) + (P(),) * 5 + (split,)
    return jax.shard_map(
        on_device, mesh=fine, in_specs=in_specs, out_specs=(split,) + (P(),) * 5, check_vma=False
    )
```
